32 devices in a mesh: seq: 16 (over z, x, core), batch: 2 (over y).
Axes of the slice: x: 2, y: 2, z: 4, core: 2. Of those that a mesh axis runs over, the one named last changes fastest.
Arguments:
- patches: bfloat16 [2, 2048, 1024], P('batch', 'seq'), may hold values from -6 to 6
- cotangent: bfloat16 [2, 2048, 1024], P('batch', 'seq'), may hold values from -6 to 6
- segment_ids: int32 [2, 2048], P('batch'), may hold values from 0 to 6, as said below
- kept_mask: int32 [2, 2048], P('batch'), may hold values from 0 to 1, as said below
- first_gain: bfloat16 [1024], P(('seq', 'batch')), may hold values from 0.5 to 1.5
- qkv_weight: bfloat16 [1024, 3072], P(('seq', 'batch')), may hold values from -0.25 to 0.25
- out_weight: bfloat16 [1024, 1024], P(('seq', 'batch')), may hold values from -1.5 to 1.5
- second_gain: bfloat16 [1024], P(('seq', 'batch')), may hold values from 0.5 to 1.5
- up_weight: bfloat16 [1024, 4096], P(('seq', 'batch')), may hold values from -0.1875 to 0.1875
- down_weight: bfloat16 [4096, 1024], P(('seq', 'batch')), may hold values from -0.09375 to 0.09375
Outputs:
- block_output: bfloat16 [2, 2048, 1024], P('batch', 'seq')
- input_grad: bfloat16 [2, 2048, 1024], P('batch', 'seq')
- first_gain_grad: float32 [1024], P(('seq', 'batch'))
- qkv_grad: float32 [1024, 3072], P(('seq', 'batch'))
- out_grad: float32 [1024, 1024], P(('seq', 'batch'))
- second_gain_grad: float32 [1024], P(('seq', 'batch'))
- up_grad: float32 [1024, 4096], P(('seq', 'batch'))
- down_grad: float32 [4096, 1024], P(('seq', 'batch'))
The draws below stay inside these ranges and needn't reach their ends.
Inputs may be any that keep to these rules, and one draw needn't show every extreme that they name: `segment_ids`: segment ids never fall along a sequence; in each sequence one segment's first slot has an index from 1 to 64 and its last slot an index from 1983 to 2046. `kept_mask`: padded slots stand only at the end of a sequence.
All inputs are finite; a program needn't handle non-finite values.
Results may differ from the reference program's by a relative error of at most 0.029.
Values may be sent and summed in bfloat16 or wider, within the bound.
No kernel may reach another device: no remote copies, remote signals or barrier semaphores. Data moves between devices by JAX's collectives and lax.ppermute only.
A program may use at most 192 MiB of HBM per device.

```python
import math
import jax
import jax.numpy as jnp
from jax import lax

D = 1024
HEADS = 16
HDIM = 64
FF = 4096
TOK_DEV = 128
SEQS = 2
SEQ_LEN = 2048


def draw_segment_ids(key, part):
    key = jax.random.fold_in(key, 11)
    keys_split = jax.random.split(key, 4)
    opening = jax.random.randint(keys_split[0], (SEQS, 1), 1, TOK_DEV // 2 + 1)
    closing = jax.random.randint(keys_split[1], (SEQS, 1), SEQ_LEN - TOK_DEV // 2, SEQ_LEN)
    before = 1 + jax.random.randint(keys_split[2], (SEQS, 2), 0, 1 << 20) % opening
    after = closing + jax.random.randint(keys_split[3], (SEQS, 2), 0, 1 << 20) % (SEQ_LEN - closing)
    cuts = jnp.concatenate([before, opening, closing, after], axis=1)
    positions = jnp.arange(SEQ_LEN, dtype=jnp.int32)
    return jnp.sum((positions[None, :, None] >= cuts[:, None, :]).astype(jnp.int32), axis=2).astype(jnp.int32)


def draw_kept_mask(key, part):
    key = jax.random.fold_in(key, 23)
    padding = jax.random.randint(key, (SEQS, 1), TOK_DEV // 2, 2 * TOK_DEV + 1)
    positions = jnp.arange(SEQ_LEN, dtype=jnp.int32)
    return (positions[None, :] < SEQ_LEN - padding).astype(jnp.int32)


def level_of(own_key, dims, cuts, low, largest):
    loudness, own = 1.0, jax.random.fold_in(own_key, 6)
    for axis_at, parts in cuts:
        steps = jnp.exp(jax.random.uniform(jax.random.fold_in(own, axis_at), (parts,), jnp.float32, low / len(cuts), largest / len(cuts)))
        loudness = loudness * jnp.repeat(steps, dims[axis_at] // parts).reshape([-1 if axis == axis_at else 1 for axis in range(len(dims))])
    return loudness


def scatter_about(rng, dims, spread, reach, cuts=(), held_as=jnp.bfloat16):
    values = jax.random.normal(rng, dims, jnp.float32) * spread
    if len(cuts) > 0:
        values = level_of(rng, dims, cuts, -0.22, 0.18) * values
    return jnp.clip(values, min=-reach, max=reach).astype(held_as)


def setup_inputs(seed: int = 0) -> dict:
    arg_keys = jax.random.split(jax.random.key(seed), 11)
    patches = scatter_about(arg_keys[0], (SEQS, SEQ_LEN, D), 1.0, 6.0, ((0, 2), (1, 16)))
    cotangent = scatter_about(arg_keys[1], (SEQS, SEQ_LEN, D), 1.0, 6.0, ((0, 2), (1, 16)))
    segment_ids = draw_segment_ids(jax.random.fold_in(arg_keys[10], 71), 0)
    kept_mask = draw_kept_mask(jax.random.fold_in(arg_keys[10], 71), 0)
    first_gain = jnp.clip(1.0 + 0.1 * jax.random.normal(arg_keys[4], (D,), jnp.float32), 0.5, 1.5).astype(jnp.bfloat16)
    qkv_weight = scatter_about(arg_keys[5], (D, 3 * D), (D // 2) ** -0.5, 0.25, ((0, 32),))
    out_weight = scatter_about(arg_keys[6], (D, D), 16 ** -0.5, 1.5, ((0, 32),))
    second_gain = jnp.clip(1.0 + 0.1 * jax.random.normal(arg_keys[7], (D,), jnp.float32), 0.5, 1.5).astype(jnp.bfloat16)
    up_weight = scatter_about(arg_keys[8], (D, FF), D ** -0.5, 0.1875, ((0, 32),))
    down_weight = scatter_about(arg_keys[9], (FF, D), FF ** -0.5, 0.09375, ((0, 32),))
    return dict(patches=patches, cotangent=cotangent, segment_ids=segment_ids, kept_mask=kept_mask, first_gain=first_gain, qkv_weight=qkv_weight, out_weight=out_weight, second_gain=second_gain, up_weight=up_weight, down_weight=down_weight)


@jax.custom_vjp
def low(v):
    return lax.optimization_barrier(v.astype(jnp.bfloat16)).astype(jnp.float32)

@jax.custom_vjp
def low_back(v):
    return v

def low_keep(v):
    return (low(v), None)

def low_pass(kept, grad):
    return (grad,)

def back_keep(v):
    return (v, None)

def back_low(kept, grad):
    return (low(grad),)
low.defvjp(low_keep, low_pass)
low_back.defvjp(back_keep, back_low)
EPSILON = 1e-05
MASKED = -1e+30

def layer_norm(values, scales):
    average = lax.optimization_barrier(jnp.mean(values, axis=-1, keepdims=True))
    centred = values - average
    variance = lax.optimization_barrier(jnp.mean(centred * centred, axis=-1, keepdims=True))
    return centred * lax.rsqrt(variance + EPSILON) * scales

def attend(queries, keys_all, values_all, segment_row, kept_row):
    length = queries.shape[0]
    block = math.gcd(length, 512)
    positions = jnp.arange(length, dtype=jnp.int32)
    head_keys = keys_all.reshape(length, HEADS, HDIM)
    head_values = values_all.reshape(length, HEADS, HDIM)
    scaling = HDIM ** (-0.5)

    def one_block(pieces):
        query_block, segment_block, position_block = pieces
        scores = jnp.einsum('qhd,khd->hqk', query_block, head_keys, precision=lax.Precision.HIGHEST) * scaling
        scores = low_back(scores)
        allowed = (segment_block[:, None] == segment_row[None, :]) & ((kept_row[None, :] == 1) | (position_block[:, None] == positions[None, :]))
        scores = jnp.where(allowed[None], scores, MASKED)
        highest = lax.optimization_barrier(jnp.max(scores, axis=-1, keepdims=True))
        expo = jnp.exp(scores - highest)
        weights = low(expo / lax.optimization_barrier(jnp.sum(expo, axis=-1, keepdims=True)))
        result = jnp.einsum('hqk,khd->qhd', weights, head_values, precision=lax.Precision.HIGHEST)
        return result.reshape(block, HEADS * HDIM)
    outputs = lax.map(jax.checkpoint(one_block), (queries.reshape(length // block, block, HEADS, HDIM), segment_row.reshape(length // block, block), positions.reshape(length // block, block)))
    return outputs.reshape(length, HEADS * HDIM)

def forward(patch_rows, first_gain, qkv_weight, out_weight, second_gain, up_weight, down_weight, segment_row, kept_row):
    width = HEADS * HDIM
    normed = low(layer_norm(patch_rows, first_gain))
    project = low_back(low(jnp.dot(normed, qkv_weight, precision=lax.Precision.HIGHEST)))
    mixed = low_back(low(attend(project[:, :width], project[:, width:2 * width], project[:, 2 * width:], segment_row, kept_row)))
    middle = patch_rows + low_back(jnp.dot(mixed, out_weight, precision=lax.Precision.HIGHEST))
    second = low(layer_norm(middle, second_gain))
    hidden_pre = low_back(jnp.dot(second, up_weight, precision=lax.Precision.HIGHEST))
    hidden = low(jax.nn.gelu(hidden_pre, approximate=False))
    return middle + jnp.dot(hidden, down_weight, precision=lax.Precision.HIGHEST)

def reference(patches, cotangent, segment_ids, kept_mask, first_gain, qkv_weight, out_weight, second_gain, up_weight, down_weight):
    params = tuple((member.astype(jnp.float32) for member in (first_gain, qkv_weight, out_weight, second_gain, up_weight, down_weight)))

    def per_sequence(totals, sequence_items):
        patch_rows, cot_rows, segment_row, kept_row = sequence_items

        def wrapped(inputs, gain_one, weight_qkv, weight_out, gain_two, weight_up, weight_down):
            return forward(inputs, gain_one, weight_qkv, weight_out, gain_two, weight_up, weight_down, segment_row, kept_row)
        result, pullback = jax.vjp(wrapped, patch_rows.astype(jnp.float32), *params)
        gradients = pullback(cot_rows.astype(jnp.float32))
        totals = tuple((total + grad_term for total, grad_term in zip(totals, gradients[1:])))
        return (totals, (result.astype(jnp.bfloat16), gradients[0].astype(jnp.bfloat16)))
    starting = tuple((jnp.zeros(member.shape, jnp.float32) for member in params))
    totals, (outputs, input_grads) = lax.scan(per_sequence, starting, (patches, cotangent, segment_ids, kept_mask))
    return (outputs, input_grads, totals[0], totals[1], totals[2], totals[3], totals[4], totals[5])
```

```python
import functools

import jax
import jax.numpy as jnp
from jax import lax
from jax.experimental import pallas as pl
from jax.experimental.pallas import tpu as pltpu
from jax.sharding import PartitionSpec as P

HEADS = 16
HDIM = 64
QUAD = 4

EPSILON = 1e-05
MASKED = -1e30
SCALING = HDIM**-0.5
BF16 = jnp.bfloat16
F32 = jnp.float32
EVERY = ("seq", "batch")


def contract(left, right, left_dim, right_dim):
    return lax.dot_general(
        left, right, (((left_dim,), (right_dim,)), ((), ())), preferred_element_type=F32
    )


def masked_scores(keys, queries, key_ids, query_ids, query_slots):
    scores = contract(keys, queries, 0, 0)
    slots = lax.broadcasted_iota(jnp.int32, scores.shape, 0)
    allowed = (key_ids == query_ids) | (slots == query_slots)
    return jnp.where(allowed, scores, MASKED)


def forward_kernel(
    tokens, q_ref, k_ref, v_ref, key_id_ref, query_id_ref, slot_ref, mixed_ref, attended_ref, log_ref
):
    scores = masked_scores(
        k_ref[...], q_ref[...], key_id_ref[...], query_id_ref[...], slot_ref[...]
    )
    highest = jnp.max(scores, axis=0, keepdims=True)
    expo = jnp.exp(scores - highest)
    totals = jnp.sum(expo, axis=0, keepdims=True)
    attended = contract(v_ref[...], expo.astype(BF16), 1, 0) / totals
    attended_ref[...] = attended
    log_ref[...] = highest + jnp.log(totals)
    low = attended.astype(BF16)
    for piece in range(low.shape[1] // tokens):
        mixed_ref[piece] = low[:, piece * tokens : (piece + 1) * tokens]


def backward_kernel(
    tokens,
    q_ref,
    k_ref,
    v_ref,
    key_id_ref,
    query_id_ref,
    slot_ref,
    attended_ref,
    log_ref,
    grad_ref,
    dq_ref,
    dk_ref,
    dv_ref,
    dk_sum,
    dv_sum,
):
    step = pl.program_id(0)
    queries = q_ref[...]
    pieces = grad_ref.shape[0]
    grads = jnp.concatenate([grad_ref[piece] for piece in range(pieces)], axis=1)
    scores = masked_scores(k_ref[...], queries, key_id_ref[...], query_id_ref[...], slot_ref[...])
    probs = jnp.exp(scores - log_ref[...])
    delta = jnp.sum(grads.astype(F32) * attended_ref[...], axis=0, keepdims=True)
    dprob = contract(v_ref[...], grads, 0, 0)
    dscore = (probs * (dprob - delta)).astype(BF16)
    dq_ref[...] = (contract(k_ref[...], dscore, 1, 0) * SCALING).astype(BF16)
    dk = contract(queries, dscore, 1, 1)
    dv = contract(grads, probs.astype(BF16), 1, 1)

    @pl.when(step == 0)
    def _():
        dk_sum[...] = dk
        dv_sum[...] = dv

    @pl.when(step > 0)
    def _():
        dk_sum[...] += dk
        dv_sum[...] += dv

    @pl.when(step == pl.num_programs(0) - 1)
    def _():
        dk_ref[...] = dk_sum[...].astype(BF16)
        dv_ref[...] = dv_sum[...].astype(BF16)


def attention_forward(queries, keys, values, key_ids, query_ids, slots, tokens):
    length, count = keys.shape[1], queries.shape[1]
    block = min(256, count)
    whole = pl.BlockSpec((HDIM, length), lambda i: (0, 0))
    part = pl.BlockSpec((HDIM, block), lambda i: (0, i))
    row = pl.BlockSpec((1, block), lambda i: (0, i))
    return pl.pallas_call(
        functools.partial(forward_kernel, tokens),
        grid=(count // block,),
        in_specs=[
            part, whole, whole, pl.BlockSpec((length, 1), lambda i: (0, 0)), row, row
        ],
        out_specs=[
            pl.BlockSpec((block // tokens, HDIM, tokens), lambda i: (i, 0, 0)), part, row
        ],
        out_shape=[
            jax.ShapeDtypeStruct((count // tokens, HDIM, tokens), BF16),
            jax.ShapeDtypeStruct((HDIM, count), F32),
            jax.ShapeDtypeStruct((1, count), F32),
        ],
        compiler_params=pltpu.CompilerParams(vmem_limit_bytes=50 << 20),
        cost_estimate=pl.CostEstimate(
            flops=4 * HDIM * length * count,
            bytes_accessed=8 * HDIM * length,
            transcendentals=length * count,
        ),
    )(queries, keys, values, key_ids, query_ids, slots)


def attention_backward(
    queries, keys, values, key_ids, query_ids, slots, attended, logs, grads, tokens
):
    length, count = keys.shape[1], queries.shape[1]
    block = min(256, count)
    whole = pl.BlockSpec((HDIM, length), lambda i: (0, 0))
    part = pl.BlockSpec((HDIM, block), lambda i: (0, i))
    row = pl.BlockSpec((1, block), lambda i: (0, i))
    return pl.pallas_call(
        functools.partial(backward_kernel, tokens),
        grid=(count // block,),
        in_specs=[
            part,
            whole,
            whole,
            pl.BlockSpec((length, 1), lambda i: (0, 0)),
            row,
            row,
            part,
            row,
            pl.BlockSpec((block // tokens, HDIM, tokens), lambda i: (i, 0, 0)),
        ],
        out_specs=[part, whole, whole],
        out_shape=[
            jax.ShapeDtypeStruct((HDIM, count), BF16),
            jax.ShapeDtypeStruct((HDIM, length), BF16),
            jax.ShapeDtypeStruct((HDIM, length), BF16),
        ],
        scratch_shapes=[pltpu.VMEM((HDIM, length), F32)] * 2,
        compiler_params=pltpu.CompilerParams(vmem_limit_bytes=56 << 20),
        cost_estimate=pl.CostEstimate(
            flops=10 * HDIM * length * count,
            bytes_accessed=16 * HDIM * length,
            transcendentals=length * count,
        ),
    )(queries, keys, values, key_ids, query_ids, slots, attended, logs, grads)


def flip(array, bit, size):
    return lax.ppermute(array, "seq", [(i, i ^ bit) for i in range(size)])


def shifter(axis, size, stride):
    def shift(array, step):
        return lax.ppermute(
            array, axis, [(i, (i + step * stride) % size) for i in range(size)]
        )

    return shift


def ring_gather(block, ring, shift):
    rows = block.shape[0]
    pieces = [(0, 0, block)]
    right = left = block
    for step in range(1, (ring - 1) // 2 + 1):
        right, left = shift(right, 1), shift(left, -1)
        pieces += [(-step, 0, right), (step, 0, left)]
    if ring == 2:
        pieces.append((1, 0, shift(block, 1)))
    elif ring % 2 == 0:
        half = rows // 2
        pieces.append((ring // 2, 0, shift(right[:half], 1)))
        pieces.append((ring // 2, half, shift(left[half:], -1)))
    return pieces


def ring_reduce(block_at, ring, shift):
    if ring == 1:
        return block_at(0)
    if ring == 2:
        return block_at(0) + shift(block_at(1).astype(BF16), 1)
    right = left = None
    if ring % 2 == 0:
        far = block_at(ring // 2).astype(BF16)
        half = far.shape[0] // 2
        right, left = shift(far[:half], 1), shift(far[half:], -1)
        for_right, for_left = block_at(ring // 2 - 1), block_at(1 - ring // 2)
        for_right = jnp.concatenate([for_right[:half] + right, for_right[half:]])
        for_left = jnp.concatenate([for_left[:half], for_left[half:] + left])
        steps = ring // 2 - 1
    else:
        steps = (ring - 1) // 2
        for_right, for_left = block_at(steps), block_at(-steps)
    for step in range(steps, 0, -1):
        right, left = shift(for_right.astype(BF16), 1), shift(for_left.astype(BF16), -1)
        for_right, for_left = block_at(step - 1) + right, left
        if step > 1:
            for_left = block_at(1 - step) + left
    return for_right + for_left


def quad_gather(rows, size):
    rows = jnp.concatenate([rows, flip(rows, 2, size)], axis=0)
    return jnp.concatenate([rows, flip(rows, 1, size)], axis=0)


def quad_scatter(rows, size):
    half = rows.shape[0] // 2
    rows = rows[:half] + flip(rows[half:].astype(BF16), 1, size)
    half = half // 2
    return rows[:half] + flip(rows[half:].astype(BF16), 2, size)


def standardize(values):
    average = jnp.mean(values, axis=-1, keepdims=True)
    centred = values - average
    variance = jnp.mean(centred * centred, axis=-1, keepdims=True)
    inverse = lax.rsqrt(variance + EPSILON)
    return centred * inverse, inverse


def standardize_back(grad, hat, inverse):
    return inverse * (
        grad
        - jnp.mean(grad, axis=-1, keepdims=True)
        - hat * jnp.mean(grad * hat, axis=-1, keepdims=True)
    )


def gelu_exact(values):
    return jax.nn.gelu(values, approximate=False)


def local(
    seqs,
    batches,
    patches,
    cotangent,
    segment_ids,
    kept_mask,
    first_gain,
    qkv_weight,
    out_weight,
    second_gain,
    up_weight,
    down_weight,
):
    width = HEADS * HDIM
    tokens = patches.shape[1]
    length = tokens * seqs
    devices = seqs * batches
    groups = seqs // QUAD
    splits = seqs // HEADS
    count = length // splits
    lines = qkv_weight.shape[0]
    hidden_rows = down_weight.shape[0]
    quarter = hidden_rows * groups * batches
    place = lax.axis_index("seq")
    group, at_batch = place // QUAD, lax.axis_index("batch")
    quads = [[QUAD * g + q for q in range(QUAD)] for g in range(groups)]
    along_groups = shifter("seq", seqs, QUAD)
    along_batch = shifter("batch", batches, 1)

    inputs = patches[0].astype(F32)
    first_hat, first_inverse = standardize(inputs)
    own = first_hat.astype(BF16)
    near = jnp.concatenate([own, flip(own, 2, seqs)], axis=0)
    first_all = jnp.zeros((groups, 2, 2, tokens, width), BF16)
    zero = jnp.int32(0)
    swap_x, swap_core = (place // 2) % 2, place % 2
    side = tokens
    for distance, start, piece in ring_gather(near, groups, along_groups):
        at = (group + distance) % groups
        both = [(swap_core, piece), (1 - swap_core, flip(piece, 1, seqs))]
        for core, part in both:
            for row in range(start, start + part.shape[0], side):
                x = swap_x if row == 0 else 1 - swap_x
                first_all = lax.dynamic_update_slice(
                    first_all,
                    part[row - start : row - start + side][None, None, None],
                    (at, x, core, zero, zero),
                )
    first_all = first_all.reshape(length, width)

    first_rows = first_gain.astype(F32)[:, None]
    second_rows = second_gain.astype(F32)[:, None]
    qkv_rows = (qkv_weight.astype(F32) * first_rows).astype(BF16)
    qkv_rows = qkv_rows.reshape(lines, 3, HEADS, HDIM).transpose(2, 0, 1, 3)
    sent = jnp.broadcast_to(
        qkv_rows.reshape(HEADS, 1, lines, 3 * HDIM), (HEADS, splits * batches, lines, 3 * HDIM)
    )
    head_weight = lax.all_to_all(
        sent.reshape(devices, lines, 3 * HDIM), EVERY, split_axis=0, concat_axis=0, tiled=True
    ).reshape(width, 3 * HDIM)
    wide = jnp.concatenate(
        [out_weight, qkv_rows.transpose(1, 0, 2, 3).reshape(lines, 3 * width)], axis=1
    )
    wide = lax.all_gather(wide, EVERY, axis=0, tiled=True)
    out_full, qkv_full = wide[:, :width], wide[:, width:]

    up_rows = (up_weight.astype(F32) * second_rows).astype(BF16)
    up_rows = up_rows.reshape(lines, groups, QUAD, batches, hidden_rows).transpose(2, 0, 1, 3, 4)
    up_rows = lax.all_to_all(
        up_rows.reshape(QUAD, lines, quarter),
        "seq",
        split_axis=0,
        concat_axis=0,
        tiled=True,
        axis_index_groups=quads,
    )
    split_rows = QUAD * lines
    packed = jnp.concatenate(
        [up_rows.reshape(split_rows, quarter), down_weight.reshape(-1, quarter)], axis=0
    )
    up_quarter = jnp.zeros((groups, QUAD, batches, lines, quarter), BF16)
    down_quarter = jnp.zeros((groups, batches, packed.shape[0] - split_rows, quarter), BF16)
    for distance, start, piece in ring_gather(packed, groups, along_groups):
        at_group = (group + distance) % groups
        for hop, inner, part in ring_gather(piece, batches, along_batch):
            at = (at_batch + hop) % batches
            first = start + inner
            if first < split_rows:
                up_quarter = lax.dynamic_update_slice(
                    up_quarter,
                    part[: split_rows - first].reshape(1, -1, 1, lines, quarter),
                    (at_group, jnp.int32(first // lines), at, zero, zero),
                )
            if first + part.shape[0] > split_rows:
                skip = max(split_rows - first, 0)
                down_quarter = lax.dynamic_update_slice(
                    down_quarter,
                    part[skip:][None, None],
                    (at_group, at, jnp.int32(first + skip - split_rows), zero),
                )
    up_quarter = up_quarter.reshape(width, quarter)
    down_quarter = down_quarter.reshape(quarter, width)
    upstream = cotangent[0]
    upstream_quad = quad_gather(upstream, seqs)

    project = contract(head_weight, first_all, 0, 1)
    keys = project[HDIM : 2 * HDIM].astype(BF16)
    values = project[2 * HDIM :].astype(BF16)
    ids = segment_ids[0]
    key_ids = jnp.where(kept_mask[0] == 1, ids, -1)[:, None]
    begin = (place % splits) * count
    queries = (project[:HDIM] * SCALING).astype(BF16)
    queries = lax.dynamic_slice_in_dim(queries, begin, count, 1)
    query_ids = lax.dynamic_slice_in_dim(ids, begin, count, 0)[None]
    slots = (begin + jnp.arange(count, dtype=jnp.int32))[None]
    mixed_blocks, attended, logs = attention_forward(
        queries, keys, values, key_ids, query_ids, slots, tokens
    )
    if splits > 1:
        sent = jnp.zeros((seqs, HDIM, tokens), BF16)
        mixed_blocks = lax.dynamic_update_slice_in_dim(sent, mixed_blocks, begin // tokens, 0)
    mixed = lax.all_to_all(mixed_blocks, "seq", split_axis=0, concat_axis=0, tiled=True)
    if splits > 1:
        mixed = mixed.reshape(HEADS, splits, HDIM, tokens).sum(1)
    mixed = mixed.reshape(width, tokens)

    middle = inputs + contract(mixed, out_full, 0, 0)
    second_hat, second_inverse = standardize(middle)
    second_quad = quad_gather(second_hat.astype(BF16), seqs)
    hidden_pre = contract(second_quad, up_quarter, 1, 0)
    hidden, gelu_back = jax.vjp(gelu_exact, hidden_pre)
    hidden = hidden.astype(BF16)
    hidden_grad = contract(upstream_quad, down_quarter, 1, 1)
    pre_grad = gelu_back(hidden_grad)[0].astype(BF16)
    second_grad = quad_scatter(contract(pre_grad, up_quarter, 1, 1), seqs)
    middle_grad = upstream.astype(F32) + standardize_back(second_grad, second_hat, second_inverse)
    middle_low = middle_grad.astype(BF16)
    mixed_grad = contract(out_full, middle_low, 1, 1).astype(BF16)

    sent = jnp.broadcast_to(
        mixed_grad.reshape(HEADS, 1, HDIM, tokens), (HEADS, splits, HDIM, tokens)
    ).reshape(seqs, HDIM, tokens)
    grads = lax.all_to_all(sent, "seq", split_axis=0, concat_axis=0, tiled=True)
    grads = lax.dynamic_slice_in_dim(grads, begin // tokens, count // tokens, 0)
    dq, dk, dv = attention_backward(
        queries, keys, values, key_ids, query_ids, slots, attended, logs, grads, tokens
    )
    if splits > 1:
        dq = lax.dynamic_update_slice_in_dim(jnp.zeros((HDIM, length), BF16), dq, begin, 1)
    project_grad = jnp.concatenate([dq, dk, dv], axis=0)
    sent = project_grad.reshape(3 * HDIM, seqs, tokens).transpose(1, 0, 2)
    got = lax.all_to_all(sent, "seq", split_axis=0, concat_axis=0, tiled=True)
    if splits > 1:
        got = got.reshape(HEADS, splits, 3 * HDIM, tokens).sum(1)
    first_grad = contract(got.reshape(3 * width, tokens), qkv_full, 0, 1)
    input_grad = middle_grad + standardize_back(first_grad, first_hat, first_inverse)
    input_grad = input_grad.astype(BF16)

    block_output = middle + quad_scatter(contract(hidden, down_quarter, 1, 0), seqs)
    block_output = block_output.astype(BF16)

    qkv_terms = contract(first_all, project_grad, 0, 1).astype(BF16)
    qkv_terms = lax.all_to_all(
        qkv_terms.reshape(devices, lines, 3 * HDIM), EVERY, split_axis=0, concat_axis=0, tiled=True
    )
    qkv_sum = qkv_terms.reshape(HEADS, splits * batches, lines, 3, HDIM).astype(F32).sum(1)
    qkv_sum = qkv_sum.transpose(1, 2, 0, 3).reshape(lines, 3 * width)

    out_terms = contract(mixed, middle_low, 1, 0).astype(BF16)
    out_sum = lax.psum_scatter(out_terms, EVERY, scatter_dimension=0, tiled=True).astype(F32)

    up_terms = contract(second_quad, pre_grad, 0, 0).astype(BF16)
    up_terms = up_terms.reshape(groups, QUAD, batches, lines, quarter)
    down_terms = contract(hidden, upstream_quad, 0, 0).astype(BF16)
    down_terms = down_terms.reshape(groups, batches, hidden_rows, width)

    def scatter(terms, rows):
        def for_batch(distance):
            at = (at_batch + distance) % batches
            return lax.dynamic_index_in_dim(terms, at, 1, keepdims=False)

        mine = ring_reduce(for_batch, batches, along_batch)

        def for_group(distance):
            at = (group + distance) % groups
            return lax.dynamic_index_in_dim(mine, at, 0, keepdims=False)

        return ring_reduce(for_group, groups, along_groups).astype(F32)

    down_sum = scatter(down_terms, hidden_rows)
    up_sum = scatter(
        up_terms.transpose(0, 2, 1, 3, 4).reshape(groups, batches, QUAD * lines, quarter),
        QUAD * lines,
    )
    up_sum = lax.all_to_all(
        up_sum.astype(BF16).reshape(QUAD, lines, quarter),
        "seq",
        split_axis=0,
        concat_axis=0,
        tiled=True,
        axis_index_groups=quads,
    ).astype(F32)
    up_sum = up_sum.reshape(QUAD, lines, groups, batches, hidden_rows).transpose(1, 2, 0, 3, 4)
    up_sum = up_sum.reshape(lines, -1)

    first_gain_grad = jnp.sum(qkv_weight.astype(F32) * qkv_sum, axis=1)
    second_gain_grad = jnp.sum(up_weight.astype(F32) * up_sum, axis=1)
    return (
        block_output[None],
        input_grad[None],
        first_gain_grad,
        qkv_sum * first_rows,
        out_sum,
        second_gain_grad,
        up_sum * second_rows,
        down_sum,
    )


def solution(mesh):
    rows = P(EVERY)
    tokens = P("batch", "seq", None)
    in_specs = (
        tokens, tokens, P("batch", None), P("batch", None), rows, P(EVERY, None), P(EVERY, None),
        rows, P(EVERY, None), P(EVERY, None),
    )
    out_specs = (
        tokens, tokens, rows, P(EVERY, None), P(EVERY, None), rows, P(EVERY, None), P(EVERY, None)
    )
    body = functools.partial(local, mesh.shape["seq"], mesh.shape["batch"])
    return jax.shard_map(body, mesh=mesh, in_specs=in_specs, out_specs=out_specs, check_vma=False)
```

```python
import functools
import math

import jax
import jax.numpy as jnp
from jax import lax
from jax.experimental import pallas as pl
from jax.experimental.pallas import tpu as pltpu
from jax.sharding import PartitionSpec as P

HEADS = 16
HDIM = 64
QUAD = 4
EIGHT = 8

EPSILON = 1e-05
MASKED = -1e30
SCALING = HDIM**-0.5
BF16 = jnp.bfloat16
F32 = jnp.float32
EVERY = ("seq", "batch")
LARGE = pl.CostEstimate(flops=30_000_000_000, bytes_accessed=1, transcendentals=0)
VMEM_LIMIT = 60 << 20
SMALL = pl.CostEstimate(flops=1, bytes_accessed=1, transcendentals=0)


def contract(left, right, left_dim, right_dim):
    return lax.dot_general(
        left, right, (((left_dim,), (right_dim,)), ((), ())), preferred_element_type=F32
    )


def masked_scores(keys, queries, key_ids, query_ids, first):
    scores = contract(keys, queries, 0, 0)
    slots = lax.broadcasted_iota(jnp.int32, scores.shape, 0)
    columns = first + lax.broadcasted_iota(jnp.int32, scores.shape, 1)
    allowed = (key_ids == query_ids) | (slots == columns)
    return jnp.where(allowed, scores, MASKED)


def load_heads(own_ref, other_ref, held, key_id_ref, key_column):
    half = own_ref.shape[1]
    held[:, :half] = own_ref[...]
    held[:, half:] = other_ref[...]
    key_column[...] = jnp.broadcast_to(key_id_ref[...], (8, 2 * half)).T[:, :1]


def forward_kernel(
    tokens, core_ref, own_ref, other_ref, key_id_ref, query_id_ref, mixed_ref, attended_ref,
    log_ref, held, key_column,
):
    step = pl.program_id(0)

    @pl.when(step == 0)
    def _():
        load_heads(own_ref, other_ref, held, key_id_ref, key_column)

    block = attended_ref.shape[1]
    first = pl.multiple_of(step * block, block)
    queries = held[:HDIM, pl.ds(first, block)]
    scores = masked_scores(
        held[HDIM : 2 * HDIM, :], queries, key_column[...], query_id_ref[...], first
    )
    highest = jnp.max(scores, axis=0, keepdims=True)
    expo = jnp.exp(scores - highest)
    totals = jnp.sum(expo, axis=0, keepdims=True)
    attended = contract(held[2 * HDIM :, :], expo.astype(BF16), 1, 0) / totals
    attended_ref[...] = attended
    log_ref[...] = highest + jnp.log(totals)
    low = attended.astype(BF16)
    for x in range(2):
        mixed_ref[0, x, 0] = low[:, x * tokens : (x + 1) * tokens]


def backward_kernel(
    tokens, core_ref, own_ref, other_ref, key_id_ref, query_id_ref, attended_ref, log_ref, grad_ref,
    out_ref, own_grad_ref, other_grad_ref, held, key_column, dk_sum, dv_sum,
):
    step = pl.program_id(0)
    steps = pl.num_programs(0)
    groups = out_ref.shape[0]
    half = own_ref.shape[1]

    @pl.when(step == 0)
    def _():
        load_heads(own_ref, other_ref, held, key_id_ref, key_column)
        dk_sum[...] = jnp.zeros_like(dk_sum)
        dv_sum[...] = jnp.zeros_like(dv_sum)

    block = attended_ref.shape[1]
    first = pl.multiple_of(step * block, block)
    queries = held[:HDIM, pl.ds(first, block)]
    keys = held[HDIM : 2 * HDIM, :]
    grads = jnp.concatenate([grad_ref[0, x, 0] for x in range(2)], axis=1)
    scores = masked_scores(keys, queries, key_column[...], query_id_ref[...], first)
    probs = jnp.exp(scores - log_ref[...])
    delta = jnp.sum(grads.astype(F32) * attended_ref[...], axis=0, keepdims=True)
    dprob = contract(held[2 * HDIM :, :], grads, 0, 0)
    dscore = (probs * (dprob - delta)).astype(BF16)
    dq = (contract(keys, dscore, 1, 0) * SCALING).astype(BF16)
    dk_sum[...] += contract(queries, dscore, 1, 1)
    dv_sum[...] += contract(grads, probs.astype(BF16), 1, 1)
    side = step // groups
    core = jnp.where(side == 0, core_ref[0], 1 - core_ref[0])
    for x in range(2):
        out_ref[step % groups, x, core, :HDIM, :] = dq[:, x * tokens : (x + 1) * tokens]
    inside = pl.multiple_of((step % groups) * block, block)

    @pl.when(side == 0)
    def _():
        own_grad_ref[:HDIM, pl.ds(inside, block)] = dq

    @pl.when(side == 1)
    def _():
        other_grad_ref[:HDIM, pl.ds(inside, block)] = dq

    @pl.when(step == steps - 1)
    def _():
        for first_row, total in ((HDIM, dk_sum), (2 * HDIM, dv_sum)):
            rows = pl.ds(first_row, HDIM)
            low = total[...].astype(BF16)
            own_grad_ref[rows, :] = low[:, :half]
            other_grad_ref[rows, :] = low[:, half:]
            for side_at in range(2):
                to_core = core_ref[0] if side_at == 0 else 1 - core_ref[0]
                for group in range(groups):
                    for x in range(2):
                        at = side_at * half + (2 * group + x) * tokens
                        out_ref[group, x, to_core, rows, :] = low[:, at : at + tokens]
        if steps < 2 * groups:
            other_grad_ref[:HDIM, :] = jnp.zeros((HDIM, half), BF16)
            for group in range(groups):
                for x in range(2):
                    out_ref[group, x, 1 - core_ref[0], :HDIM, :] = jnp.zeros((HDIM, tokens), BF16)


def side_core(step, groups, core):
    return jnp.where(step < groups, core, 1 - core)


def attention_specs(length, block, tokens, groups):
    half = length // 2
    whole = pl.BlockSpec((3 * HDIM, half), lambda i, core: (0, 0))
    part = pl.BlockSpec((HDIM, block), lambda i, core: (0, i))
    row = pl.BlockSpec((1, block), lambda i, core: (0, i))
    column = pl.BlockSpec((1, length), lambda i, core: (0, 0))
    tile = pl.BlockSpec(
        (1, 2, 1, HDIM, tokens),
        lambda i, core: (i % groups, 0, side_core(i, groups, core[0]), 0, 0),
    )
    return whole, part, row, column, tile


def attention_forward(core, own, other, key_ids, query_ids, tokens, splits):
    length = 2 * own.shape[1]
    block = 2 * tokens
    groups = length // (2 * block)
    count = length // splits
    whole, part, row, column, tile = attention_specs(length, block, tokens, groups)
    return pl.pallas_call(
        functools.partial(forward_kernel, tokens),
        grid_spec=pltpu.PrefetchScalarGridSpec(
            num_scalar_prefetch=1,
            grid=(count // block,),
            in_specs=[whole, whole, column, row],
            out_specs=[tile, part, row],
            scratch_shapes=[
                pltpu.VMEM((3 * HDIM, length), BF16), pltpu.VMEM((length, 1), jnp.int32)
            ],
        ),
        out_shape=[
            jax.ShapeDtypeStruct((groups, 2, 2, HDIM, tokens), BF16),
            jax.ShapeDtypeStruct((HDIM, count), F32),
            jax.ShapeDtypeStruct((1, count), F32),
        ],
        compiler_params=pltpu.CompilerParams(vmem_limit_bytes=VMEM_LIMIT),
        cost_estimate=SMALL,
    )(core, own, other, key_ids, query_ids)


def attention_backward(core, own, other, key_ids, query_ids, attended, logs, grads, tokens, splits):
    length = 2 * own.shape[1]
    half = length // 2
    block = 2 * tokens
    groups = length // (2 * block)
    count = length // splits
    whole, part, row, column, tile = attention_specs(length, block, tokens, groups)
    return pl.pallas_call(
        functools.partial(backward_kernel, tokens),
        grid_spec=pltpu.PrefetchScalarGridSpec(
            num_scalar_prefetch=1,
            grid=(count // block,),
            in_specs=[whole, whole, column, row, part, row, tile],
            out_specs=[
                pl.BlockSpec(
                    (groups, 2, 2, 3 * HDIM, tokens), lambda i, core: (0, 0, 0, 0, 0)
                ),
                whole,
                whole,
            ],
            scratch_shapes=[
                pltpu.VMEM((3 * HDIM, length), BF16),
                pltpu.VMEM((length, 1), jnp.int32),
                pltpu.VMEM((HDIM, length), F32),
                pltpu.VMEM((HDIM, length), F32),
            ],
        ),
        out_shape=[
            jax.ShapeDtypeStruct((groups, 2, 2, 3 * HDIM, tokens), BF16),
            jax.ShapeDtypeStruct((3 * HDIM, half), BF16),
            jax.ShapeDtypeStruct((3 * HDIM, half), BF16),
        ],
        compiler_params=pltpu.CompilerParams(vmem_limit_bytes=VMEM_LIMIT),
        cost_estimate=LARGE,
    )(core, own, other, key_ids, query_ids, attended, logs, grads)


def project_kernel(layout, tokens, where_ref, mine_w_ref, theirs_w_ref, *refs):
    pieces, (mine_ref, theirs_ref, all_ref) = refs[:-3], refs[-3:]
    for index, (source, row) in enumerate(layout):
        if isinstance(source, tuple):
            hat = jnp.concatenate([pieces[member][...] for member in source], axis=0)
        else:
            hat = pieces[source][row : row + tokens]
        at = where_ref[index]
        columns = pl.ds(pl.multiple_of(at * tokens, tokens), tokens)
        mine_ref[:, columns] = contract(mine_w_ref[...], hat, 1, 1).astype(BF16)
        theirs_ref[:, columns] = contract(theirs_w_ref[...], hat, 1, 1).astype(BF16)
        all_ref[at] = hat


def project_pieces(where, mine_w, theirs_w, pieces, layout, tokens):
    blocks = len(layout)
    width = mine_w.shape[1]
    columns = mine_w.shape[0]
    return whole_call(
        functools.partial(project_kernel, layout, tokens),
        where,
        [mine_w, theirs_w, *pieces],
        [
            jax.ShapeDtypeStruct((columns, blocks * tokens), BF16),
            jax.ShapeDtypeStruct((columns, blocks * tokens), BF16),
            jax.ShapeDtypeStruct((blocks, tokens, width), BF16),
        ],
    )


def whole(array):
    rank = len(array.shape)
    return pl.BlockSpec(array.shape, lambda *step: (0,) * rank)


def whole_call(kernel, scalars, arrays, outs, scratch=(), cost=SMALL):
    return pl.pallas_call(
        kernel,
        grid=(1,),
        in_specs=[pl.BlockSpec(memory_space=pltpu.SMEM)] + [whole(array) for array in arrays],
        out_specs=[whole(out) for out in outs],
        out_shape=outs,
        scratch_shapes=list(scratch),
        compiler_params=pltpu.CompilerParams(vmem_limit_bytes=VMEM_LIMIT),
        cost_estimate=cost,
    )(scalars, *arrays)


def together(refs):
    values = [ref[...] for ref in refs]
    return values[0] if len(values) == 1 else jnp.concatenate(values, axis=0)


def mlp_kernel(count, toggles, place_ref, *refs):
    pieces, refs = refs[:count], refs[count:]
    all_ref, up_ref, down_ref, hidden_ref, pre_grad_ref = refs[:5]
    hat = together(pieces)
    upstream = jnp.concatenate([all_ref[place_ref[0] ^ toggle] for toggle in toggles], axis=0)
    units = up_ref.shape[1]
    block = min(256, units)
    grad = out = None
    for first in range(0, units, block):
        chunk = slice(first, first + block)
        up, down = up_ref[:, chunk], down_ref[chunk, :]
        pre = contract(hat, up, 1, 0)
        cdf = 0.5 * (1.0 + lax.erf(pre * (0.5**0.5)))
        slope = cdf + pre * jnp.exp(-0.5 * pre * pre) * ((2.0 * math.pi) ** -0.5)
        hidden = (pre * cdf).astype(BF16)
        pre_grad = (contract(upstream, down, 1, 1) * slope).astype(BF16)
        hidden_ref[:, chunk] = hidden
        pre_grad_ref[:, chunk] = pre_grad
        grad_term = contract(pre_grad, up, 1, 1)
        out_term = contract(hidden, down, 1, 0)
        grad = grad_term if grad is None else grad + grad_term
        out = out_term if out is None else out + out_term
    for total, kept_refs in ((out, refs[5 : 5 + count]), (grad, refs[5 + count :])):
        first = 0
        for ref in kept_refs:
            ref[...] = total[first : first + ref.shape[0]].astype(ref.dtype)
            first += ref.shape[0]


def mlp(hats, toggles, place, upstream_all, up, down):
    count = len(hats)
    rows = sum(hat.shape[0] for hat in hats)
    width, units = up.shape
    sums = [
        jax.ShapeDtypeStruct(hat.shape, F32 if 2 * index < count else BF16)
        for index, hat in enumerate(hats)
    ]
    outs = whole_call(
        functools.partial(mlp_kernel, count, toggles),
        place,
        [*hats, upstream_all, up, down],
        [
            jax.ShapeDtypeStruct((rows, units), BF16),
            jax.ShapeDtypeStruct((rows, units), BF16),
            *sums,
            *sums,
        ],
    )
    return outs[0], outs[1], list(outs[2 : 2 + count]), list(outs[2 + count :])


def mlp_weight_kernel(counts, toggles, blocks, at_ref, *refs):
    hats, pres, hiddens = (
        refs[: counts[0]], refs[counts[0] : sum(counts[:2])], refs[sum(counts[:2]) : sum(counts)]
    )
    refs = refs[sum(counts) :]
    all_ref, up_refs, down_refs = refs[0], refs[1 : 1 + blocks], refs[1 + blocks : 1 + 2 * blocks]
    hat_held, hidden_held = refs[1 + 2 * blocks :]
    hat_held[...] = together(hats)
    hidden_held[...] = together(hiddens)
    pre_grad = together(pres)
    upstream = jnp.concatenate([all_ref[at_ref[0] ^ toggle] for toggle in toggles], axis=0)
    for index in range(blocks):
        for held, other, out_ref in (
            (hat_held, pre_grad, up_refs[index]), (hidden_held, upstream, down_refs[index])
        ):
            wide = out_ref.shape[0]
            columns = pl.ds(pl.multiple_of(at_ref[1 + index] * wide, wide), wide)
            out_ref[...] = contract(held[:, columns], other, 0, 0).astype(BF16)


def mlp_weight_terms(numbers, blocks, hats, toggles, pres, hiddens, upstream_all):
    tokens = sum(hat.shape[0] for hat in hats)
    width, units = hats[0].shape[1], pres[0].shape[1]
    counts = (len(hats), len(pres), len(hiddens))
    outs = whole_call(
        functools.partial(mlp_weight_kernel, counts, toggles, blocks),
        numbers,
        [*hats, *pres, *hiddens, upstream_all],
        [jax.ShapeDtypeStruct((width // blocks, units), BF16)] * blocks
        + [jax.ShapeDtypeStruct((units // blocks, width), BF16)] * blocks,
        [pltpu.VMEM((tokens, width), BF16), pltpu.VMEM((tokens, units), BF16)],
        LARGE,
    )
    return list(outs[:blocks]), list(outs[blocks:])


def out_weight_kernel(order, at_ref, mixed_ref, grad_ref, *refs):
    out_refs, held = refs[:-1], refs[-1]
    terms = contract(mixed_ref[...], grad_ref[...], 1, 0).astype(BF16)
    held[...] = terms.reshape(held.shape)
    for index, ref in enumerate(out_refs):
        toggle_core, toggle_x = index // 2, index % 2
        for y in range(2):
            for block, (g, p) in enumerate(order):
                ref[y, block] = held[
                    at_ref[g], at_ref[0] ^ toggle_x, at_ref[1] ^ toggle_core, at_ref[p],
                    at_ref[2] ^ y,
                ]


def out_weight_terms(at, order, mixed, grad, shape):
    lines, width = shape[-2:]
    return whole_call(
        functools.partial(out_weight_kernel, order),
        at,
        [mixed, grad],
        [jax.ShapeDtypeStruct((2, len(order), lines, width), BF16)] * 4,
        [pltpu.VMEM(shape, BF16)],
        LARGE,
    )


def finish_input_kernel(got_ref, weight_ref, hat_ref, inverse_ref, middle_ref, out_ref, total):
    step = pl.program_id(0)
    term = contract(got_ref[...], weight_ref[...], 0, 1)

    @pl.when(step == 0)
    def _():
        total[...] = term

    @pl.when(step > 0)
    def _():
        total[...] += term

    @pl.when(step == pl.num_programs(0) - 1)
    def _():
        grad = standardize_back(total[...], hat_ref[...], inverse_ref[...])
        out_ref[...] = (middle_ref[...] + grad).astype(BF16)


def finish_input(got, weight, hat, inverse, middle_grad):
    columns, tokens = got.shape
    width = weight.shape[0]
    block = columns // 4
    rows = [hat, inverse, middle_grad]
    return pl.pallas_call(
        finish_input_kernel,
        grid=(4,),
        in_specs=[
            pl.BlockSpec((block, tokens), lambda i: (i, 0)),
            pl.BlockSpec((width, block), lambda i: (0, i)),
            *[whole(array) for array in rows],
        ],
        out_specs=pl.BlockSpec((tokens, width), lambda i: (0, 0)),
        out_shape=jax.ShapeDtypeStruct((tokens, width), BF16),
        scratch_shapes=[pltpu.VMEM((tokens, width), F32)],
        compiler_params=pltpu.CompilerParams(vmem_limit_bytes=VMEM_LIMIT),
        cost_estimate=LARGE,
    )(got, weight, *rows)


def finish_qkv_kernel(gain_ref, terms_ref, weight_ref, out_ref, gain_grad_ref):
    copies = terms_ref.shape[0] // HEADS
    gains = gain_ref[...]
    total = None
    for head in range(HEADS):
        term = terms_ref[head * copies].astype(F32)
        for copy in range(1, copies):
            term += terms_ref[head * copies + copy].astype(F32)
        for kind in range(3):
            first = (kind * HEADS + head) * HDIM
            columns = slice(first, first + HDIM)
            part = term[:, kind * HDIM : (kind + 1) * HDIM]
            out_ref[:, columns] = part * gains
            part = part * weight_ref[:, columns].astype(F32)
            total = part if total is None else total + part
    gain_grad_ref[...] = jnp.sum(total, axis=1, keepdims=True)


def finish_qkv(gains, terms, weight):
    lines, columns = weight.shape
    outs = [
        jax.ShapeDtypeStruct((lines, columns), F32), jax.ShapeDtypeStruct((lines, 1), F32)
    ]
    arrays = [gains, terms, weight]
    return pl.pallas_call(
        finish_qkv_kernel,
        grid=(1,),
        in_specs=[whole(array) for array in arrays],
        out_specs=[whole(out) for out in outs],
        out_shape=outs,
        compiler_params=pltpu.CompilerParams(vmem_limit_bytes=VMEM_LIMIT),
        cost_estimate=SMALL,
    )(*arrays)


def finish_up_kernel(sizes, at_ref, gain_ref, near_ref, far_ref, weight_ref, out_ref, gain_grad_ref):
    groups, batches = sizes
    chunk = near_ref.shape[-1] // (groups * (batches // 2))
    gains = gain_ref[...]
    total = None
    for y, ref in enumerate((near_ref, far_ref)):
        for x in range(2):
            for core in range(2):
                quad = 2 * (at_ref[0] ^ x) + (at_ref[1] ^ core)
                term = ref[x, core].astype(F32)
                for index in range(groups * (batches // 2)):
                    group, pair = index // (batches // 2), index % (batches // 2)
                    block = (QUAD * group + quad) * batches + 2 * pair + (at_ref[2] ^ y)
                    columns = pl.ds(pl.multiple_of(block * chunk, chunk), chunk)
                    part = term[:, index * chunk : (index + 1) * chunk]
                    out_ref[:, columns] = part * gains
                    part = part * weight_ref[:, columns].astype(F32)
                    total = part if total is None else total + part
    gain_grad_ref[...] = jnp.sum(total, axis=1, keepdims=True)


def finish_up(at, gains, near, far, weight, sizes):
    lines, columns = weight.shape
    return whole_call(
        functools.partial(finish_up_kernel, sizes),
        at,
        [gains, near, far, weight],
        [jax.ShapeDtypeStruct((lines, columns), F32), jax.ShapeDtypeStruct((lines, 1), F32)],
    )


def place_kernel(plan, count, at_ref, *refs):
    sources, targets = refs[:count], refs[count:]
    for source, block, lanes, target, where in plan:
        rows = sources[source][block] if lanes is None else sources[source][block, :, lanes]
        targets[target][tuple(at_ref[entry] for entry in where)] = rows


def place(at, sources, plan, shapes):
    outs = [jax.ShapeDtypeStruct(shape, BF16) for shape in shapes]
    return whole_call(functools.partial(place_kernel, plan, len(sources)), at, sources, outs)


def flip(array, axis, bit, size):
    return lax.ppermute(array, axis, [(i, i ^ bit) for i in range(size)])


def shifter(axis, size, stride):
    def shift(array, step):
        return lax.ppermute(
            array, axis, [(i, (i + step * stride) % size) for i in range(size)]
        )

    return shift


def after(array, *others):
    return lax.optimization_barrier((array, *others))[0]


def join(*values):
    flat, shape = jax.tree.flatten(values)
    return jax.tree.unflatten(shape, lax.optimization_barrier(tuple(flat)))


class Ring:
    def __init__(self, block, ring, shift, split):
        self.ring, self.shift, self.split = ring, shift, split
        self.right = self.left = block
        self.taken = 0

    def step(self, *gates):
        self.taken += 1
        right, left = after(self.right, *gates), after(self.left, *gates)
        if 2 * self.taken == self.ring:
            right, left = right[: self.split], left[self.split :]
        self.right, self.left = self.shift(right, 1), self.shift(left, -1)
        return [self.right, self.left]


def standardize(values):
    average = jnp.mean(values, axis=-1, keepdims=True)
    centred = values - average
    variance = jnp.mean(centred * centred, axis=-1, keepdims=True)
    inverse = lax.rsqrt(variance + EPSILON)
    return centred * inverse, inverse


def standardize_back(grad, hat, inverse):
    return inverse * (
        grad
        - jnp.mean(grad, axis=-1, keepdims=True)
        - hat * jnp.mean(grad * hat, axis=-1, keepdims=True)
    )


def local(
    seqs,
    batches,
    patches,
    cotangent,
    segment_ids,
    kept_mask,
    first_gain,
    qkv_weight,
    out_weight,
    second_gain,
    up_weight,
    down_weight,
):
    width = HEADS * HDIM
    tokens = patches.shape[1]
    length = tokens * seqs
    devices = seqs * batches
    groups = seqs // QUAD
    pairs = batches // 2
    splits = seqs // HEADS
    lines = qkv_weight.shape[0]
    hidden_rows = down_weight.shape[0]
    units = hidden_rows * groups * pairs
    at_seq = lax.axis_index("seq")
    at_batch = lax.axis_index("batch")
    group, at_x, at_core = at_seq // QUAD, (at_seq // 2) % 2, at_seq % 2
    pair, at_y = at_batch // 2, at_batch % 2
    quad = at_seq % QUAD
    along_groups = shifter("seq", seqs, QUAD)
    along_pairs = shifter("batch", batches, 2)
    distances = sorted(range(groups), key=lambda step: min(step, groups - step))
    hops = [(step, hop) for hop in range(pairs) for step in distances]

    def flip_x(array, *gates):
        return flip(after(array, *gates), "seq", 2, seqs)

    def flip_core(array, *gates):
        return flip(after(array, *gates), "seq", 1, seqs)

    def flip_y(array, *gates):
        return flip(after(array, *gates), "batch", 1, batches)

    def pick(array, at, axis):
        return lax.dynamic_index_in_dim(array, at, axis, keepdims=False)

    def rows(*arrays):
        return jnp.concatenate(arrays, axis=0)

    def shifted(array, step, hop):
        array = along_groups(array, step) if step else array
        return along_pairs(array, hop) if hop else array

    def fetch(block, *gates):
        block = after(block, *gates)
        return [shifted(block, step, hop) for step, hop in hops[1:]]

    def owners(hop_list=hops):
        return [((group - step) % groups, (pair - hop) % pairs) for step, hop in hop_list]

    def deliver(terms, *gates):
        return [
            shifted(after(term, *gates), step, hop) for term, (step, hop) in zip(terms[1:], hops[1:])
        ]

    def in_order(terms):
        return [
            pick(pick(terms, (group + step) % groups, 0), (pair + hop) % pairs, 0)
            for step, hop in hops
        ]

    out_full = lax.all_gather(out_weight, EVERY, axis=0, tiled=True)
    at, plan = [], []
    for index, (g, p) in enumerate(owners()):
        first = len(at)
        at += [g, p]
        for row, (y, x, c) in enumerate(
            (y, x, c) for y in range(2) for x in range(2) for c in range(2)
        ):
            plan.append((index, (y, x, c), None, 0, (first, len(at), first + 1, len(at) + 1)))
            at += [quad ^ (2 * x + c), at_y ^ y]
        plan.append((len(hops) + index, slice(None), None, 1, (first, first + 1)))
    place_numbers = jnp.stack(at).astype(jnp.int32)
    order = [(3 + 2 * index, 4 + 2 * index) for index in range(len(hops))]
    at = [at_x, at_core, at_y]
    for step, hop in hops:
        at += [(group + step) % groups, (pair + hop) % pairs]
    out_numbers = jnp.stack(at).astype(jnp.int32)
    place_at = (4 * at_x + 2 * at_core + at_y).astype(jnp.int32)[None]
    group_numbers = [(group + step) % groups for step in distances]
    group_numbers = jnp.stack([place_at[0], *group_numbers]).astype(jnp.int32)
    core = at_core.astype(jnp.int32)[None]
    sides = jnp.stack([at_x, at_core, at_y]).astype(jnp.int32)
    numbers = [place_numbers, out_numbers, place_at, group_numbers, core, sides]

    inputs = patches[0].astype(F32)
    first_hat, first_inverse = standardize(inputs)
    own = first_hat.astype(BF16)
    first_rows = first_gain.astype(F32)[:, None]
    second_rows = second_gain.astype(F32)[:, None]
    ring = Ring(own, groups, along_groups, tokens // 2)
    rounds = [[own], ring.step()]
    beside = []
    qkv_rows = after(qkv_weight, own).astype(F32) * first_rows
    qkv_rows = qkv_rows.reshape(lines, 3, HEADS, HDIM).transpose(2, 0, 1, 3)
    scales = jnp.array([SCALING, 1.0, 1.0], F32)[:, None]
    sent = jnp.broadcast_to(
        (qkv_rows * scales).astype(BF16).reshape(HEADS, 1, lines, 3 * HDIM),
        (HEADS, splits * batches, lines, 3 * HDIM),
    ).reshape(devices, lines, 3 * HDIM)
    eights = [
        [(QUAD * g + q) * batches + 2 * p + y for q in range(QUAD) for y in range(2)]
        for g in range(groups)
        for p in range(pairs)
    ]
    qkv_part = qkv_rows.astype(BF16).transpose(1, 0, 2, 3).reshape(lines, 3 * width)
    up_rows = (after(up_weight, own).astype(F32) * second_rows).astype(BF16)
    up_rows = up_rows.reshape(lines, groups, 2, 2, pairs, 2, hidden_rows)
    up_rows = up_rows.transpose(2, 3, 5, 0, 1, 4, 6).reshape(2, 2, 2, lines, units)
    up_kept = pick(up_rows, at_core, 1)
    up_core = flip_core(pick(up_rows, 1 - at_core, 1))
    rounds[1], up_core = join(rounds[1], up_core)

    while ring.taken < groups // 2:
        beside.append(flip_x(rows(*sum(rounds if len(rounds) == 2 else rounds[-1:], []))))
        rounds.append(ring.step(*rounds[-1]))
    up_rows = jnp.stack([up_kept, up_core], axis=1)
    up_kept, up_x = pick(up_rows, at_x, 0), flip_x(pick(up_rows, 1 - at_x, 0), *rounds[1])

    def by_side(row):
        row = row.reshape(2 * groups, 2, tokens)
        sides = [pick(row, side, 1) for side in (at_core, 1 - at_core)]
        return rows(*sides).reshape(length)

    ids = by_side(segment_ids[0])
    key_ids = jnp.where(by_side(kept_mask[0]) == 1, ids, -1)[None]
    head_weight = lax.all_to_all(
        after(sent, *rounds[1]), EVERY, split_axis=0, concat_axis=0, tiled=True
    )
    farthest = rounds[-1]
    rounds, beside, up_x, head_weight, ids, key_ids, numbers = join(
        rounds, beside, up_x, head_weight, ids, key_ids, numbers
    )

    place_numbers, out_numbers, place_at, group_numbers, core, sides = numbers

    beside.append(flip_x(rows(*rounds[-1])))
    head_weight = head_weight.reshape(width, 3 * HDIM).T
    near_weight = flip_core(head_weight)
    up_rows = jnp.stack([up_kept, up_x], axis=0)
    up_kept, up_y = pick(up_rows, at_y, 2), flip_y(pick(up_rows, 1 - at_y, 2))
    down_around = fetch(down_weight, *farthest)
    beside, near_weight, up_y, down_around[:-1] = join(
        beside, near_weight, up_y, down_around[:-1]
    )
    up_packed = jnp.stack([up_kept, up_y], axis=0)
    up_around = fetch(up_packed)

    pieces, layout, where = [own], [(0, 0)], [2 * group + at_x]
    flipped = [(1, 0, 2 * group + 1 - at_x)]
    for number in range(1, len(rounds)):
        steps = [number] if 2 * number == groups else [-number, number]
        spots = [2 * ((group + step) % groups) for step in steps]
        if len(steps) == 1 and len(rounds[number]) == 2:
            layout.append(((len(pieces), len(pieces) + 1), 0))
        else:
            layout += [(len(pieces) + index, 0) for index in range(len(steps))]
        where += [spot + at_x for spot in spots]
        pieces += rounds[number]
        first = tokens if number == 1 and groups > 2 else 0
        flipped += [
            (number, first + row * tokens, spot + 1 - at_x) for row, spot in enumerate(spots)
        ]
    layout += [(len(pieces) + number - 1, row) for number, row, spot in flipped]
    where += [spot for number, row, spot in flipped]
    pieces += beside
    where = jnp.stack(where).astype(jnp.int32)
    mine, theirs, first_own = project_pieces(
        where, head_weight, near_weight, pieces, layout, tokens
    )

    other = flip_core(theirs)
    upstream = cotangent[0]
    upstream_all = lax.all_gather(
        after(upstream, mine), EVERY, axis=0, axis_index_groups=eights
    )

    query_ids = ids[None]
    mixed_blocks, attended, logs = attention_forward(
        core, mine, other, key_ids, query_ids, tokens, splits
    )
    mixed_blocks = mixed_blocks.reshape(seqs, HDIM, tokens)
    if splits > 1:
        filled = (jnp.arange(seqs, dtype=jnp.int32) % 2 == at_core)[:, None, None]
        mixed_blocks = jnp.where(filled, mixed_blocks, 0)
    mixed_blocks, down_around, up_around[:-1] = join(
        mixed_blocks, down_around, up_around[:-1]
    )

    mixed = lax.all_to_all(mixed_blocks, "seq", split_axis=0, concat_axis=0, tiled=True)
    if splits > 1:
        mixed = mixed.reshape(HEADS, splits, HDIM, tokens).sum(1)
    mixed, out_full = join(mixed.reshape(width, tokens), out_full)

    middle = inputs + contract(mixed, out_full, 0, 0)
    second_hat, second_inverse = standardize(middle)
    second = second_hat.astype(BF16)
    second_x, second_y, second_core = flip_x(second), flip_y(second), flip_core(second)
    second_core, up_around, upstream_all = join(second_core, up_around, upstream_all)
    qkv_full = lax.all_gather(after(qkv_part, second_core), EVERY, axis=0, tiled=True)
    up_part, down_part = place(
        place_numbers,
        [up_packed, *up_around, down_weight, *down_around],
        plan,
        [(groups, QUAD, pairs, 2, lines, units), (groups, pairs, hidden_rows, width)],
    )
    up_part = up_part.reshape(width, units)
    down_part = down_part.reshape(units, width)

    weights = (place_at, upstream_all, up_part, down_part)
    hidden_near, pre_near, sum_near, grad_near = mlp([second, second_core], (0, 2), *weights)
    second_x, second_y, grad_near = join(second_x, second_y, grad_near)
    second_xy = flip_x(second_y)
    second_x_core, second_y_core = flip_core(second_x), flip_core(second_y)
    hidden_mid, pre_mid, sum_mid, grad_mid = mlp(
        [second_x, second_y, second_x_core, second_y_core], (4, 1, 6, 3), *weights
    )
    second_xy, grad_mid = join(second_xy, grad_mid)
    second_xy_core = flip_core(second_xy)
    hidden_far, pre_far, sum_far, grad_far = mlp([second_xy, second_xy_core], (5, 7), *weights)

    far_sum = grad_far[0] + flip_core(grad_far[1])
    far_x = flip_x(far_sum.astype(BF16))
    x_sum = grad_mid[0] + flip_core(grad_mid[2])
    y_sum = grad_mid[1] + flip_core(grad_mid[3])
    near_sum = grad_near[0] + flip_core(grad_near[1])
    mid_x = flip_x(x_sum.astype(BF16), far_x)
    mid_y = flip_y((y_sum + far_x).astype(BF16))
    sum_other = [flip_core(term, far_sum) for term in (sum_near[1], *sum_mid[2:], sum_far[1])]
    seconds = [
        second, second_core, second_x, second_y, second_x_core, second_y_core, second_xy,
        second_xy_core,
    ]
    toggles = (0, 2, 4, 1, 6, 3, 5, 7)
    hiddens = [hidden_near, hidden_mid, hidden_far]
    pres = [pre_near, pre_mid, after(pre_far, far_sum)]
    if pairs == 1:
        up_terms, down_terms = mlp_weight_terms(
            group_numbers, len(hops), seconds, toggles, pres, hiddens, upstream_all
        )
    else:
        up_terms = contract(rows(*seconds), rows(*pres), 0, 0).astype(BF16)
        up_terms = up_terms.reshape(groups, QUAD, pairs, 2, lines, units).swapaxes(1, 2)
        sorted_places = jnp.stack([place_at[0] ^ toggle for toggle in toggles])
        down_terms = jnp.take(upstream_all, sorted_places, axis=0).reshape(-1, width)
        down_terms = contract(rows(*hiddens), down_terms, 0, 0).astype(BF16)
        down_terms = down_terms.reshape(groups, pairs, hidden_rows, width)
        up_terms, down_terms = in_order(up_terms), in_order(down_terms)
    mid_x, mid_y, up_terms, down_terms, sum_other = join(
        mid_x, mid_y, up_terms, down_terms, sum_other
    )
    second_grad = near_sum + mid_x + mid_y

    middle_grad = upstream.astype(F32) + standardize_back(second_grad, second_hat, second_inverse)
    middle_low = middle_grad.astype(BF16)
    mixed_grad = contract(out_full, middle_low, 1, 1).astype(BF16)
    up_got = deliver(up_terms, second_grad)
    sent = jnp.broadcast_to(
        mixed_grad.reshape(HEADS, 1, HDIM, tokens), (HEADS, splits, HDIM, tokens)
    ).reshape(seqs, HDIM, tokens)
    grads = lax.all_to_all(sent, "seq", split_axis=0, concat_axis=0, tiled=True)
    out_kept, out_kept_x, out_sent, out_sent_x = out_weight_terms(
        out_numbers, order, after(mixed, sent), middle_low,
        (groups, 2, 2, pairs, 2, lines, width),
    )
    out_core, out_core_x = flip_core(out_sent), flip_core(out_sent_x)
    first_own = first_own.reshape(length // 2, width)
    first_other = flip_core(first_own, sent)
    grads, first_other, out_core, out_core_x, qkv_full = join(
        grads, first_other, out_core, out_core_x, qkv_full
    )

    grads = grads.reshape(groups, 2, 2, HDIM, tokens)
    out_x = flip_x(out_kept_x + out_core_x)
    project_grad, own_grad, other_grad = attention_backward(
        core, mine, other, key_ids, query_ids, attended, logs, grads, tokens, splits
    )
    project_grad, own_grad, other_grad, out_x, up_got = join(
        project_grad, own_grad, other_grad, out_x, up_got
    )

    got = lax.all_to_all(
        project_grad.reshape(seqs, 3 * HDIM, tokens), "seq", split_axis=0, concat_axis=0, tiled=True
    )
    up_sum = sum(up_got, up_terms[0]).astype(BF16).reshape(2, 2, 2, lines, units)
    up_kept, up_core = pick(up_sum, at_core, 1), flip_core(pick(up_sum, 1 - at_core, 1))
    up_rows = jnp.stack([up_kept, up_core], axis=1)
    up_kept, up_x = pick(up_rows, at_x, 0), flip_x(pick(up_rows, 1 - at_x, 0))
    up_rows = jnp.stack([up_kept, up_x], axis=0)
    up_kept, up_y = pick(up_rows, at_y, 2), flip_y(pick(up_rows, 1 - at_y, 2))
    out_sum = out_kept + out_core + out_x
    out_sum = out_sum[0] + flip_y(out_sum[1], got)
    far_x = flip_x((sum_far[0] + after(sum_other[3], project_grad)).astype(BF16))
    mid_x = flip_x((sum_mid[0] + after(sum_other[1], project_grad)).astype(BF16))
    out_got = deliver([out_sum[index] for index in range(len(hops))])
    qkv_terms = contract(first_own, own_grad, 0, 1)
    qkv_terms = qkv_terms + contract(first_other, other_grad, 0, 1)
    if splits > 1:
        got = got.reshape(HEADS, splits, 3 * HDIM, tokens).sum(1)
    qkv_terms = after(qkv_terms, got)
    got, far_x, mid_x = join(got, far_x, mid_x)
    down_got = deliver(down_terms, got)

    qkv_terms = lax.all_to_all(
        qkv_terms.astype(BF16).reshape(devices, lines, 3 * HDIM),
        EVERY, split_axis=0, concat_axis=0, tiled=True,
    )
    mid_y = flip_y((sum_mid[1] + sum_other[2] + far_x).astype(BF16))

    input_grad = finish_input(
        got.reshape(3 * width, tokens), qkv_full, first_hat, first_inverse, middle_grad
    )
    block_output = middle + (sum_near[0] + sum_other[0] + mid_x + mid_y)
    block_output = block_output.astype(BF16)
    qkv_terms, input_grad, block_output = join(qkv_terms, input_grad, block_output)
    qkv_sum, first_gain_grad = finish_qkv(first_rows, qkv_terms, qkv_weight)
    if hidden_rows % 128 == 0:
        up_sum, second_gain_grad = finish_up(
            sides, second_rows, up_kept, up_y,
            up_weight, (groups, batches),
        )
    else:
        up_sum = jnp.stack([up_kept, up_y], axis=2)
        for axis, at in ((0, at_x), (1, at_core), (2, at_y)):
            up_sum = jnp.where(at == 0, up_sum, jnp.flip(up_sum, axis))
        up_sum = up_sum.astype(F32).reshape(2, 2, 2, lines, groups, pairs, hidden_rows)
        up_sum = up_sum.transpose(3, 4, 0, 1, 5, 2, 6).reshape(lines, -1)
        second_gain_grad = jnp.sum(up_weight.astype(F32) * up_sum, axis=1)
        up_sum = up_sum * second_rows
    down_sum = sum(down_got, down_terms[0]).astype(F32).reshape(hidden_rows, width)
    out_sum = sum(out_got, out_sum[0]).astype(F32)

    return (
        block_output[None],
        input_grad[None],
        first_gain_grad.reshape(lines),
        qkv_sum,
        out_sum,
        second_gain_grad.reshape(lines),
        up_sum,
        down_sum,
    )


def solution(mesh):
    rows = P(EVERY)
    tokens = P("batch", "seq", None)
    in_specs = (
        tokens, tokens, P("batch", None), P("batch", None), rows, P(EVERY, None), P(EVERY, None),
        rows, P(EVERY, None), P(EVERY, None),
    )
    out_specs = (
        tokens, tokens, rows, P(EVERY, None), P(EVERY, None), rows, P(EVERY, None), P(EVERY, None)
    )
    body = functools.partial(local, mesh.shape["seq"], mesh.shape["batch"])
    return jax.shard_map(body, mesh=mesh, in_specs=in_specs, out_specs=out_specs, check_vma=False)
```

```python
import functools
import math

import jax
import jax.numpy as jnp
from jax import lax
from jax.experimental import pallas as pl
from jax.experimental.pallas import tpu as pltpu
from jax.sharding import PartitionSpec as P

HEADS = 16
HDIM = 64
QUAD = 4
EIGHT = 8

EPSILON = 1e-05
MASKED = -1e30
SCALING = HDIM**-0.5
BF16 = jnp.bfloat16
F32 = jnp.float32
EVERY = ("seq", "batch")
LARGE = pl.CostEstimate(flops=30_000_000_000, bytes_accessed=1, transcendentals=0)
VMEM_LIMIT = 60 << 20
SMALL = pl.CostEstimate(flops=1, bytes_accessed=1, transcendentals=0)


def contract(left, right, left_dim, right_dim):
    return lax.dot_general(
        left, right, (((left_dim,), (right_dim,)), ((), ())), preferred_element_type=F32
    )


def masked_scores(keys, queries, key_ids, query_ids, row, first):
    scores = contract(keys, queries, 0, 0)
    slots = row + lax.broadcasted_iota(jnp.int32, scores.shape, 0)
    columns = first + lax.broadcasted_iota(jnp.int32, scores.shape, 1)
    allowed = (key_ids == query_ids) | (slots == columns)
    return jnp.where(allowed, scores, MASKED)


def chunks(length, step):
    step = min(step, length)
    return [slice(row, row + step) for row in range(0, length, step)]


def load_heads(own_ref, other_ref, held, key_id_ref, key_column):
    half = own_ref.shape[1]
    held[:, :half] = own_ref[...]
    held[:, half:] = other_ref[...]
    key_column[...] = jnp.broadcast_to(key_id_ref[...], (8, 2 * half)).T[:, :1]


def forward_kernel(
    tokens, core_ref, own_ref, other_ref, key_id_ref, query_id_ref, mixed_ref, attended_ref,
    log_ref, held, key_column,
):
    step = pl.program_id(0)

    @pl.when(step == 0)
    def _():
        load_heads(own_ref, other_ref, held, key_id_ref, key_column)

    block = attended_ref.shape[1]
    first = pl.multiple_of(step * block, block)
    queries = held[:HDIM, pl.ds(first, block)]
    scores, highest = [], None
    parts = chunks(held.shape[1], 512)
    for part in parts:
        scores.append(
            masked_scores(
                held[HDIM : 2 * HDIM, part], queries, key_column[part], query_id_ref[...],
                part.start, first,
            )
        )
        top = jnp.max(scores[-1], axis=0, keepdims=True)
        highest = top if highest is None else jnp.maximum(highest, top)
    totals = attended = None
    for part, score in zip(parts, scores):
        expo = jnp.exp(score - highest)
        total = jnp.sum(expo, axis=0, keepdims=True)
        term = contract(held[2 * HDIM :, part], expo.astype(BF16), 1, 0)
        totals = total if totals is None else totals + total
        attended = term if attended is None else attended + term
    attended = attended / totals
    attended_ref[...] = attended
    log_ref[...] = highest + jnp.log(totals)
    low = attended.astype(BF16)
    for index in range(block // tokens):
        mixed_ref[index // 2, index % 2, 0] = low[:, index * tokens : (index + 1) * tokens]


def backward_kernel(
    tokens, core_ref, own_ref, other_ref, key_id_ref, query_id_ref, attended_ref, log_ref, grad_ref,
    out_ref, own_grad_ref, other_grad_ref, held, key_column, dk_sum, dv_sum,
):
    step = pl.program_id(0)
    steps = pl.num_programs(0)
    groups = out_ref.shape[0]
    half = own_ref.shape[1]

    @pl.when(step == 0)
    def _():
        load_heads(own_ref, other_ref, held, key_id_ref, key_column)
        dk_sum[...] = jnp.zeros_like(dk_sum)
        dv_sum[...] = jnp.zeros_like(dv_sum)

    block = attended_ref.shape[1]
    first = pl.multiple_of(step * block, block)
    queries = held[:HDIM, pl.ds(first, block)]
    count = block // tokens
    grads = jnp.concatenate(
        [grad_ref[index // 2, index % 2, 0] for index in range(count)], axis=1
    )
    logs = log_ref[...]
    delta = jnp.sum(grads.astype(F32) * attended_ref[...], axis=0, keepdims=True)
    dq = None
    for part in chunks(held.shape[1], 1024):
        keys = held[HDIM : 2 * HDIM, part]
        scores = masked_scores(
            keys, queries, key_column[part], query_id_ref[...], part.start, first
        )
        probs = jnp.exp(scores - logs)
        dprob = contract(held[2 * HDIM :, part], grads, 0, 0)
        dscore = (probs * (dprob - delta)).astype(BF16)
        term = contract(keys, dscore, 1, 0)
        dq = term if dq is None else dq + term
        dk_sum[:, part] += contract(queries, dscore, 1, 1)
        dv_sum[:, part] += contract(grads, probs.astype(BF16), 1, 1)
    dq = (dq * SCALING).astype(BF16)
    per_side = half // block
    side = step // per_side
    core = jnp.where(side == 0, core_ref[0], 1 - core_ref[0])
    for index in range(count):
        group = step % per_side * (count // 2) + index // 2
        out_ref[group, index % 2, core, :HDIM, :] = dq[:, index * tokens : (index + 1) * tokens]
    inside = pl.multiple_of((step % per_side) * block, block)

    @pl.when(side == 0)
    def _():
        own_grad_ref[:HDIM, pl.ds(inside, block)] = dq

    @pl.when(side == 1)
    def _():
        other_grad_ref[:HDIM, pl.ds(inside, block)] = dq

    @pl.when(step == steps - 1)
    def _():
        for first_row, total in ((HDIM, dk_sum), (2 * HDIM, dv_sum)):
            rows = pl.ds(first_row, HDIM)
            low = total[...].astype(BF16)
            own_grad_ref[rows, :] = low[:, :half]
            other_grad_ref[rows, :] = low[:, half:]
            for side_at in range(2):
                to_core = core_ref[0] if side_at == 0 else 1 - core_ref[0]
                for group in range(groups):
                    for x in range(2):
                        at = side_at * half + (2 * group + x) * tokens
                        out_ref[group, x, to_core, rows, :] = low[:, at : at + tokens]
        if steps < 2 * (half // block):
            other_grad_ref[:HDIM, :] = jnp.zeros((HDIM, half), BF16)
            for group in range(groups):
                for x in range(2):
                    out_ref[group, x, 1 - core_ref[0], :HDIM, :] = jnp.zeros((HDIM, tokens), BF16)


def side_core(step, per_side, core):
    return jnp.where(step < per_side, core, 1 - core)


def attention_specs(length, block, tokens, groups):
    half = length // 2
    whole = pl.BlockSpec((3 * HDIM, half), lambda i, core: (0, 0))
    part = pl.BlockSpec((HDIM, block), lambda i, core: (0, i))
    row = pl.BlockSpec((1, block), lambda i, core: (0, i))
    column = pl.BlockSpec((1, length), lambda i, core: (0, 0))
    per_side = half // block
    tile = pl.BlockSpec(
        (groups // per_side, 2, 1, HDIM, tokens),
        lambda i, core: (i % per_side, 0, side_core(i, per_side, core[0]), 0, 0),
    )
    return whole, part, row, column, tile


def attention_forward(core, own, other, key_ids, query_ids, tokens, splits):
    length = 2 * own.shape[1]
    groups = length // (4 * tokens)
    block = 4 * tokens if groups % 2 == 0 else 2 * tokens
    count = length // splits
    whole, part, row, column, tile = attention_specs(length, block, tokens, groups)
    return pl.pallas_call(
        functools.partial(forward_kernel, tokens),
        grid_spec=pltpu.PrefetchScalarGridSpec(
            num_scalar_prefetch=1,
            grid=(count // block,),
            in_specs=[whole, whole, column, row],
            out_specs=[tile, part, row],
            scratch_shapes=[
                pltpu.VMEM((3 * HDIM, length), BF16), pltpu.VMEM((length, 1), jnp.int32)
            ],
        ),
        out_shape=[
            jax.ShapeDtypeStruct((groups, 2, 2, HDIM, tokens), BF16),
            jax.ShapeDtypeStruct((HDIM, count), F32),
            jax.ShapeDtypeStruct((1, count), F32),
        ],
        compiler_params=pltpu.CompilerParams(vmem_limit_bytes=VMEM_LIMIT),
        cost_estimate=SMALL,
    )(core, own, other, key_ids, query_ids)


def attention_backward(core, own, other, key_ids, query_ids, attended, logs, grads, tokens, splits):
    length = 2 * own.shape[1]
    half = length // 2
    groups = length // (4 * tokens)
    block = 4 * tokens if groups % 2 == 0 else 2 * tokens
    count = length // splits
    whole, part, row, column, tile = attention_specs(length, block, tokens, groups)
    return pl.pallas_call(
        functools.partial(backward_kernel, tokens),
        grid_spec=pltpu.PrefetchScalarGridSpec(
            num_scalar_prefetch=1,
            grid=(count // block,),
            in_specs=[whole, whole, column, row, part, row, tile],
            out_specs=[
                pl.BlockSpec(
                    (groups, 2, 2, 3 * HDIM, tokens), lambda i, core: (0, 0, 0, 0, 0)
                ),
                whole,
                whole,
            ],
            scratch_shapes=[
                pltpu.VMEM((3 * HDIM, length), BF16),
                pltpu.VMEM((length, 1), jnp.int32),
                pltpu.VMEM((HDIM, length), F32),
                pltpu.VMEM((HDIM, length), F32),
            ],
        ),
        out_shape=[
            jax.ShapeDtypeStruct((groups, 2, 2, 3 * HDIM, tokens), BF16),
            jax.ShapeDtypeStruct((3 * HDIM, half), BF16),
            jax.ShapeDtypeStruct((3 * HDIM, half), BF16),
        ],
        compiler_params=pltpu.CompilerParams(vmem_limit_bytes=VMEM_LIMIT),
        cost_estimate=LARGE,
    )(core, own, other, key_ids, query_ids, attended, logs, grads)


def standard_kernel(patches_ref, out_ref):
    out_ref[...] = standardize(patches_ref[...].astype(F32))[0].astype(BF16)


def standard_patches(patches):
    return pl.pallas_call(
        standard_kernel,
        grid=(1,),
        in_specs=[whole(patches)],
        out_specs=whole(patches),
        out_shape=jax.ShapeDtypeStruct(patches.shape, BF16),
        cost_estimate=SMALL,
    )(patches)


def project_kernel(layout, tokens, where_ref, mine_w_ref, theirs_w_ref, *refs):
    pieces, (mine_ref, theirs_ref, all_ref) = refs[:-3], refs[-3:]
    for index, (source, row) in enumerate(layout):
        if isinstance(source, tuple):
            hat = jnp.concatenate([pieces[member][...] for member in source], axis=0)
        else:
            hat = pieces[source][row : row + tokens]
        at = where_ref[index]
        columns = pl.ds(pl.multiple_of(at * tokens, tokens), tokens)
        mine_ref[:, columns] = contract(mine_w_ref[...], hat, 1, 1).astype(BF16)
        theirs_ref[:, columns] = contract(theirs_w_ref[...], hat, 1, 1).astype(BF16)
        all_ref[at] = hat


def project_pieces(where, mine_w, theirs_w, pieces, layout, tokens):
    blocks = len(layout)
    width = mine_w.shape[1]
    columns = mine_w.shape[0]
    return whole_call(
        functools.partial(project_kernel, layout, tokens),
        where,
        [mine_w, theirs_w, *pieces],
        [
            jax.ShapeDtypeStruct((columns, blocks * tokens), BF16),
            jax.ShapeDtypeStruct((columns, blocks * tokens), BF16),
            jax.ShapeDtypeStruct((blocks, tokens, width), BF16),
        ],
    )


def whole(array):
    rank = len(array.shape)
    return pl.BlockSpec(array.shape, lambda *step: (0,) * rank)


def whole_call(kernel, scalars, arrays, outs, scratch=(), cost=SMALL):
    return pl.pallas_call(
        kernel,
        grid=(1,),
        in_specs=[pl.BlockSpec(memory_space=pltpu.SMEM)] + [whole(array) for array in arrays],
        out_specs=[whole(out) for out in outs],
        out_shape=outs,
        scratch_shapes=list(scratch),
        compiler_params=pltpu.CompilerParams(vmem_limit_bytes=VMEM_LIMIT),
        cost_estimate=cost,
    )(scalars, *arrays)


def together(refs):
    values = [ref[...] for ref in refs]
    return values[0] if len(values) == 1 else jnp.concatenate(values, axis=0)


def mlp_kernel(count, toggles, place_ref, *refs):
    pieces, refs = refs[:count], refs[count:]
    all_ref, up_ref, down_ref, hidden_ref, pre_grad_ref = refs[:5]
    hat = together(pieces)
    upstream = jnp.concatenate([all_ref[place_ref[0] ^ toggle] for toggle in toggles], axis=0)
    units = up_ref.shape[1]
    block = min(256, units)
    grad = out = None
    for first in range(0, units, block):
        chunk = slice(first, first + block)
        up, down = up_ref[:, chunk], down_ref[chunk, :]
        pre = contract(hat, up, 1, 0)
        cdf = 0.5 * (1.0 + lax.erf(pre * (0.5**0.5)))
        slope = cdf + pre * jnp.exp(-0.5 * pre * pre) * ((2.0 * math.pi) ** -0.5)
        hidden = (pre * cdf).astype(BF16)
        pre_grad = (contract(upstream, down, 1, 1) * slope).astype(BF16)
        hidden_ref[:, chunk] = hidden
        pre_grad_ref[:, chunk] = pre_grad
        grad_term = contract(pre_grad, up, 1, 1)
        out_term = contract(hidden, down, 1, 0)
        grad = grad_term if grad is None else grad + grad_term
        out = out_term if out is None else out + out_term
    for total, kept_refs in ((out, refs[5 : 5 + count]), (grad, refs[5 + count :])):
        first = 0
        for ref in kept_refs:
            ref[...] = total[first : first + ref.shape[0]].astype(ref.dtype)
            first += ref.shape[0]


def mlp(hats, toggles, place, upstream_all, up, down):
    count = len(hats)
    rows = sum(hat.shape[0] for hat in hats)
    width, units = up.shape
    sums = [
        jax.ShapeDtypeStruct(hat.shape, F32 if 2 * index < count else BF16)
        for index, hat in enumerate(hats)
    ]
    outs = whole_call(
        functools.partial(mlp_kernel, count, toggles),
        place,
        [*hats, upstream_all, up, down],
        [
            jax.ShapeDtypeStruct((rows, units), BF16),
            jax.ShapeDtypeStruct((rows, units), BF16),
            *sums,
            *sums,
        ],
    )
    return outs[0], outs[1], list(outs[2 : 2 + count]), list(outs[2 + count :])


def mlp_weight_kernel(counts, sizes, toggles, at_ref, *refs):
    halves, batches, lines, hidden_rows = sizes
    hats, pres, hiddens = (
        refs[: counts[0]], refs[counts[0] : sum(counts[:2])], refs[sum(counts[:2]) : sum(counts)]
    )
    refs = refs[sum(counts) :]
    all_ref, out_refs, (up_held, down_held) = refs[0], refs[1:-2], refs[-2:]
    upstream = jnp.concatenate([all_ref[at_ref[0] ^ toggle] for toggle in toggles], axis=0)
    up = contract(together(hats), together(pres), 0, 0).astype(BF16)
    up_held[...] = up.reshape(up_held.shape)
    down = contract(together(hiddens), upstream, 0, 0).astype(BF16)
    down_held[...] = down.reshape(down_held.shape)
    units = up_held.shape[-1]
    for hop, out_ref in enumerate(out_refs):
        b = at_ref[1 + halves + hop]
        for step in range(halves):
            g = at_ref[1 + step]
            for quad in range(QUAD):
                for z in range(2):
                    first = (2 * quad + z) * lines
                    out_ref[step, first : first + lines] = up_held[g, z, quad, b]
            for part in range(2):
                first = EIGHT * lines + part * hidden_rows
                columns = slice(part * units, (part + 1) * units)
                out_ref[step, first : first + hidden_rows] = down_held[g, b, :, columns]


def mlp_weight_terms(numbers, sizes, hats, toggles, pres, hiddens, upstream_all):
    halves, batches, lines, hidden_rows = sizes
    width, units = hats[0].shape[1], pres[0].shape[1]
    counts = (len(hats), len(pres), len(hiddens))
    out = jax.ShapeDtypeStruct((halves, EIGHT * lines + 2 * hidden_rows, units), BF16)
    outs = whole_call(
        functools.partial(mlp_weight_kernel, counts, sizes, toggles),
        numbers,
        [*hats, *pres, *hiddens, upstream_all],
        [out] * batches,
        [
            pltpu.VMEM((halves, 2, QUAD, batches, lines, units), BF16),
            pltpu.VMEM((halves, batches, hidden_rows, width), BF16),
        ],
        LARGE,
    )
    return list(outs)


def two_sums_kernel(count, *refs):
    for index in range(count):
        total = refs[index][...] + refs[count + index][...].astype(F32)
        refs[2 * count + index][...] = total.astype(BF16)


def two_sums(left, right, gate):
    arrays = [*left, after(right[0], gate), *right[1:]]
    outs = [jax.ShapeDtypeStruct(term.shape, BF16) for term in left]
    return pl.pallas_call(
        functools.partial(two_sums_kernel, len(left)),
        grid=(1,),
        in_specs=[whole(array) for array in arrays],
        out_specs=[whole(out) for out in outs],
        out_shape=outs,
        compiler_params=pltpu.CompilerParams(vmem_limit_bytes=VMEM_LIMIT),
        cost_estimate=LARGE,
    )(*arrays)


def out_weight_kernel(order, at_ref, mixed_ref, grad_ref, *refs):
    out_refs, held = refs[:-1], refs[-1]
    terms = contract(mixed_ref[...], grad_ref[...], 1, 0).astype(BF16)
    held[...] = terms.reshape(held.shape)
    for index, ref in enumerate(out_refs):
        toggle_core, toggle_x = index // 2, index % 2
        for y in range(2):
            for block, (g, p) in enumerate(order):
                ref[y, block] = held[
                    at_ref[g], at_ref[0] ^ toggle_x, at_ref[1] ^ toggle_core, at_ref[p],
                    at_ref[2] ^ y,
                ]


def out_weight_terms(at, order, mixed, grad, shape):
    lines, width = shape[-2:]
    return whole_call(
        functools.partial(out_weight_kernel, order),
        at,
        [mixed, grad],
        [jax.ShapeDtypeStruct((2, len(order), lines, width), BF16)] * 4,
        [pltpu.VMEM(shape, BF16)],
    )


def finish_input_kernel(got_ref, weight_ref, patches_ref, middle_ref, out_ref, total):
    step = pl.program_id(0)
    term = contract(weight_ref[...], got_ref[...], 1, 0)

    @pl.when(step == 0)
    def _():
        total[...] = term

    @pl.when(step > 0)
    def _():
        total[...] += term

    @pl.when(step == pl.num_programs(0) - 1)
    def _():
        hat, inverse = standardize(patches_ref[...].astype(F32))
        grad = standardize_back(total[...].T, hat, inverse)
        out_ref[...] = (middle_ref[...] + grad).astype(BF16)


def finish_input(got, weight, patches, middle_grad):
    columns, tokens = got.shape
    width = weight.shape[0]
    block = columns // 4
    rows = [patches, middle_grad]
    return pl.pallas_call(
        finish_input_kernel,
        grid=(4,),
        in_specs=[
            pl.BlockSpec((block, tokens), lambda i: (i, 0)),
            pl.BlockSpec((width, block), lambda i: (0, i)),
            *[whole(array) for array in rows],
        ],
        out_specs=pl.BlockSpec((tokens, width), lambda i: (0, 0)),
        out_shape=jax.ShapeDtypeStruct((tokens, width), BF16),
        scratch_shapes=[pltpu.VMEM((width, tokens), F32)],
        compiler_params=pltpu.CompilerParams(vmem_limit_bytes=VMEM_LIMIT),
        cost_estimate=LARGE,
    )(got, weight, *rows)


def finish_qkv_kernel(gain_ref, terms_ref, weight_ref, out_ref, gain_grad_ref):
    copies = terms_ref.shape[0] // HEADS
    gains = gain_ref[...]
    total = None
    for head in range(HEADS):
        term = terms_ref[head * copies].astype(F32)
        for copy in range(1, copies):
            term += terms_ref[head * copies + copy].astype(F32)
        for kind in range(3):
            first = (kind * HEADS + head) * HDIM
            columns = slice(first, first + HDIM)
            part = term[:, kind * HDIM : (kind + 1) * HDIM]
            out_ref[:, columns] = part * gains[:, :HDIM]
            part = part * weight_ref[:, columns].astype(F32)
            total = part if total is None else total + part
    gain_grad_ref[...] = jnp.sum(total.T, axis=0, keepdims=True)


def finish_qkv(gains, terms, weight):
    lines, columns = weight.shape
    outs = [
        jax.ShapeDtypeStruct((lines, columns), F32), jax.ShapeDtypeStruct((1, lines), F32)
    ]
    arrays = [gains, terms, weight]
    return pl.pallas_call(
        finish_qkv_kernel,
        grid=(1,),
        in_specs=[whole(array) for array in arrays],
        out_specs=[whole(out) for out in outs],
        out_shape=outs,
        compiler_params=pltpu.CompilerParams(vmem_limit_bytes=VMEM_LIMIT),
        cost_estimate=SMALL,
    )(*arrays)


def finish_up_kernel(sizes, at_ref, gain_ref, near_ref, far_ref, weight_ref, out_ref, gain_grad_ref):
    halves, batches = sizes
    chunk = near_ref.shape[-1] // (halves * batches)
    gains = gain_ref[...]
    total = None
    for z, ref in enumerate((near_ref, far_ref)):
        for x in range(2):
            for core in range(2):
                quad = 2 * (at_ref[0] ^ x) + (at_ref[1] ^ core)
                term = ref[x, core].astype(F32)
                for index in range(halves * batches):
                    group = 2 * (index // batches) + (at_ref[2] ^ z)
                    block = (QUAD * group + quad) * batches + index % batches
                    columns = pl.ds(pl.multiple_of(block * chunk, chunk), chunk)
                    part = term[:, index * chunk : (index + 1) * chunk]
                    out_ref[:, columns] = part * gains
                    part = part * weight_ref[:, columns].astype(F32)
                    total = part if total is None else total + part
    gain_grad_ref[...] = jnp.sum(total.T, axis=0, keepdims=True)


def finish_up(at, gains, near, far, weight, sizes):
    lines, columns = weight.shape
    return whole_call(
        functools.partial(finish_up_kernel, sizes),
        at,
        [gains, near, far, weight],
        [jax.ShapeDtypeStruct((lines, columns), F32), jax.ShapeDtypeStruct((1, lines), F32)],
    )


def place_kernel(plan, count, at_ref, *refs):
    sources, targets = refs[:count], refs[count:]
    for source, block, lanes, target, where in plan:
        rows = sources[source][block] if lanes is None else sources[source][block, :, lanes]
        targets[target][tuple(at_ref[entry] for entry in where)] = rows


def place(at, sources, plan, shapes):
    outs = [jax.ShapeDtypeStruct(shape, BF16) for shape in shapes]
    return whole_call(functools.partial(place_kernel, plan, len(sources)), at, sources, outs)


def flip(array, axis, bit, size):
    return lax.ppermute(array, axis, [(i, i ^ bit) for i in range(size)])


def shifter(axis, size, stride):
    def shift(array, step):
        return lax.ppermute(
            array, axis, [(i, (i + step * stride) % size) for i in range(size)]
        )

    return shift


def after(array, *others):
    return lax.optimization_barrier((array, *others))[0]


def join(*values):
    flat, shape = jax.tree.flatten(values)
    return jax.tree.unflatten(shape, lax.optimization_barrier(tuple(flat)))


class Ring:
    def __init__(self, block, ring, shift, split):
        self.ring, self.shift, self.split = ring, shift, split
        self.right = self.left = block
        self.taken = 0

    def step(self, *gates):
        self.taken += 1
        right, left = after(self.right, *gates), after(self.left, *gates)
        if 2 * self.taken == self.ring:
            right, left = right[: self.split], left[self.split :]
        self.right, self.left = self.shift(right, 1), self.shift(left, -1)
        return [self.right, self.left]


class Reduce:
    def __init__(self, block_at, ring, shift):
        self.block_at, self.ring, self.shift = block_at, ring, shift
        self.distance = ring // 2
        self.got = self.half = None
        if ring == 1:
            self.sum = block_at(0)

    def step(self, *gates):
        distance, shift, block_at = self.distance, self.shift, self.block_at
        if distance == 0:
            return []
        self.distance -= 1
        if self.ring == 2:
            self.got = [shift(after(block_at(1).astype(BF16), *gates), 1)]
        elif self.got is None and self.ring % 2 == 0:
            far = block_at(distance).astype(BF16)
            self.half = far.shape[0] // 2
            self.got = [
                shift(after(far[: self.half], *gates), 1),
                shift(after(far[self.half :], *gates), -1),
            ]
        else:
            terms = [block_at(distance), block_at(-distance)]
            if self.half is not None:
                at = self.half
                terms = [
                    jnp.concatenate([terms[0][:at] + self.got[0], terms[0][at:]]),
                    jnp.concatenate([terms[1][:at], terms[1][at:] + self.got[1]]),
                ]
                self.half = None
            elif self.got is not None:
                terms = [term + got for term, got in zip(terms, self.got)]
            self.got = [
                shift(after(term.astype(BF16), *gates), way)
                for term, way in zip(terms, (1, -1))
            ]
        if self.distance == 0:
            self.sum = block_at(0)
            for got in self.got:
                self.sum = self.sum + got
        return self.got

    def finish(self, *gates):
        new = []
        while self.distance > 0:
            new = self.step(*gates)
        return new


def standardize(values):
    average = jnp.mean(values, axis=-1, keepdims=True)
    centred = values - average
    variance = jnp.mean(centred * centred, axis=-1, keepdims=True)
    inverse = lax.rsqrt(variance + EPSILON)
    return centred * inverse, inverse


def standardize_back(grad, hat, inverse):
    return inverse * (
        grad
        - jnp.mean(grad, axis=-1, keepdims=True)
        - hat * jnp.mean(grad * hat, axis=-1, keepdims=True)
    )


def local(
    seqs,
    batches,
    patches,
    cotangent,
    segment_ids,
    kept_mask,
    first_gain,
    qkv_weight,
    out_weight,
    second_gain,
    up_weight,
    down_weight,
):
    width = HEADS * HDIM
    tokens = patches.shape[1]
    length = tokens * seqs
    devices = seqs * batches
    groups = seqs // QUAD
    pairs = batches // 2
    splits = seqs // HEADS
    lines = qkv_weight.shape[0]
    hidden_rows = down_weight.shape[0]
    halves = groups // 2
    units = hidden_rows * halves * batches
    at_seq = lax.axis_index("seq")
    at_batch = lax.axis_index("batch")
    group, at_x, at_core = at_seq // QUAD, (at_seq // 2) % 2, at_seq % 2
    pair, at_y = at_batch // 2, at_batch % 2
    half_group, at_z = group // 2, group % 2
    quad = at_seq % QUAD
    along_groups = shifter("seq", seqs, QUAD)
    along_pairs = shifter("batch", batches, 2)
    along_halves = shifter("seq", seqs, 2 * QUAD)
    along_batch = shifter("batch", batches, 1)
    distances = sorted(range(groups), key=lambda step: min(step, groups - step))
    hops = [(step, hop) for hop in range(pairs) for step in distances]

    def flip_x(array, *gates):
        return flip(after(array, *gates), "seq", 2, seqs)

    def flip_core(array, *gates):
        return flip(after(array, *gates), "seq", 1, seqs)

    def flip_z(array, *gates):
        return flip(after(array, *gates), "seq", QUAD, seqs)

    def flip_y(array, *gates):
        return flip(after(array, *gates), "batch", 1, batches)

    def pick(array, at, axis):
        return lax.dynamic_index_in_dim(array, at, axis, keepdims=False)

    def rows(*arrays):
        return jnp.concatenate(arrays, axis=0)

    def shifted(array, step, hop):
        array = along_groups(array, step) if step else array
        return along_pairs(array, hop) if hop else array

    def from_halves(block, *gates):
        block = after(block, *gates)
        return [along_halves(block, step) for step in range(1, halves)]

    def from_batch(block, *gates):
        block = after(block, *gates)
        return [along_batch(block, hop) for hop in range(1, batches)]

    def deliver(terms, *gates):
        return [
            shifted(after(term, *gates), step, hop) for term, (step, hop) in zip(terms[1:], hops[1:])
        ]

    out_full = lax.all_gather(out_weight, EVERY, axis=0, tiled=True)
    at, plan = [], []
    for step in range(halves):
        for hop in range(batches):
            index = step * batches + hop
            first = len(at)
            at += [(half_group - step) % halves, (at_batch - hop) % batches]
            for block in range(EIGHT):
                z, x, c = block // 4, block // 2 % 2, block % 2
                where = (first, len(at), len(at) + 1, first + 1)
                plan.append((index, (z, x, c), None, 0, where))
                at += [at_z ^ z, quad ^ (2 * x + c)]
            plan.append((halves * batches + index, slice(None), None, 1, (first, first + 1)))
    place_numbers = jnp.stack(at).astype(jnp.int32)
    order = [(3 + 2 * index, 4 + 2 * index) for index in range(len(hops))]
    at = [at_x, at_core, at_y]
    for step, hop in hops:
        at += [(group + step) % groups, (pair + hop) % pairs]
    out_numbers = jnp.stack(at).astype(jnp.int32)
    place_at = (4 * at_z + 2 * at_x + at_core).astype(jnp.int32)[None]
    group_numbers = [(half_group + step) % halves for step in range(halves)]
    group_numbers += [(at_batch + hop) % batches for hop in range(batches)]
    group_numbers = jnp.stack([place_at[0], *group_numbers]).astype(jnp.int32)
    core = at_core.astype(jnp.int32)[None]
    sides = jnp.stack([at_x, at_core, at_z]).astype(jnp.int32)
    numbers = [place_numbers, out_numbers, place_at, group_numbers, core, sides]

    inputs = patches[0].astype(F32)
    own = standard_patches(patches[0])
    first_rows = first_gain.astype(F32)[:, None]
    second_rows = second_gain.astype(F32)[:, None]
    wide_gains = [
        jnp.broadcast_to(gains, (lines, 128)) for gains in (first_rows, second_rows)
    ]
    ring = Ring(own, groups, along_groups, tokens // 2)
    rounds = [[own], ring.step()]
    beside = [flip_x(own)]
    qkv_rows = after(qkv_weight, own).astype(F32) * first_rows
    qkv_rows = qkv_rows.reshape(lines, 3, HEADS, HDIM).transpose(2, 0, 1, 3)
    scales = jnp.array([SCALING, 1.0, 1.0], F32)[:, None]
    sent = jnp.broadcast_to(
        (qkv_rows * scales).astype(BF16).reshape(HEADS, 1, lines, 3 * HDIM),
        (HEADS, splits * batches, lines, 3 * HDIM),
    ).reshape(devices, lines, 3 * HDIM)
    eights = [
        [((2 * g + z) * QUAD + q) * batches + b for z in range(2) for q in range(QUAD)]
        for g in range(halves)
        for b in range(batches)
    ]
    qkv_part = qkv_rows.astype(BF16).transpose(1, 0, 2, 3).reshape(lines, 3 * width)
    up_rows = (after(up_weight, own).astype(F32) * second_rows).astype(BF16)
    up_rows = up_rows.reshape(lines, halves, 2, 2, 2, batches, hidden_rows)
    up_rows = up_rows.transpose(3, 4, 2, 0, 1, 5, 6).reshape(2, 2, 2, lines, units)
    up_kept = pick(up_rows, at_core, 1)
    up_core = flip_core(pick(up_rows, 1 - at_core, 1))
    head_weight = lax.all_to_all(sent, EVERY, split_axis=0, concat_axis=0, tiled=True)
    rounds[1], beside, up_core = join(rounds[1], beside, up_core)

    while ring.taken < groups // 2:
        beside.append(flip_x(rows(*rounds[-1])))
        rounds.append(ring.step(*rounds[-1]))
    up_rows = jnp.stack([up_kept, up_core], axis=1)
    up_kept, up_x = pick(up_rows, at_x, 0), flip_x(pick(up_rows, 1 - at_x, 0), *rounds[1])

    def by_side(row):
        row = row.reshape(2 * groups, 2, tokens)
        sides = [pick(row, side, 1) for side in (at_core, 1 - at_core)]
        return rows(*sides).reshape(length)

    ids = by_side(segment_ids[0])
    key_ids = jnp.where(by_side(kept_mask[0]) == 1, ids, -1)[None]
    farthest = rounds[-1]
    down_rows = [[down_weight, *from_batch(down_weight, *rounds[1])]]
    rounds, beside, up_x, head_weight, ids, key_ids, numbers, down_rows = join(
        rounds, beside, up_x, head_weight, ids, key_ids, numbers, down_rows
    )

    place_numbers, out_numbers, place_at, group_numbers, core, sides = numbers

    beside.append(flip_x(rows(*rounds[-1])))
    head_weight = head_weight.reshape(width, 3 * HDIM).T
    near_weight = flip_core(head_weight)
    up_rows = jnp.stack([up_kept, up_x], axis=0)
    up_kept, up_z = pick(up_rows, at_z, 2), flip_z(pick(up_rows, 1 - at_z, 2))
    down_far = from_halves(down_weight, *farthest)
    beside, near_weight, up_z = join(beside, near_weight, up_z)
    up_packed = jnp.stack([up_kept, up_z], axis=0)
    up_far = from_halves(up_packed)
    up_rows = [[up_packed, *from_batch(up_packed)]]

    pieces, layout, where = [own], [(0, 0)], [2 * group + at_x]
    flipped = [(0, 0, 2 * group + 1 - at_x)]
    for number in range(1, len(rounds)):
        steps = [number] if 2 * number == groups else [-number, number]
        spots = [2 * ((group + step) % groups) for step in steps]
        if len(steps) == 1 and len(rounds[number]) == 2:
            layout.append(((len(pieces), len(pieces) + 1), 0))
        else:
            layout += [(len(pieces) + index, 0) for index in range(len(steps))]
        where += [spot + at_x for spot in spots]
        pieces += rounds[number]
        flipped += [(number, row * tokens, spot + 1 - at_x) for row, spot in enumerate(spots)]
    layout += [(len(pieces) + number, row) for number, row, spot in flipped]
    where += [spot for number, row, spot in flipped]
    pieces += beside
    where = jnp.stack(where).astype(jnp.int32)
    mine, theirs, first_own = project_pieces(
        where, head_weight, near_weight, pieces, layout, tokens
    )

    other = flip_core(theirs)
    first_own = first_own.reshape(length // 2, width)
    first_other = flip_core(first_own)
    upstream = cotangent[0]
    upstream_all = lax.all_gather(
        after(upstream, mine), EVERY, axis=0, axis_index_groups=eights
    )

    query_ids = ids[None]
    mixed_blocks, attended, logs = attention_forward(
        core, mine, other, key_ids, query_ids, tokens, splits
    )
    mixed_blocks = mixed_blocks.reshape(seqs, HDIM, tokens)
    if splits > 1:
        filled = (jnp.arange(seqs, dtype=jnp.int32) % 2 == at_core)[:, None, None]
        mixed_blocks = jnp.where(filled, mixed_blocks, 0)
    mixed_blocks, down_rows, up_rows, down_far, first_other = join(
        mixed_blocks, down_rows, up_rows, down_far, first_other
    )
    down_rows += [[block, *from_batch(block)] for block in down_far]

    mixed = lax.all_to_all(mixed_blocks, "seq", split_axis=0, concat_axis=0, tiled=True)
    if splits > 1:
        mixed = mixed.reshape(HEADS, splits, HDIM, tokens).sum(1)
    mixed, out_full, up_far, wide_gains = join(
        mixed.reshape(width, tokens), out_full, up_far, wide_gains
    )
    up_rows += [[block, *from_batch(block)] for block in up_far]

    qkv_full = lax.all_gather(after(qkv_part, mixed_blocks), EVERY, axis=0, tiled=True)

    middle = inputs + contract(mixed, out_full, 0, 0)
    second_hat, second_inverse = standardize(middle)
    second = second_hat.astype(BF16)
    second_x, second_z, second_core = flip_x(second), flip_z(second), flip_core(second)
    second_x, second_z, second_core, up_rows, down_rows, upstream_all = join(
        second_x, second_z, second_core, up_rows, down_rows, upstream_all
    )
    second_xz = flip_x(second_z)
    second_x_core, second_z_core = flip_core(second_x), flip_core(second_z)
    up_part, down_part = place(
        place_numbers,
        sum(up_rows + down_rows, []),
        plan,
        [(halves, 2, QUAD, batches, lines, units), (halves, batches, hidden_rows, width)],
    )
    up_part = up_part.reshape(width, units)
    down_part = down_part.reshape(units, width)

    weights = (place_at, upstream_all, up_part, down_part)
    hidden_near, pre_near, sum_near, grad_near = mlp([second, second_core], (0, 1), *weights)
    second_x_core, second_z_core, grad_near = join(second_x_core, second_z_core, grad_near)
    hidden_mid, pre_mid, sum_mid, grad_mid = mlp(
        [second_x, second_z, second_x_core, second_z_core], (2, 4, 3, 5), *weights
    )
    second_xz, grad_mid = join(second_xz, grad_mid)
    second_xz_core = flip_core(second_xz)
    hidden_far, pre_far, sum_far, grad_far = mlp([second_xz, second_xz_core], (6, 7), *weights)

    far_sum = grad_far[0] + flip_core(grad_far[1])
    far_x = flip_x(far_sum.astype(BF16))
    x_sum = grad_mid[0] + flip_core(grad_mid[2])
    z_sum = grad_mid[1] + flip_core(grad_mid[3])
    near_sum = grad_near[0] + flip_core(grad_near[1])
    seconds = [
        second, second_core, second_x, second_z, second_x_core, second_z_core, second_xz,
        second_xz_core,
    ]
    toggles = (0, 1, 2, 4, 3, 5, 6, 7)
    hiddens = [hidden_near, hidden_mid, hidden_far]
    pres = [pre_near, pre_mid, after(pre_far, far_sum)]
    if lines % 16 == 0 and hidden_rows % 16 == 0:
        mlp_terms = mlp_weight_terms(
            group_numbers, (halves, batches, lines, hidden_rows), seconds, toggles, pres, hiddens,
            upstream_all,
        )
    else:
        up_terms = contract(rows(*seconds), rows(*pres), 0, 0).astype(BF16)
        up_terms = up_terms.reshape(halves, 2, QUAD, batches, lines, units)
        up_terms = up_terms.transpose(3, 0, 2, 1, 4, 5).reshape(batches, halves, -1, units)
        sorted_places = jnp.stack([place_at[0] ^ toggle for toggle in toggles])
        down_terms = jnp.take(upstream_all, sorted_places, axis=0).reshape(-1, width)
        down_terms = contract(rows(*hiddens), down_terms, 0, 0).astype(BF16)
        down_terms = down_terms.reshape(halves, batches, hidden_rows, 2, units)
        down_terms = down_terms.transpose(1, 0, 3, 2, 4).reshape(batches, halves, -1, units)
        mlp_terms = jnp.roll(
            jnp.concatenate([up_terms, down_terms], axis=2), (-at_batch, -half_group), (0, 1)
        )
        mlp_terms = [mlp_terms[hop] for hop in range(batches)]
    sum_other = [flip_core(term, far_sum) for term in (sum_near[1], *sum_mid[2:])]
    sum_other.append(flip_core(sum_far[1], mlp_terms[0]))
    far_x, sum_other[3] = join(far_x, sum_other[3])
    mid_x = flip_x(x_sum.astype(BF16), far_x)
    mid_z = flip_z((z_sum + far_x).astype(BF16))
    over_batch = Reduce(lambda hop: mlp_terms[hop % batches], batches, along_batch)
    over_batch.step()
    mid_x, mid_z = join(mid_x, mid_z)
    second_grad = near_sum + mid_x + mid_z

    middle_grad = upstream.astype(F32) + standardize_back(second_grad, second_hat, second_inverse)
    middle_low = middle_grad.astype(BF16)
    mixed_grad = contract(out_full, middle_low, 1, 1).astype(BF16)
    sent = jnp.broadcast_to(
        mixed_grad.reshape(HEADS, 1, HDIM, tokens), (HEADS, splits, HDIM, tokens)
    ).reshape(seqs, HDIM, tokens)
    grads = lax.all_to_all(sent, "seq", split_axis=0, concat_axis=0, tiled=True)
    far_part, x_part, z_part = two_sums(
        [sum_far[0], *sum_mid[:2]], [sum_other[3], *sum_other[1:3]], sent
    )
    while over_batch.distance > 0:
        over_batch.step()
    grads, over_batch.got, qkv_full = join(grads, over_batch.got, qkv_full)
    over_batch.sum = sum(over_batch.got, over_batch.block_at(0))
    over_halves = Reduce(lambda step: over_batch.sum[step % halves], halves, along_halves)

    grads = grads.reshape(groups, 2, 2, HDIM, tokens)
    far_x, mid_x = flip_x(far_part), flip_x(x_part)
    last_step = over_halves.finish(grads)
    project_grad, own_grad, other_grad = attention_backward(
        core, mine, other, key_ids, query_ids, attended, logs, grads, tokens, splits
    )
    project_grad, own_grad, other_grad, far_x, mid_x = join(
        project_grad, own_grad, other_grad, far_x, mid_x
    )

    got = lax.all_to_all(
        project_grad.reshape(seqs, 3 * HDIM, tokens), "seq", split_axis=0, concat_axis=0, tiled=True
    )
    mlp_sum = sum(last_step, over_halves.block_at(0)).astype(BF16)
    up_sum = mlp_sum[: EIGHT * lines].reshape(2, 2, 2, lines, units)
    up_kept, up_core = pick(up_sum, at_core, 1), flip_core(pick(up_sum, 1 - at_core, 1))
    up_rows = jnp.stack([up_kept, up_core], axis=1)
    up_kept, up_x = pick(up_rows, at_x, 0), flip_x(pick(up_rows, 1 - at_x, 0))
    out_kept, out_kept_x, out_sent, out_sent_x = out_weight_terms(
        out_numbers, order, after(mixed, project_grad), middle_low,
        (groups, 2, 2, pairs, 2, lines, width),
    )
    out_core, out_core_x = flip_core(out_sent), flip_core(out_sent_x)
    out_x = flip_x(out_kept_x + out_core_x)
    qkv_terms = contract(first_own, own_grad, 0, 1)
    qkv_terms = qkv_terms + contract(first_other, other_grad, 0, 1)
    if splits > 1:
        got = got.reshape(HEADS, splits, 3 * HDIM, tokens).sum(1)
    qkv_terms = after(qkv_terms, got)
    mid_z = flip_z(z_part + far_x)
    got, up_x, out_x, mid_z = join(got, up_x, out_x, mid_z)

    qkv_terms = lax.all_to_all(
        qkv_terms.astype(BF16).reshape(devices, lines, 3 * HDIM),
        EVERY, split_axis=0, concat_axis=0, tiled=True,
    )

    input_grad = finish_input(
        got.reshape(3 * width, tokens), qkv_full, patches[0], middle_grad
    )
    up_rows = jnp.stack([up_kept, up_x], axis=0)
    up_kept, up_z = pick(up_rows, at_z, 2), flip_z(pick(up_rows, 1 - at_z, 2))
    out_sum = out_kept + out_core + out_x
    out_sum = out_sum[0] + flip_y(out_sum[1])
    out_got = deliver([out_sum[index] for index in range(len(hops))])
    block_output = middle + (sum_near[0] + sum_other[0] + mid_x + mid_z)
    block_output = block_output.astype(BF16)
    qkv_terms, input_grad, block_output = join(qkv_terms, input_grad, block_output)
    qkv_sum, first_gain_grad = finish_qkv(wide_gains[0], qkv_terms, qkv_weight)
    if hidden_rows % 128 == 0:
        up_sum, second_gain_grad = finish_up(
            sides, wide_gains[1], up_kept, up_z,
            up_weight, (halves, batches),
        )
    else:
        up_sum = jnp.stack([up_kept, up_z], axis=2)
        for axis, at in ((0, at_x), (1, at_core), (2, at_z)):
            up_sum = jnp.where(at == 0, up_sum, jnp.flip(up_sum, axis))
        up_sum = up_sum.astype(F32).reshape(2, 2, 2, lines, halves, batches, hidden_rows)
        up_sum = up_sum.transpose(3, 4, 2, 0, 1, 5, 6).reshape(lines, -1)
        second_gain_grad = jnp.sum(up_weight.astype(F32) * up_sum, axis=1)
        up_sum = up_sum * second_rows
    down_sum = mlp_sum[EIGHT * lines :].astype(F32).reshape(2, hidden_rows, units)
    down_sum = jnp.concatenate([down_sum[0], down_sum[1]], axis=1)
    out_sum = sum(out_got, out_sum[0]).astype(F32)

    return (
        block_output[None],
        input_grad[None],
        first_gain_grad.reshape(lines),
        qkv_sum,
        out_sum,
        second_gain_grad.reshape(lines),
        up_sum,
        down_sum,
    )


def solution(mesh):
    rows = P(EVERY)
    tokens = P("batch", "seq", None)
    in_specs = (
        tokens, tokens, P("batch", None), P("batch", None), rows, P(EVERY, None), P(EVERY, None),
        rows, P(EVERY, None), P(EVERY, None),
    )
    out_specs = (
        tokens, tokens, rows, P(EVERY, None), P(EVERY, None), rows, P(EVERY, None), P(EVERY, None)
    )
    body = functools.partial(local, mesh.shape["seq"], mesh.shape["batch"])
    return jax.shard_map(body, mesh=mesh, in_specs=in_specs, out_specs=out_specs, check_vma=False)
```

```python
import functools
import math

import jax
import jax.numpy as jnp
from jax import lax
from jax.experimental import pallas as pl
from jax.experimental.pallas import tpu as pltpu
from jax.sharding import PartitionSpec as P

HEADS = 16
HDIM = 64
QUAD = 4
EIGHT = 8

EPSILON = 1e-05
MASKED = -1e30
SCALING = HDIM**-0.5
BF16 = jnp.bfloat16
F32 = jnp.float32
EVERY = ("seq", "batch")
LARGE = pl.CostEstimate(flops=30_000_000_000, bytes_accessed=1, transcendentals=0)
VMEM_LIMIT = 60 << 20
SMALL = pl.CostEstimate(flops=1, bytes_accessed=1, transcendentals=0)


def contract(left, right, left_dim, right_dim):
    return lax.dot_general(
        left, right, (((left_dim,), (right_dim,)), ((), ())), preferred_element_type=F32
    )


def masked_scores(keys, queries, key_ids, query_ids, row, first):
    scores = contract(keys, queries, 0, 0)
    slots = row + lax.broadcasted_iota(jnp.int32, scores.shape, 0)
    columns = first + lax.broadcasted_iota(jnp.int32, scores.shape, 1)
    allowed = (key_ids == query_ids) | (slots == columns)
    return jnp.where(allowed, scores, MASKED)


def chunks(length, step):
    step = min(step, length)
    return [slice(row, row + step) for row in range(0, length, step)]


def load_heads(own_ref, other_ref, held, key_id_ref, key_column):
    half = own_ref.shape[1]
    held[:, :half] = own_ref[...]
    held[:, half:] = other_ref[...]
    key_column[...] = jnp.broadcast_to(key_id_ref[...], (8, 2 * half)).T[:, :1]


def forward_kernel(
    tokens, core_ref, own_ref, other_ref, key_id_ref, query_id_ref, mixed_ref, attended_ref,
    log_ref, held, key_column,
):
    step = pl.program_id(0)

    @pl.when(step == 0)
    def _():
        load_heads(own_ref, other_ref, held, key_id_ref, key_column)

    block = attended_ref.shape[1]
    first = pl.multiple_of(step * block, block)
    queries = held[:HDIM, pl.ds(first, block)]
    scores, highest = [], None
    parts = chunks(held.shape[1], 512)
    for part in parts:
        scores.append(
            masked_scores(
                held[HDIM : 2 * HDIM, part], queries, key_column[part], query_id_ref[...],
                part.start, first,
            )
        )
        top = jnp.max(scores[-1], axis=0, keepdims=True)
        highest = top if highest is None else jnp.maximum(highest, top)
    totals = attended = None
    for part, score in zip(parts, scores):
        expo = jnp.exp(score - highest)
        total = jnp.sum(expo, axis=0, keepdims=True)
        term = contract(held[2 * HDIM :, part], expo.astype(BF16), 1, 0)
        totals = total if totals is None else totals + total
        attended = term if attended is None else attended + term
    attended = attended / totals
    attended_ref[...] = attended
    log_ref[...] = highest + jnp.log(totals)
    low = attended.astype(BF16)
    for index in range(block // tokens):
        mixed_ref[index // 2, index % 2, 0] = low[:, index * tokens : (index + 1) * tokens]


def backward_kernel(
    tokens, core_ref, own_ref, other_ref, key_id_ref, query_id_ref, attended_ref, log_ref, grad_ref,
    out_ref, own_grad_ref, other_grad_ref, held, key_column, dk_sum, dv_sum,
):
    step = pl.program_id(0)
    steps = pl.num_programs(0)
    groups = out_ref.shape[0]
    half = own_ref.shape[1]

    @pl.when(step == 0)
    def _():
        load_heads(own_ref, other_ref, held, key_id_ref, key_column)
        dk_sum[...] = jnp.zeros_like(dk_sum)
        dv_sum[...] = jnp.zeros_like(dv_sum)

    block = attended_ref.shape[1]
    first = pl.multiple_of(step * block, block)
    queries = held[:HDIM, pl.ds(first, block)]
    count = block // tokens
    grads = jnp.concatenate(
        [grad_ref[index // 2, index % 2, 0] for index in range(count)], axis=1
    )
    logs = log_ref[...]
    delta = jnp.sum(grads.astype(F32) * attended_ref[...], axis=0, keepdims=True)
    dq = None
    for part in chunks(held.shape[1], 1024):
        keys = held[HDIM : 2 * HDIM, part]
        scores = masked_scores(
            keys, queries, key_column[part], query_id_ref[...], part.start, first
        )
        probs = jnp.exp(scores - logs)
        dprob = contract(held[2 * HDIM :, part], grads, 0, 0)
        dscore = (probs * (dprob - delta)).astype(BF16)
        term = contract(keys, dscore, 1, 0)
        dq = term if dq is None else dq + term
        dk_sum[:, part] += contract(queries, dscore, 1, 1)
        dv_sum[:, part] += contract(grads, probs.astype(BF16), 1, 1)
    dq = (dq * SCALING).astype(BF16)
    per_side = half // block
    side = step // per_side
    core = jnp.where(side == 0, core_ref[0], 1 - core_ref[0])
    for index in range(count):
        group = step % per_side * (count // 2) + index // 2
        out_ref[group, index % 2, core, :HDIM, :] = dq[:, index * tokens : (index + 1) * tokens]
    inside = pl.multiple_of((step % per_side) * block, block)

    @pl.when(side == 0)
    def _():
        own_grad_ref[:HDIM, pl.ds(inside, block)] = dq

    @pl.when(side == 1)
    def _():
        other_grad_ref[:HDIM, pl.ds(inside, block)] = dq

    @pl.when(step == steps - 1)
    def _():
        for first_row, total in ((HDIM, dk_sum), (2 * HDIM, dv_sum)):
            rows = pl.ds(first_row, HDIM)
            low = total[...].astype(BF16)
            own_grad_ref[rows, :] = low[:, :half]
            other_grad_ref[rows, :] = low[:, half:]
            for side_at in range(2):
                to_core = core_ref[0] if side_at == 0 else 1 - core_ref[0]
                for group in range(groups):
                    for x in range(2):
                        at = side_at * half + (2 * group + x) * tokens
                        out_ref[group, x, to_core, rows, :] = low[:, at : at + tokens]
        if steps < 2 * (half // block):
            other_grad_ref[:HDIM, :] = jnp.zeros((HDIM, half), BF16)
            for group in range(groups):
                for x in range(2):
                    out_ref[group, x, 1 - core_ref[0], :HDIM, :] = jnp.zeros((HDIM, tokens), BF16)


def side_core(step, per_side, core):
    return jnp.where(step < per_side, core, 1 - core)


def attention_specs(length, block, tokens, groups):
    half = length // 2
    whole = pl.BlockSpec((3 * HDIM, half), lambda i, core: (0, 0))
    part = pl.BlockSpec((HDIM, block), lambda i, core: (0, i))
    row = pl.BlockSpec((1, block), lambda i, core: (0, i))
    column = pl.BlockSpec((1, length), lambda i, core: (0, 0))
    per_side = half // block
    tile = pl.BlockSpec(
        (groups // per_side, 2, 1, HDIM, tokens),
        lambda i, core: (i % per_side, 0, side_core(i, per_side, core[0]), 0, 0),
    )
    return whole, part, row, column, tile


def attention_forward(core, own, other, key_ids, query_ids, tokens, splits):
    length = 2 * own.shape[1]
    groups = length // (4 * tokens)
    block = 4 * tokens if groups % 2 == 0 else 2 * tokens
    count = length // splits
    whole, part, row, column, tile = attention_specs(length, block, tokens, groups)
    return pl.pallas_call(
        functools.partial(forward_kernel, tokens),
        grid_spec=pltpu.PrefetchScalarGridSpec(
            num_scalar_prefetch=1,
            grid=(count // block,),
            in_specs=[whole, whole, column, row],
            out_specs=[tile, part, row],
            scratch_shapes=[
                pltpu.VMEM((3 * HDIM, length), BF16), pltpu.VMEM((length, 1), jnp.int32)
            ],
        ),
        out_shape=[
            jax.ShapeDtypeStruct((groups, 2, 2, HDIM, tokens), BF16),
            jax.ShapeDtypeStruct((HDIM, count), F32),
            jax.ShapeDtypeStruct((1, count), F32),
        ],
        compiler_params=pltpu.CompilerParams(vmem_limit_bytes=VMEM_LIMIT),
        cost_estimate=SMALL,
    )(core, own, other, key_ids, query_ids)


def attention_backward(core, own, other, key_ids, query_ids, attended, logs, grads, tokens, splits):
    length = 2 * own.shape[1]
    half = length // 2
    groups = length // (4 * tokens)
    block = 4 * tokens if groups % 2 == 0 else 2 * tokens
    count = length // splits
    whole, part, row, column, tile = attention_specs(length, block, tokens, groups)
    return pl.pallas_call(
        functools.partial(backward_kernel, tokens),
        grid_spec=pltpu.PrefetchScalarGridSpec(
            num_scalar_prefetch=1,
            grid=(count // block,),
            in_specs=[whole, whole, column, row, part, row, tile],
            out_specs=[
                pl.BlockSpec(
                    (groups, 2, 2, 3 * HDIM, tokens), lambda i, core: (0, 0, 0, 0, 0)
                ),
                whole,
                whole,
            ],
            scratch_shapes=[
                pltpu.VMEM((3 * HDIM, length), BF16),
                pltpu.VMEM((length, 1), jnp.int32),
                pltpu.VMEM((HDIM, length), F32),
                pltpu.VMEM((HDIM, length), F32),
            ],
        ),
        out_shape=[
            jax.ShapeDtypeStruct((groups, 2, 2, 3 * HDIM, tokens), BF16),
            jax.ShapeDtypeStruct((3 * HDIM, half), BF16),
            jax.ShapeDtypeStruct((3 * HDIM, half), BF16),
        ],
        compiler_params=pltpu.CompilerParams(vmem_limit_bytes=VMEM_LIMIT),
        cost_estimate=LARGE,
    )(core, own, other, key_ids, query_ids, attended, logs, grads)


def standard_kernel(patches_ref, out_ref):
    out_ref[...] = standardize(patches_ref[...].astype(F32))[0].astype(BF16)


def standard_patches(patches):
    return pl.pallas_call(
        standard_kernel,
        grid=(1,),
        in_specs=[whole(patches)],
        out_specs=whole(patches),
        out_shape=jax.ShapeDtypeStruct(patches.shape, BF16),
        cost_estimate=SMALL,
    )(patches)


def project_kernel(layout, tokens, where_ref, mine_w_ref, theirs_w_ref, *refs):
    pieces, (mine_ref, theirs_ref, all_ref) = refs[:-3], refs[-3:]
    for index, (source, row) in enumerate(layout):
        if isinstance(source, tuple):
            hat = jnp.concatenate([pieces[member][...] for member in source], axis=0)
        else:
            hat = pieces[source][row : row + tokens]
        at = where_ref[index]
        columns = pl.ds(pl.multiple_of(at * tokens, tokens), tokens)
        mine_ref[:, columns] = contract(mine_w_ref[...], hat, 1, 1).astype(BF16)
        theirs_ref[:, columns] = contract(theirs_w_ref[...], hat, 1, 1).astype(BF16)
        all_ref[at] = hat


def project_pieces(where, mine_w, theirs_w, pieces, layout, tokens):
    blocks = len(layout)
    width = mine_w.shape[1]
    columns = mine_w.shape[0]
    return whole_call(
        functools.partial(project_kernel, layout, tokens),
        where,
        [mine_w, theirs_w, *pieces],
        [
            jax.ShapeDtypeStruct((columns, blocks * tokens), BF16),
            jax.ShapeDtypeStruct((columns, blocks * tokens), BF16),
            jax.ShapeDtypeStruct((blocks, tokens, width), BF16),
        ],
    )


def whole(array):
    rank = len(array.shape)
    return pl.BlockSpec(array.shape, lambda *step: (0,) * rank)


def whole_call(kernel, scalars, arrays, outs, scratch=(), cost=SMALL):
    return pl.pallas_call(
        kernel,
        grid=(1,),
        in_specs=[pl.BlockSpec(memory_space=pltpu.SMEM)] + [whole(array) for array in arrays],
        out_specs=[whole(out) for out in outs],
        out_shape=outs,
        scratch_shapes=list(scratch),
        compiler_params=pltpu.CompilerParams(vmem_limit_bytes=VMEM_LIMIT),
        cost_estimate=cost,
    )(scalars, *arrays)


def together(refs):
    values = [ref[...] for ref in refs]
    return values[0] if len(values) == 1 else jnp.concatenate(values, axis=0)


def mlp_kernel(count, toggles, place_ref, *refs):
    pieces, refs = refs[:count], refs[count:]
    all_ref, up_ref, down_ref, hidden_ref, pre_grad_ref = refs[:5]
    hat = together(pieces)
    upstream = jnp.concatenate([all_ref[place_ref[0] ^ toggle] for toggle in toggles], axis=0)
    units = up_ref.shape[1]
    block = min(256, units)
    grad = out = None
    for first in range(0, units, block):
        chunk = slice(first, first + block)
        up, down = up_ref[:, chunk], down_ref[chunk, :]
        pre = contract(hat, up, 1, 0)
        cdf = 0.5 * (1.0 + lax.erf(pre * (0.5**0.5)))
        slope = cdf + pre * jnp.exp(-0.5 * pre * pre) * ((2.0 * math.pi) ** -0.5)
        hidden = (pre * cdf).astype(BF16)
        pre_grad = (contract(upstream, down, 1, 1) * slope).astype(BF16)
        hidden_ref[:, chunk] = hidden
        pre_grad_ref[:, chunk] = pre_grad
        grad_term = contract(pre_grad, up, 1, 1)
        out_term = contract(hidden, down, 1, 0)
        grad = grad_term if grad is None else grad + grad_term
        out = out_term if out is None else out + out_term
    for total, kept_refs in ((out, refs[5 : 5 + count]), (grad, refs[5 + count :])):
        first = 0
        for ref in kept_refs:
            ref[...] = total[first : first + ref.shape[0]].astype(ref.dtype)
            first += ref.shape[0]


def mlp(hats, toggles, place, upstream_all, up, down):
    count = len(hats)
    rows = sum(hat.shape[0] for hat in hats)
    width, units = up.shape
    sums = [
        jax.ShapeDtypeStruct(hat.shape, F32 if 2 * index < count else BF16)
        for index, hat in enumerate(hats)
    ]
    outs = whole_call(
        functools.partial(mlp_kernel, count, toggles),
        place,
        [*hats, upstream_all, up, down],
        [
            jax.ShapeDtypeStruct((rows, units), BF16),
            jax.ShapeDtypeStruct((rows, units), BF16),
            *sums,
            *sums,
        ],
    )
    return outs[0], outs[1], list(outs[2 : 2 + count]), list(outs[2 + count :])


def mlp_weight_kernel(counts, sizes, toggles, at_ref, *refs):
    halves, batches, lines, hidden_rows = sizes
    hats, pres, hiddens = (
        refs[: counts[0]], refs[counts[0] : sum(counts[:2])], refs[sum(counts[:2]) : sum(counts)]
    )
    refs = refs[sum(counts) :]
    all_ref, out_refs, (up_held, down_held) = refs[0], refs[1:-2], refs[-2:]
    upstream = jnp.concatenate([all_ref[at_ref[0] ^ toggle] for toggle in toggles], axis=0)
    up = contract(together(hats), together(pres), 0, 0).astype(BF16)
    up_held[...] = up.reshape(up_held.shape)
    down = contract(together(hiddens), upstream, 0, 0).astype(BF16)
    down_held[...] = down.reshape(down_held.shape)
    units = up_held.shape[-1]
    for hop, out_ref in enumerate(out_refs):
        b = at_ref[1 + halves + hop]
        for step in range(halves):
            g = at_ref[1 + step]
            for quad in range(QUAD):
                for z in range(2):
                    first = (2 * quad + z) * lines
                    out_ref[step, first : first + lines] = up_held[g, z, quad, b]
            for part in range(2):
                first = EIGHT * lines + part * hidden_rows
                columns = slice(part * units, (part + 1) * units)
                out_ref[step, first : first + hidden_rows] = down_held[g, b, :, columns]


def mlp_weight_terms(numbers, sizes, hats, toggles, pres, hiddens, upstream_all):
    halves, batches, lines, hidden_rows = sizes
    width, units = hats[0].shape[1], pres[0].shape[1]
    counts = (len(hats), len(pres), len(hiddens))
    out = jax.ShapeDtypeStruct((halves, EIGHT * lines + 2 * hidden_rows, units), BF16)
    outs = whole_call(
        functools.partial(mlp_weight_kernel, counts, sizes, toggles),
        numbers,
        [*hats, *pres, *hiddens, upstream_all],
        [out] * batches,
        [
            pltpu.VMEM((halves, 2, QUAD, batches, lines, units), BF16),
            pltpu.VMEM((halves, batches, hidden_rows, width), BF16),
        ],
        LARGE,
    )
    return list(outs)


def two_sums_kernel(count, *refs):
    for index in range(count):
        total = refs[index][...] + refs[count + index][...].astype(F32)
        refs[2 * count + index][...] = total.astype(BF16)


def two_sums(left, right, gate):
    arrays = [*left, after(right[0], gate), *right[1:]]
    outs = [jax.ShapeDtypeStruct(term.shape, BF16) for term in left]
    return pl.pallas_call(
        functools.partial(two_sums_kernel, len(left)),
        grid=(1,),
        in_specs=[whole(array) for array in arrays],
        out_specs=[whole(out) for out in outs],
        out_shape=outs,
        compiler_params=pltpu.CompilerParams(vmem_limit_bytes=VMEM_LIMIT),
        cost_estimate=LARGE,
    )(*arrays)


def out_weight_kernel(order, at_ref, mixed_ref, grad_ref, *refs):
    out_refs, held = refs[:-1], refs[-1]
    terms = contract(mixed_ref[...], grad_ref[...], 1, 0).astype(BF16)
    held[...] = terms.reshape(held.shape)
    for index, ref in enumerate(out_refs):
        toggle_core, toggle_x = index // 2, index % 2
        for y in range(2):
            for block, (g, p) in enumerate(order):
                ref[y, block] = held[
                    at_ref[g], at_ref[0] ^ toggle_x, at_ref[1] ^ toggle_core, at_ref[p],
                    at_ref[2] ^ y,
                ]


def out_weight_terms(at, order, mixed, grad, shape):
    lines, width = shape[-2:]
    return whole_call(
        functools.partial(out_weight_kernel, order),
        at,
        [mixed, grad],
        [jax.ShapeDtypeStruct((2, len(order), lines, width), BF16)] * 4,
        [pltpu.VMEM(shape, BF16)],
    )


def finish_input_kernel(got_ref, weight_ref, patches_ref, middle_ref, out_ref, total):
    step = pl.program_id(0)
    total[step] = contract(weight_ref[...], got_ref[...], 1, 0).T

    @pl.when(step == pl.num_programs(0) - 1)
    def _():
        grad = jnp.concatenate([total[index] for index in range(total.shape[0])], axis=1)
        hat, inverse = standardize(patches_ref[...].astype(F32))
        grad = standardize_back(grad, hat, inverse)
        out_ref[...] = (middle_ref[...] + grad).astype(BF16)


def finish_input(got, weight, patches, middle_grad):
    columns, tokens = got.shape
    width = weight.shape[0]
    block = width // 4
    rows = [patches, middle_grad]
    return pl.pallas_call(
        finish_input_kernel,
        grid=(4,),
        in_specs=[
            whole(got),
            pl.BlockSpec((block, columns), lambda i: (i, 0)),
            *[whole(array) for array in rows],
        ],
        out_specs=pl.BlockSpec((tokens, width), lambda i: (0, 0)),
        out_shape=jax.ShapeDtypeStruct((tokens, width), BF16),
        scratch_shapes=[pltpu.VMEM((4, tokens, block), F32)],
        compiler_params=pltpu.CompilerParams(vmem_limit_bytes=VMEM_LIMIT),
        cost_estimate=LARGE,
    )(got, weight, *rows)


def as_column(row_ref):
    row = row_ref[...].astype(F32)
    size = (row.shape[1], row.shape[1])
    same = lax.broadcasted_iota(jnp.int32, size, 0) == lax.broadcasted_iota(jnp.int32, size, 1)
    return jnp.sum(jnp.where(same, row, 0.0), axis=1, keepdims=True)


def finish_qkv_kernel(gain_ref, terms_ref, weight_ref, out_ref, gain_grad_ref):
    copies = terms_ref.shape[0] // HEADS
    gains = as_column(gain_ref)
    total = None
    for head in range(HEADS):
        term = terms_ref[head * copies].astype(F32)
        for copy in range(1, copies):
            term += terms_ref[head * copies + copy].astype(F32)
        for kind in range(3):
            first = (kind * HEADS + head) * HDIM
            columns = slice(first, first + HDIM)
            part = term[:, kind * HDIM : (kind + 1) * HDIM]
            out_ref[:, columns] = part * gains
            part = part * weight_ref[:, columns].astype(F32)
            total = part if total is None else total + part
    gain_grad_ref[...] = jnp.sum(total.T, axis=0, keepdims=True)


def finish_qkv(gains, terms, weight):
    lines, columns = weight.shape
    outs = [
        jax.ShapeDtypeStruct((lines, columns), F32), jax.ShapeDtypeStruct((1, lines), F32)
    ]
    arrays = [gains, terms, weight]
    return pl.pallas_call(
        finish_qkv_kernel,
        grid=(1,),
        in_specs=[whole(array) for array in arrays],
        out_specs=[whole(out) for out in outs],
        out_shape=outs,
        compiler_params=pltpu.CompilerParams(vmem_limit_bytes=VMEM_LIMIT),
        cost_estimate=SMALL,
    )(*arrays)


def finish_up_kernel(sizes, at_ref, gain_ref, near_ref, far_ref, weight_ref, out_ref, gain_grad_ref):
    halves, batches = sizes
    chunk = near_ref.shape[-1] // (halves * batches)
    gains = as_column(gain_ref)
    total = None
    for z, ref in enumerate((near_ref, far_ref)):
        for x in range(2):
            for core in range(2):
                quad = 2 * (at_ref[0] ^ x) + (at_ref[1] ^ core)
                term = ref[x, core].astype(F32)
                for index in range(halves * batches):
                    group = 2 * (index // batches) + (at_ref[2] ^ z)
                    block = (QUAD * group + quad) * batches + index % batches
                    columns = pl.ds(pl.multiple_of(block * chunk, chunk), chunk)
                    part = term[:, index * chunk : (index + 1) * chunk]
                    out_ref[:, columns] = part * gains
                    part = part * weight_ref[:, columns].astype(F32)
                    total = part if total is None else total + part
    gain_grad_ref[...] = jnp.sum(total.T, axis=0, keepdims=True)


def finish_up(at, gains, near, far, weight, sizes):
    lines, columns = weight.shape
    return whole_call(
        functools.partial(finish_up_kernel, sizes),
        at,
        [gains, near, far, weight],
        [jax.ShapeDtypeStruct((lines, columns), F32), jax.ShapeDtypeStruct((1, lines), F32)],
    )


def place_kernel(plan, count, at_ref, *refs):
    sources, targets = refs[:count], refs[count:]
    for source, block, lanes, target, where in plan:
        rows = sources[source][block] if lanes is None else sources[source][block, :, lanes]
        targets[target][tuple(at_ref[entry] for entry in where)] = rows


def place(at, sources, plan, shapes):
    outs = [jax.ShapeDtypeStruct(shape, BF16) for shape in shapes]
    return whole_call(functools.partial(place_kernel, plan, len(sources)), at, sources, outs)


def flip(array, axis, bit, size):
    return lax.ppermute(array, axis, [(i, i ^ bit) for i in range(size)])


def shifter(axis, size, stride):
    def shift(array, step):
        return lax.ppermute(
            array, axis, [(i, (i + step * stride) % size) for i in range(size)]
        )

    return shift


def after(array, *others):
    return lax.optimization_barrier((array, *others))[0]


def join(*values):
    flat, shape = jax.tree.flatten(values)
    return jax.tree.unflatten(shape, lax.optimization_barrier(tuple(flat)))


class Ring:
    def __init__(self, block, ring, shift, split):
        self.ring, self.shift, self.split = ring, shift, split
        self.right = self.left = block
        self.taken = 0

    def step(self, *gates):
        self.taken += 1
        right, left = after(self.right, *gates), after(self.left, *gates)
        if 2 * self.taken == self.ring:
            right, left = right[: self.split], left[self.split :]
        self.right, self.left = self.shift(right, 1), self.shift(left, -1)
        return [self.right, self.left]


class Reduce:
    def __init__(self, block_at, ring, shift):
        self.block_at, self.ring, self.shift = block_at, ring, shift
        self.distance = ring // 2
        self.got = self.half = None
        if ring == 1:
            self.sum = block_at(0)

    def step(self, *gates):
        distance, shift, block_at = self.distance, self.shift, self.block_at
        if distance == 0:
            return []
        self.distance -= 1
        if self.ring == 2:
            self.got = [shift(after(block_at(1).astype(BF16), *gates), 1)]
        elif self.got is None and self.ring % 2 == 0:
            far = block_at(distance).astype(BF16)
            self.half = far.shape[0] // 2
            self.got = [
                shift(after(far[: self.half], *gates), 1),
                shift(after(far[self.half :], *gates), -1),
            ]
        else:
            terms = [block_at(distance), block_at(-distance)]
            if self.half is not None:
                at = self.half
                terms = [
                    jnp.concatenate([terms[0][:at] + self.got[0], terms[0][at:]]),
                    jnp.concatenate([terms[1][:at], terms[1][at:] + self.got[1]]),
                ]
                self.half = None
            elif self.got is not None:
                terms = [term + got for term, got in zip(terms, self.got)]
            self.got = [
                shift(after(term.astype(BF16), *gates), way)
                for term, way in zip(terms, (1, -1))
            ]
        if self.distance == 0:
            self.sum = block_at(0)
            for got in self.got:
                self.sum = self.sum + got
        return self.got

    def finish(self, *gates):
        new = []
        while self.distance > 0:
            new = self.step(*gates)
        return new


def standardize(values):
    average = jnp.mean(values, axis=-1, keepdims=True)
    centred = values - average
    variance = jnp.mean(centred * centred, axis=-1, keepdims=True)
    inverse = lax.rsqrt(variance + EPSILON)
    return centred * inverse, inverse


def standardize_back(grad, hat, inverse):
    return inverse * (
        grad
        - jnp.mean(grad, axis=-1, keepdims=True)
        - hat * jnp.mean(grad * hat, axis=-1, keepdims=True)
    )


def local(
    seqs,
    batches,
    patches,
    cotangent,
    segment_ids,
    kept_mask,
    first_gain,
    qkv_weight,
    out_weight,
    second_gain,
    up_weight,
    down_weight,
):
    width = HEADS * HDIM
    tokens = patches.shape[1]
    length = tokens * seqs
    devices = seqs * batches
    groups = seqs // QUAD
    pairs = batches // 2
    splits = seqs // HEADS
    lines = qkv_weight.shape[0]
    hidden_rows = down_weight.shape[0]
    halves = groups // 2
    units = hidden_rows * halves * batches
    at_seq = lax.axis_index("seq")
    at_batch = lax.axis_index("batch")
    group, at_x, at_core = at_seq // QUAD, (at_seq // 2) % 2, at_seq % 2
    pair, at_y = at_batch // 2, at_batch % 2
    half_group, at_z = group // 2, group % 2
    quad = at_seq % QUAD
    along_groups = shifter("seq", seqs, QUAD)
    along_pairs = shifter("batch", batches, 2)
    along_halves = shifter("seq", seqs, 2 * QUAD)
    along_batch = shifter("batch", batches, 1)
    distances = sorted(range(groups), key=lambda step: min(step, groups - step))
    hops = [(step, hop) for hop in range(pairs) for step in distances]

    def flip_x(array, *gates):
        return flip(after(array, *gates), "seq", 2, seqs)

    def flip_core(array, *gates):
        return flip(after(array, *gates), "seq", 1, seqs)

    def flip_z(array, *gates):
        return flip(after(array, *gates), "seq", QUAD, seqs)

    def flip_y(array, *gates):
        return flip(after(array, *gates), "batch", 1, batches)

    def pick(array, at, axis):
        return lax.dynamic_index_in_dim(array, at, axis, keepdims=False)

    def rows(*arrays):
        return jnp.concatenate(arrays, axis=0)

    def shifted(array, step, hop):
        array = along_groups(array, step) if step else array
        return along_pairs(array, hop) if hop else array

    def from_halves(block, *gates):
        block = after(block, *gates)
        return [along_halves(block, step) for step in range(1, halves)]

    def from_batch(block, *gates):
        block = after(block, *gates)
        return [along_batch(block, hop) for hop in range(1, batches)]

    def deliver(terms, *gates):
        return [
            shifted(after(term, *gates), step, hop) for term, (step, hop) in zip(terms[1:], hops[1:])
        ]

    out_full = lax.all_gather(out_weight, EVERY, axis=0, tiled=True)
    at, plan = [], []
    for step in range(halves):
        for hop in range(batches):
            index = step * batches + hop
            first = len(at)
            at += [(half_group - step) % halves, (at_batch - hop) % batches]
            for block in range(EIGHT):
                z, x, c = block // 4, block // 2 % 2, block % 2
                where = (first, len(at), len(at) + 1, first + 1)
                plan.append((index, (z, x, c), None, 0, where))
                at += [at_z ^ z, quad ^ (2 * x + c)]
            plan.append((halves * batches + index, slice(None), None, 1, (first, first + 1)))
    place_numbers = jnp.stack(at).astype(jnp.int32)
    order = [(3 + 2 * index, 4 + 2 * index) for index in range(len(hops))]
    at = [at_x, at_core, at_y]
    for step, hop in hops:
        at += [(group + step) % groups, (pair + hop) % pairs]
    out_numbers = jnp.stack(at).astype(jnp.int32)
    place_at = (4 * at_z + 2 * at_x + at_core).astype(jnp.int32)[None]
    group_numbers = [(half_group + step) % halves for step in range(halves)]
    group_numbers += [(at_batch + hop) % batches for hop in range(batches)]
    group_numbers = jnp.stack([place_at[0], *group_numbers]).astype(jnp.int32)
    core = at_core.astype(jnp.int32)[None]
    sides = jnp.stack([at_x, at_core, at_z]).astype(jnp.int32)
    numbers = [place_numbers, out_numbers, place_at, group_numbers, core, sides]

    inputs = patches[0].astype(F32)
    own = standard_patches(patches[0])
    first_rows = first_gain.astype(F32)[:, None]
    second_rows = second_gain.astype(F32)[:, None]
    ring = Ring(own, groups, along_groups, tokens // 2)
    rounds = [[own], ring.step()]
    beside = [flip_x(own)]
    qkv_rows = after(qkv_weight, own).astype(F32) * first_rows
    qkv_rows = qkv_rows.reshape(lines, 3, HEADS, HDIM).transpose(2, 0, 1, 3)
    scales = jnp.array([SCALING, 1.0, 1.0], F32)[:, None]
    sent = jnp.broadcast_to(
        (qkv_rows * scales).astype(BF16).reshape(HEADS, 1, lines, 3 * HDIM),
        (HEADS, splits * batches, lines, 3 * HDIM),
    ).reshape(devices, lines, 3 * HDIM)
    eights = [
        [((2 * g + z) * QUAD + q) * batches + b for z in range(2) for q in range(QUAD)]
        for g in range(halves)
        for b in range(batches)
    ]
    up_rows = (after(up_weight, own).astype(F32) * second_rows).astype(BF16)
    up_rows = up_rows.reshape(lines, halves, 2, 2, 2, batches, hidden_rows)
    up_rows = up_rows.transpose(3, 4, 2, 0, 1, 5, 6).reshape(2, 2, 2, lines, units)
    up_kept = pick(up_rows, at_core, 1)
    up_core = flip_core(pick(up_rows, 1 - at_core, 1))
    head_weight = lax.all_to_all(sent, EVERY, split_axis=0, concat_axis=0, tiled=True)
    rounds[1], beside, up_core = join(rounds[1], beside, up_core)

    while ring.taken < groups // 2:
        beside.append(flip_x(rows(*rounds[-1])))
        rounds.append(ring.step(*rounds[-1]))
    def by_side(row):
        row = row.reshape(2 * groups, 2, tokens)
        sides = [pick(row, side, 1) for side in (at_core, 1 - at_core)]
        return rows(*sides).reshape(length)

    ids = by_side(segment_ids[0])
    key_ids = jnp.where(by_side(kept_mask[0]) == 1, ids, -1)[None]
    farthest = rounds[-1]
    down_rows = [[down_weight, *from_batch(down_weight, *rounds[1])]]
    beside.append(flip_x(rows(*rounds[-1])))
    head_weight, ids, key_ids, numbers, rounds = join(
        head_weight, ids, key_ids, numbers, rounds
    )

    place_numbers, out_numbers, place_at, group_numbers, core, sides = numbers

    head_weight = head_weight.reshape(width, 3 * HDIM).T
    near_weight = flip_core(head_weight)
    up_rows = jnp.stack([up_kept, up_core], axis=1)
    up_kept, up_x = pick(up_rows, at_x, 0), flip_x(pick(up_rows, 1 - at_x, 0))
    down_far = from_halves(down_weight, *farthest)
    beside, near_weight = join(beside, near_weight)

    pieces, layout, where = [own], [(0, 0)], [2 * group + at_x]
    flipped = [(0, 0, 2 * group + 1 - at_x)]
    for number in range(1, len(rounds)):
        steps = [number] if 2 * number == groups else [-number, number]
        spots = [2 * ((group + step) % groups) for step in steps]
        if len(steps) == 1 and len(rounds[number]) == 2:
            layout.append(((len(pieces), len(pieces) + 1), 0))
        else:
            layout += [(len(pieces) + index, 0) for index in range(len(steps))]
        where += [spot + at_x for spot in spots]
        pieces += rounds[number]
        flipped += [(number, row * tokens, spot + 1 - at_x) for row, spot in enumerate(spots)]
    layout += [(len(pieces) + number, row) for number, row, spot in flipped]
    where += [spot for number, row, spot in flipped]
    pieces += beside
    where = jnp.stack(where).astype(jnp.int32)
    mine, theirs, first_own = project_pieces(
        where, head_weight, near_weight, pieces, layout, tokens
    )

    other = flip_core(theirs)
    other, up_x = join(other, up_x)
    up_rows = jnp.stack([up_kept, up_x], axis=0)
    up_kept, up_z = pick(up_rows, at_z, 2), flip_z(pick(up_rows, 1 - at_z, 2))
    first_own = first_own.reshape(length // 2, width)
    first_other = flip_core(first_own)
    upstream = cotangent[0]
    upstream_all = lax.all_gather(
        after(upstream, mine), EVERY, axis=0, axis_index_groups=eights
    )

    query_ids = ids[None]
    mixed_blocks, attended, logs = attention_forward(
        core, mine, other, key_ids, query_ids, tokens, splits
    )
    mixed_blocks = mixed_blocks.reshape(seqs, HDIM, tokens)
    if splits > 1:
        filled = (jnp.arange(seqs, dtype=jnp.int32) % 2 == at_core)[:, None, None]
        mixed_blocks = jnp.where(filled, mixed_blocks, 0)
    mixed_blocks, down_rows, up_z, down_far, first_other = join(
        mixed_blocks, down_rows, up_z, down_far, first_other
    )
    up_packed = jnp.stack([up_kept, up_z], axis=0)
    up_far = from_halves(up_packed)
    up_rows = [[up_packed, *from_batch(up_packed)]]
    down_rows += [[block, *from_batch(block)] for block in down_far]

    mixed = lax.all_to_all(mixed_blocks, "seq", split_axis=0, concat_axis=0, tiled=True)
    if splits > 1:
        mixed = mixed.reshape(HEADS, splits, HDIM, tokens).sum(1)
    mixed, out_full = join(mixed.reshape(width, tokens), out_full)
    up_rows += [[block, *from_batch(block)] for block in up_far]

    qkv_part = after(qkv_rows.astype(BF16), mixed_blocks).transpose(1, 0, 2, 3)
    qkv_part = qkv_part.reshape(lines, 3 * width)
    qkv_full = lax.all_gather(qkv_part, EVERY, axis=0, tiled=True)

    middle = inputs + contract(mixed, out_full, 0, 0)
    second_hat, second_inverse = standardize(middle)
    second = second_hat.astype(BF16)
    second_x, second_z, second_core = flip_x(second), flip_z(second), flip_core(second)
    second_x, second_z, second_core, up_rows, down_rows, upstream_all = join(
        second_x, second_z, second_core, up_rows, down_rows, upstream_all
    )
    second_xz = flip_x(second_z)
    second_x_core, second_z_core = flip_core(second_x), flip_core(second_z)
    up_part, down_part = place(
        place_numbers,
        sum(up_rows + down_rows, []),
        plan,
        [(halves, 2, QUAD, batches, lines, units), (halves, batches, hidden_rows, width)],
    )
    up_part = up_part.reshape(width, units)
    down_part = down_part.reshape(units, width)

    weights = (place_at, upstream_all, up_part, down_part)
    hidden_near, pre_near, sum_near, grad_near = mlp([second, second_core], (0, 1), *weights)
    second_x_core, second_z_core, second_xz, grad_near = join(
        second_x_core, second_z_core, second_xz, grad_near
    )
    second_xz_core = flip_core(second_xz)
    hidden_mid, pre_mid, sum_mid, grad_mid = mlp(
        [second_x, second_z, second_x_core, second_z_core], (2, 4, 3, 5), *weights
    )
    second_xz_core, grad_mid = join(second_xz_core, grad_mid)
    hidden_far, pre_far, sum_far, grad_far = mlp([second_xz, second_xz_core], (6, 7), *weights)

    far_sum = grad_far[0] + flip_core(grad_far[1])
    far_x = flip_x(far_sum.astype(BF16))
    x_sum = grad_mid[0] + flip_core(grad_mid[2])
    z_sum = grad_mid[1] + flip_core(grad_mid[3])
    near_sum = grad_near[0] + flip_core(grad_near[1])
    seconds = [
        second, second_core, second_x, second_z, second_x_core, second_z_core, second_xz,
        second_xz_core,
    ]
    toggles = (0, 1, 2, 4, 3, 5, 6, 7)
    hiddens = [hidden_near, hidden_mid, hidden_far]
    pres = [pre_near, pre_mid, after(pre_far, far_sum)]
    if lines % 16 == 0 and hidden_rows % 16 == 0:
        mlp_terms = mlp_weight_terms(
            group_numbers, (halves, batches, lines, hidden_rows), seconds, toggles, pres, hiddens,
            upstream_all,
        )
    else:
        up_terms = contract(rows(*seconds), rows(*pres), 0, 0).astype(BF16)
        up_terms = up_terms.reshape(halves, 2, QUAD, batches, lines, units)
        up_terms = up_terms.transpose(3, 0, 2, 1, 4, 5).reshape(batches, halves, -1, units)
        sorted_places = jnp.stack([place_at[0] ^ toggle for toggle in toggles])
        down_terms = jnp.take(upstream_all, sorted_places, axis=0).reshape(-1, width)
        down_terms = contract(rows(*hiddens), down_terms, 0, 0).astype(BF16)
        down_terms = down_terms.reshape(halves, batches, hidden_rows, 2, units)
        down_terms = down_terms.transpose(1, 0, 3, 2, 4).reshape(batches, halves, -1, units)
        mlp_terms = jnp.roll(
            jnp.concatenate([up_terms, down_terms], axis=2), (-at_batch, -half_group), (0, 1)
        )
        mlp_terms = [mlp_terms[hop] for hop in range(batches)]
    sum_other = [flip_core(term, far_sum) for term in (sum_near[1], *sum_mid[2:])]
    sum_other.append(flip_core(sum_far[1], mlp_terms[0]))
    far_x, sum_other[3] = join(far_x, sum_other[3])
    mid_x = flip_x(x_sum.astype(BF16), far_x)
    mid_z = flip_z((z_sum + far_x).astype(BF16))
    over_batch = Reduce(lambda hop: mlp_terms[hop % batches], batches, along_batch)
    over_batch.step()
    mid_x, mid_z = join(mid_x, mid_z)
    second_grad = near_sum + mid_x + mid_z

    middle_grad = upstream.astype(F32) + standardize_back(second_grad, second_hat, second_inverse)
    middle_low = middle_grad.astype(BF16)
    mixed_grad = contract(out_full, middle_low, 1, 1).astype(BF16)
    sent = jnp.broadcast_to(
        mixed_grad.reshape(HEADS, 1, HDIM, tokens), (HEADS, splits, HDIM, tokens)
    ).reshape(seqs, HDIM, tokens)
    grads = lax.all_to_all(sent, "seq", split_axis=0, concat_axis=0, tiled=True)
    far_part, x_part, z_part = two_sums(
        [sum_far[0], *sum_mid[:2]], [sum_other[3], *sum_other[1:3]], sent
    )
    while over_batch.distance > 0:
        over_batch.step()
    grads, over_batch.got, qkv_full = join(grads, over_batch.got, qkv_full)
    over_halves = Reduce(
        lambda step: sum(
            [got[step % halves] for got in over_batch.got], over_batch.block_at(0)[step % halves]
        ),
        halves,
        along_halves,
    )

    grads = grads.reshape(groups, 2, 2, HDIM, tokens)
    far_x, mid_x = flip_x(far_part), flip_x(x_part)
    last_step = over_halves.finish(grads)
    project_grad, own_grad, other_grad = attention_backward(
        core, mine, other, key_ids, query_ids, attended, logs, grads, tokens, splits
    )
    project_grad, own_grad, other_grad, far_x, mid_x = join(
        project_grad, own_grad, other_grad, far_x, mid_x
    )

    got = lax.all_to_all(
        project_grad.reshape(seqs, 3 * HDIM, tokens), "seq", split_axis=0, concat_axis=0, tiled=True
    )
    mlp_sum = sum(last_step, over_halves.block_at(0)).astype(BF16)
    up_sum = mlp_sum[: EIGHT * lines].reshape(2, 2, 2, lines, units)
    up_kept, up_core = pick(up_sum, at_core, 1), flip_core(pick(up_sum, 1 - at_core, 1))
    up_rows = jnp.stack([up_kept, up_core], axis=1)
    up_kept, up_x = pick(up_rows, at_x, 0), flip_x(pick(up_rows, 1 - at_x, 0))
    out_kept, out_kept_x, out_sent, out_sent_x = out_weight_terms(
        out_numbers, order, after(mixed, project_grad), middle_low,
        (groups, 2, 2, pairs, 2, lines, width),
    )
    out_core, out_core_x = flip_core(out_sent), flip_core(out_sent_x)
    out_x = flip_x(out_kept_x + out_core_x)
    qkv_terms = contract(first_own, own_grad, 0, 1)
    qkv_terms = qkv_terms + contract(first_other, other_grad, 0, 1)
    if splits > 1:
        got = got.reshape(HEADS, splits, 3 * HDIM, tokens).sum(1)
    qkv_terms = after(qkv_terms, got)
    mid_z = flip_z(z_part + far_x)
    got, up_x, out_x, mid_z = join(got, up_x, out_x, mid_z)

    qkv_terms = lax.all_to_all(
        qkv_terms.astype(BF16).reshape(devices, lines, 3 * HDIM),
        EVERY, split_axis=0, concat_axis=0, tiled=True,
    )

    input_grad = finish_input(
        got.reshape(3 * width, tokens), qkv_full, patches[0], middle_grad
    )
    up_rows = jnp.stack([up_kept, up_x], axis=0)
    up_kept, up_z = pick(up_rows, at_z, 2), flip_z(pick(up_rows, 1 - at_z, 2))
    out_sum = out_kept + out_core + out_x
    out_sum = out_sum[0] + flip_y(out_sum[1])
    out_got = deliver([out_sum[index] for index in range(len(hops))])
    block_output = middle + (sum_near[0] + sum_other[0] + mid_x + mid_z)
    block_output = block_output.astype(BF16)
    qkv_terms, input_grad, block_output = join(qkv_terms, input_grad, block_output)
    qkv_sum, first_gain_grad = finish_qkv(first_gain.reshape(1, lines), qkv_terms, qkv_weight)
    if hidden_rows % 128 == 0:
        up_sum, second_gain_grad = finish_up(
            sides, second_gain.reshape(1, lines), up_kept, up_z,
            up_weight, (halves, batches),
        )
    else:
        up_sum = jnp.stack([up_kept, up_z], axis=2)
        for axis, at in ((0, at_x), (1, at_core), (2, at_z)):
            up_sum = jnp.where(at == 0, up_sum, jnp.flip(up_sum, axis))
        up_sum = up_sum.astype(F32).reshape(2, 2, 2, lines, halves, batches, hidden_rows)
        up_sum = up_sum.transpose(3, 4, 2, 0, 1, 5, 6).reshape(lines, -1)
        second_gain_grad = jnp.sum(up_weight.astype(F32) * up_sum, axis=1)
        up_sum = up_sum * second_rows
    down_sum = mlp_sum[EIGHT * lines :].astype(F32).reshape(2, hidden_rows, units)
    down_sum = jnp.concatenate([down_sum[0], down_sum[1]], axis=1)
    out_sum = sum(out_got, out_sum[0]).astype(F32)

    return (
        block_output[None],
        input_grad[None],
        first_gain_grad.reshape(lines),
        qkv_sum,
        out_sum,
        second_gain_grad.reshape(lines),
        up_sum,
        down_sum,
    )


def solution(mesh):
    rows = P(EVERY)
    tokens = P("batch", "seq", None)
    in_specs = (
        tokens, tokens, P("batch", None), P("batch", None), rows, P(EVERY, None), P(EVERY, None),
        rows, P(EVERY, None), P(EVERY, None),
    )
    out_specs = (
        tokens, tokens, rows, P(EVERY, None), P(EVERY, None), rows, P(EVERY, None), P(EVERY, None)
    )
    body = functools.partial(local, mesh.shape["seq"], mesh.shape["batch"])
    return jax.shard_map(body, mesh=mesh, in_specs=in_specs, out_specs=out_specs, check_vma=False)
```

```python
import functools
import math

import jax
import jax.numpy as jnp
from jax import lax
from jax.experimental import pallas as pl
from jax.experimental.pallas import tpu as pltpu
from jax.sharding import PartitionSpec as P

HEADS = 16
HDIM = 64
QUAD = 4
EIGHT = 8

EPSILON = 1e-05
MASKED = -1e30
SCALING = HDIM**-0.5
BF16 = jnp.bfloat16
F32 = jnp.float32
EVERY = ("seq", "batch")
LARGE = pl.CostEstimate(flops=30_000_000_000, bytes_accessed=1, transcendentals=0)
VMEM_LIMIT = 60 << 20
SMALL = pl.CostEstimate(flops=1, bytes_accessed=1, transcendentals=0)


def contract(left, right, left_dim, right_dim):
    return lax.dot_general(
        left, right, (((left_dim,), (right_dim,)), ((), ())), preferred_element_type=F32
    )


def masked_scores(keys, queries, key_ids, query_ids, row, first):
    scores = contract(keys, queries, 0, 0)
    slots = row + lax.broadcasted_iota(jnp.int32, scores.shape, 0)
    columns = first + lax.broadcasted_iota(jnp.int32, scores.shape, 1)
    allowed = (key_ids == query_ids) | (slots == columns)
    return jnp.where(allowed, scores, MASKED)


def chunks(length, step):
    step = min(step, length)
    return [slice(row, row + step) for row in range(0, length, step)]


def load_heads(own_ref, other_ref, held, key_id_ref, key_column):
    half = own_ref.shape[1]
    held[:, :half] = own_ref[...]
    held[:, half:] = other_ref[...]
    key_column[...] = jnp.broadcast_to(key_id_ref[...], (8, 2 * half)).T[:, :1]


def forward_kernel(
    tokens, core_ref, own_ref, other_ref, key_id_ref, query_id_ref, mixed_ref, attended_ref,
    log_ref, held, key_column,
):
    step = pl.program_id(0)

    @pl.when(step == 0)
    def _():
        load_heads(own_ref, other_ref, held, key_id_ref, key_column)

    block = attended_ref.shape[1]
    first = pl.multiple_of(step * block, block)
    queries = held[:HDIM, pl.ds(first, block)]
    scores, highest = [], None
    parts = chunks(held.shape[1], 512)
    for part in parts:
        scores.append(
            masked_scores(
                held[HDIM : 2 * HDIM, part], queries, key_column[part], query_id_ref[...],
                part.start, first,
            )
        )
        top = jnp.max(scores[-1], axis=0, keepdims=True)
        highest = top if highest is None else jnp.maximum(highest, top)
    totals = attended = None
    for part, score in zip(parts, scores):
        expo = jnp.exp(score - highest)
        total = jnp.sum(expo, axis=0, keepdims=True)
        term = contract(held[2 * HDIM :, part], expo.astype(BF16), 1, 0)
        totals = total if totals is None else totals + total
        attended = term if attended is None else attended + term
    attended = attended / totals
    attended_ref[...] = attended
    log_ref[...] = highest + jnp.log(totals)
    low = attended.astype(BF16)
    for index in range(block // tokens):
        mixed_ref[index // 2, index % 2, 0] = low[:, index * tokens : (index + 1) * tokens]


def backward_kernel(
    tokens, core_ref, own_ref, other_ref, key_id_ref, query_id_ref, attended_ref, log_ref, grad_ref,
    out_ref, own_grad_ref, other_grad_ref, held, key_column, dk_sum, dv_sum,
):
    step = pl.program_id(0)
    steps = pl.num_programs(0)
    groups = out_ref.shape[0]
    half = own_ref.shape[1]

    @pl.when(step == 0)
    def _():
        load_heads(own_ref, other_ref, held, key_id_ref, key_column)
        dk_sum[...] = jnp.zeros_like(dk_sum)
        dv_sum[...] = jnp.zeros_like(dv_sum)

    block = attended_ref.shape[1]
    first = pl.multiple_of(step * block, block)
    queries = held[:HDIM, pl.ds(first, block)]
    count = block // tokens
    grads = jnp.concatenate(
        [grad_ref[index // 2, index % 2, 0] for index in range(count)], axis=1
    )
    logs = log_ref[...]
    delta = jnp.sum(grads.astype(F32) * attended_ref[...], axis=0, keepdims=True)
    dq = None
    for part in chunks(held.shape[1], 1024):
        keys = held[HDIM : 2 * HDIM, part]
        scores = masked_scores(
            keys, queries, key_column[part], query_id_ref[...], part.start, first
        )
        probs = jnp.exp(scores - logs)
        dprob = contract(held[2 * HDIM :, part], grads, 0, 0)
        dscore = (probs * (dprob - delta)).astype(BF16)
        term = contract(keys, dscore, 1, 0)
        dq = term if dq is None else dq + term
        dk_sum[:, part] += contract(queries, dscore, 1, 1)
        dv_sum[:, part] += contract(grads, probs.astype(BF16), 1, 1)
    dq = (dq * SCALING).astype(BF16)
    per_side = half // block
    side = step // per_side
    core = jnp.where(side == 0, core_ref[0], 1 - core_ref[0])
    for index in range(count):
        group = step % per_side * (count // 2) + index // 2
        out_ref[group, index % 2, core, :HDIM, :] = dq[:, index * tokens : (index + 1) * tokens]
    inside = pl.multiple_of((step % per_side) * block, block)

    @pl.when(side == 0)
    def _():
        own_grad_ref[:HDIM, pl.ds(inside, block)] = dq

    @pl.when(side == 1)
    def _():
        other_grad_ref[:HDIM, pl.ds(inside, block)] = dq

    @pl.when(step == steps - 1)
    def _():
        for first_row, total in ((HDIM, dk_sum), (2 * HDIM, dv_sum)):
            rows = pl.ds(first_row, HDIM)
            low = total[...].astype(BF16)
            own_grad_ref[rows, :] = low[:, :half]
            other_grad_ref[rows, :] = low[:, half:]
            for side_at in range(2):
                to_core = core_ref[0] if side_at == 0 else 1 - core_ref[0]
                for group in range(groups):
                    for x in range(2):
                        at = side_at * half + (2 * group + x) * tokens
                        out_ref[group, x, to_core, rows, :] = low[:, at : at + tokens]
        if steps < 2 * (half // block):
            other_grad_ref[:HDIM, :] = jnp.zeros((HDIM, half), BF16)
            for group in range(groups):
                for x in range(2):
                    out_ref[group, x, 1 - core_ref[0], :HDIM, :] = jnp.zeros((HDIM, tokens), BF16)


def side_core(step, per_side, core):
    return jnp.where(step < per_side, core, 1 - core)


def attention_specs(length, block, tokens, groups):
    half = length // 2
    whole = pl.BlockSpec((3 * HDIM, half), lambda i, core: (0, 0))
    part = pl.BlockSpec((HDIM, block), lambda i, core: (0, i))
    row = pl.BlockSpec((1, block), lambda i, core: (0, i))
    column = pl.BlockSpec((1, length), lambda i, core: (0, 0))
    per_side = half // block
    tile = pl.BlockSpec(
        (groups // per_side, 2, 1, HDIM, tokens),
        lambda i, core: (i % per_side, 0, side_core(i, per_side, core[0]), 0, 0),
    )
    return whole, part, row, column, tile


def attention_forward(core, own, other, key_ids, query_ids, tokens, splits):
    length = 2 * own.shape[1]
    groups = length // (4 * tokens)
    block = 4 * tokens if groups % 2 == 0 else 2 * tokens
    count = length // splits
    whole, part, row, column, tile = attention_specs(length, block, tokens, groups)
    return pl.pallas_call(
        functools.partial(forward_kernel, tokens),
        grid_spec=pltpu.PrefetchScalarGridSpec(
            num_scalar_prefetch=1,
            grid=(count // block,),
            in_specs=[whole, whole, column, row],
            out_specs=[tile, part, row],
            scratch_shapes=[
                pltpu.VMEM((3 * HDIM, length), BF16), pltpu.VMEM((length, 1), jnp.int32)
            ],
        ),
        out_shape=[
            jax.ShapeDtypeStruct((groups, 2, 2, HDIM, tokens), BF16),
            jax.ShapeDtypeStruct((HDIM, count), F32),
            jax.ShapeDtypeStruct((1, count), F32),
        ],
        compiler_params=pltpu.CompilerParams(vmem_limit_bytes=VMEM_LIMIT),
        cost_estimate=SMALL,
    )(core, own, other, key_ids, query_ids)


def attention_backward(core, own, other, key_ids, query_ids, attended, logs, grads, tokens, splits):
    length = 2 * own.shape[1]
    half = length // 2
    groups = length // (4 * tokens)
    block = 4 * tokens if groups % 2 == 0 else 2 * tokens
    count = length // splits
    whole, part, row, column, tile = attention_specs(length, block, tokens, groups)
    return pl.pallas_call(
        functools.partial(backward_kernel, tokens),
        grid_spec=pltpu.PrefetchScalarGridSpec(
            num_scalar_prefetch=1,
            grid=(count // block,),
            in_specs=[whole, whole, column, row, part, row, tile],
            out_specs=[
                pl.BlockSpec(
                    (groups, 2, 2, 3 * HDIM, tokens), lambda i, core: (0, 0, 0, 0, 0)
                ),
                whole,
                whole,
            ],
            scratch_shapes=[
                pltpu.VMEM((3 * HDIM, length), BF16),
                pltpu.VMEM((length, 1), jnp.int32),
                pltpu.VMEM((HDIM, length), F32),
                pltpu.VMEM((HDIM, length), F32),
            ],
        ),
        out_shape=[
            jax.ShapeDtypeStruct((groups, 2, 2, 3 * HDIM, tokens), BF16),
            jax.ShapeDtypeStruct((3 * HDIM, half), BF16),
            jax.ShapeDtypeStruct((3 * HDIM, half), BF16),
        ],
        compiler_params=pltpu.CompilerParams(vmem_limit_bytes=VMEM_LIMIT),
        cost_estimate=LARGE,
    )(core, own, other, key_ids, query_ids, attended, logs, grads)


def standard_kernel(patches_ref, out_ref):
    out_ref[...] = standardize(patches_ref[...].astype(F32))[0].astype(BF16)


def standard_patches(patches):
    return pl.pallas_call(
        standard_kernel,
        grid=(1,),
        in_specs=[whole(patches)],
        out_specs=whole(patches),
        out_shape=jax.ShapeDtypeStruct(patches.shape, BF16),
        cost_estimate=SMALL,
    )(patches)


def project_kernel(layout, tokens, where_ref, mine_w_ref, theirs_w_ref, *refs):
    pieces, (mine_ref, theirs_ref, all_ref) = refs[:-3], refs[-3:]
    for index, (source, row) in enumerate(layout):
        if isinstance(source, tuple):
            hat = jnp.concatenate([pieces[member][...] for member in source], axis=0)
        else:
            hat = pieces[source][row : row + tokens]
        at = where_ref[index]
        columns = pl.ds(pl.multiple_of(at * tokens, tokens), tokens)
        mine_ref[:, columns] = contract(mine_w_ref[...], hat, 1, 1).astype(BF16)
        theirs_ref[:, columns] = contract(theirs_w_ref[...], hat, 1, 1).astype(BF16)
        all_ref[at] = hat


def project_pieces(where, mine_w, theirs_w, pieces, layout, tokens):
    blocks = len(layout)
    width = mine_w.shape[1]
    columns = mine_w.shape[0]
    return whole_call(
        functools.partial(project_kernel, layout, tokens),
        where,
        [mine_w, theirs_w, *pieces],
        [
            jax.ShapeDtypeStruct((columns, blocks * tokens), BF16),
            jax.ShapeDtypeStruct((columns, blocks * tokens), BF16),
            jax.ShapeDtypeStruct((blocks, tokens, width), BF16),
        ],
    )


def whole(array):
    rank = len(array.shape)
    return pl.BlockSpec(array.shape, lambda *step: (0,) * rank)


def whole_call(kernel, scalars, arrays, outs, scratch=(), cost=SMALL):
    return pl.pallas_call(
        kernel,
        grid=(1,),
        in_specs=[pl.BlockSpec(memory_space=pltpu.SMEM)] + [whole(array) for array in arrays],
        out_specs=[whole(out) for out in outs],
        out_shape=outs,
        scratch_shapes=list(scratch),
        compiler_params=pltpu.CompilerParams(vmem_limit_bytes=VMEM_LIMIT),
        cost_estimate=cost,
    )(scalars, *arrays)


def together(refs):
    values = [ref[...] for ref in refs]
    return values[0] if len(values) == 1 else jnp.concatenate(values, axis=0)


def mlp_kernel(count, toggles, place_ref, *refs):
    pieces, refs = refs[:count], refs[count:]
    all_ref, up_ref, down_ref, hidden_ref, pre_grad_ref = refs[:5]
    hat = together(pieces)
    upstream = jnp.concatenate([all_ref[place_ref[0] ^ toggle] for toggle in toggles], axis=0)
    units = up_ref.shape[1]
    block = min(256, units)
    grad = out = None
    for first in range(0, units, block):
        chunk = slice(first, first + block)
        up, down = up_ref[:, chunk], down_ref[chunk, :]
        pre = contract(hat, up, 1, 0)
        cdf = 0.5 * (1.0 + lax.erf(pre * (0.5**0.5)))
        slope = cdf + pre * jnp.exp(-0.5 * pre * pre) * ((2.0 * math.pi) ** -0.5)
        hidden = (pre * cdf).astype(BF16)
        pre_grad = (contract(upstream, down, 1, 1) * slope).astype(BF16)
        hidden_ref[:, chunk] = hidden
        pre_grad_ref[:, chunk] = pre_grad
        grad_term = contract(pre_grad, up, 1, 1)
        out_term = contract(hidden, down, 1, 0)
        grad = grad_term if grad is None else grad + grad_term
        out = out_term if out is None else out + out_term
    for total, kept_refs in ((out, refs[5 : 5 + count]), (grad, refs[5 + count :])):
        first = 0
        for ref in kept_refs:
            ref[...] = total[first : first + ref.shape[0]].astype(ref.dtype)
            first += ref.shape[0]


def mlp(hats, toggles, place, upstream_all, up, down):
    count = len(hats)
    rows = sum(hat.shape[0] for hat in hats)
    width, units = up.shape
    sums = [
        jax.ShapeDtypeStruct(hat.shape, F32 if 2 * index < count else BF16)
        for index, hat in enumerate(hats)
    ]
    outs = whole_call(
        functools.partial(mlp_kernel, count, toggles),
        place,
        [*hats, upstream_all, up, down],
        [
            jax.ShapeDtypeStruct((rows, units), BF16),
            jax.ShapeDtypeStruct((rows, units), BF16),
            *sums,
            *sums,
        ],
    )
    return outs[0], outs[1], list(outs[2 : 2 + count]), list(outs[2 + count :])


def mlp_weight_kernel(counts, sizes, toggles, at_ref, *refs):
    halves, batches, lines, hidden_rows = sizes
    hats, pres, hiddens = (
        refs[: counts[0]], refs[counts[0] : sum(counts[:2])], refs[sum(counts[:2]) : sum(counts)]
    )
    refs = refs[sum(counts) :]
    all_ref, out_refs, (up_held, down_held) = refs[0], refs[1:-2], refs[-2:]
    upstream = jnp.concatenate([all_ref[at_ref[0] ^ toggle] for toggle in toggles], axis=0)
    up = contract(together(hats), together(pres), 0, 0).astype(BF16)
    up_held[...] = up.reshape(up_held.shape)
    down = contract(together(hiddens), upstream, 0, 0).astype(BF16)
    down_held[...] = down.reshape(down_held.shape)
    units = up_held.shape[-1]
    for hop, out_ref in enumerate(out_refs):
        b = at_ref[1 + halves + hop]
        for step in range(halves):
            g = at_ref[1 + step]
            for quad in range(QUAD):
                for z in range(2):
                    first = (2 * quad + z) * lines
                    out_ref[step, first : first + lines] = up_held[g, z, quad, b]
            for part in range(2):
                first = EIGHT * lines + part * hidden_rows
                columns = slice(part * units, (part + 1) * units)
                out_ref[step, first : first + hidden_rows] = down_held[g, b, :, columns]


def mlp_weight_terms(numbers, sizes, hats, toggles, pres, hiddens, upstream_all):
    halves, batches, lines, hidden_rows = sizes
    width, units = hats[0].shape[1], pres[0].shape[1]
    counts = (len(hats), len(pres), len(hiddens))
    out = jax.ShapeDtypeStruct((halves, EIGHT * lines + 2 * hidden_rows, units), BF16)
    outs = whole_call(
        functools.partial(mlp_weight_kernel, counts, sizes, toggles),
        numbers,
        [*hats, *pres, *hiddens, upstream_all],
        [out] * batches,
        [
            pltpu.VMEM((halves, 2, QUAD, batches, lines, units), BF16),
            pltpu.VMEM((halves, batches, hidden_rows, width), BF16),
        ],
        LARGE,
    )
    return list(outs)


def two_sums_kernel(count, *refs):
    for index in range(count):
        total = refs[index][...] + refs[count + index][...].astype(F32)
        refs[2 * count + index][...] = total.astype(BF16)


def two_sums(left, right, gate):
    arrays = [*left, after(right[0], gate), *right[1:]]
    outs = [jax.ShapeDtypeStruct(term.shape, BF16) for term in left]
    return pl.pallas_call(
        functools.partial(two_sums_kernel, len(left)),
        grid=(1,),
        in_specs=[whole(array) for array in arrays],
        out_specs=[whole(out) for out in outs],
        out_shape=outs,
        compiler_params=pltpu.CompilerParams(vmem_limit_bytes=VMEM_LIMIT),
        cost_estimate=LARGE,
    )(*arrays)


def out_weight_kernel(order, at_ref, mixed_ref, grad_ref, *refs):
    out_refs, held = refs[:-1], refs[-1]
    terms = contract(mixed_ref[...], grad_ref[...], 1, 0).astype(BF16)
    held[...] = terms.reshape(held.shape)
    for index, ref in enumerate(out_refs):
        toggle_core, toggle_x = index // 2, index % 2
        for y in range(2):
            for block, (g, p) in enumerate(order):
                ref[y, block] = held[
                    at_ref[g], at_ref[0] ^ toggle_x, at_ref[1] ^ toggle_core, at_ref[p],
                    at_ref[2] ^ y,
                ]


def out_weight_terms(at, order, mixed, grad, shape):
    lines, width = shape[-2:]
    return whole_call(
        functools.partial(out_weight_kernel, order),
        at,
        [mixed, grad],
        [jax.ShapeDtypeStruct((2, len(order), lines, width), BF16)] * 4,
        [pltpu.VMEM(shape, BF16)],
    )


def finish_input_kernel(got_ref, weight_ref, patches_ref, middle_ref, out_ref, total):
    step = pl.program_id(0)
    total[step] = contract(weight_ref[...], got_ref[...], 1, 0).T

    @pl.when(step == pl.num_programs(0) - 1)
    def _():
        grad = jnp.concatenate([total[index] for index in range(total.shape[0])], axis=1)
        hat, inverse = standardize(patches_ref[...].astype(F32))
        grad = standardize_back(grad, hat, inverse)
        out_ref[...] = (middle_ref[...] + grad).astype(BF16)


def finish_input(got, weight, patches, middle_grad):
    columns, tokens = got.shape
    width = weight.shape[0]
    block = width // 4
    rows = [patches, middle_grad]
    return pl.pallas_call(
        finish_input_kernel,
        grid=(4,),
        in_specs=[
            whole(got),
            pl.BlockSpec((block, columns), lambda i: (i, 0)),
            *[whole(array) for array in rows],
        ],
        out_specs=pl.BlockSpec((tokens, width), lambda i: (0, 0)),
        out_shape=jax.ShapeDtypeStruct((tokens, width), BF16),
        scratch_shapes=[pltpu.VMEM((4, tokens, block), F32)],
        compiler_params=pltpu.CompilerParams(vmem_limit_bytes=VMEM_LIMIT),
        cost_estimate=LARGE,
    )(got, weight, *rows)


def as_column(row_ref):
    row = row_ref[...].astype(F32)
    size = (row.shape[1], row.shape[1])
    same = lax.broadcasted_iota(jnp.int32, size, 0) == lax.broadcasted_iota(jnp.int32, size, 1)
    return jnp.sum(jnp.where(same, row, 0.0), axis=1, keepdims=True)


def finish_qkv_kernel(gain_ref, terms_ref, weight_ref, out_ref, gain_grad_ref):
    copies = terms_ref.shape[0] // HEADS
    gains = as_column(gain_ref)
    total = None
    for head in range(HEADS):
        term = terms_ref[head * copies].astype(F32)
        for copy in range(1, copies):
            term += terms_ref[head * copies + copy].astype(F32)
        for kind in range(3):
            first = (kind * HEADS + head) * HDIM
            columns = slice(first, first + HDIM)
            part = term[:, kind * HDIM : (kind + 1) * HDIM]
            out_ref[:, columns] = part * gains
            part = part * weight_ref[:, columns].astype(F32)
            total = part if total is None else total + part
    gain_grad_ref[...] = jnp.sum(total.T, axis=0, keepdims=True)


def finish_qkv(gains, terms, weight):
    lines, columns = weight.shape
    outs = [
        jax.ShapeDtypeStruct((lines, columns), F32), jax.ShapeDtypeStruct((1, lines), F32)
    ]
    arrays = [gains, terms, weight]
    return pl.pallas_call(
        finish_qkv_kernel,
        grid=(1,),
        in_specs=[whole(array) for array in arrays],
        out_specs=[whole(out) for out in outs],
        out_shape=outs,
        compiler_params=pltpu.CompilerParams(vmem_limit_bytes=VMEM_LIMIT),
        cost_estimate=SMALL,
    )(*arrays)


def finish_up_kernel(sizes, at_ref, gain_ref, near_ref, far_ref, weight_ref, out_ref, gain_grad_ref):
    halves, batches = sizes
    chunk = near_ref.shape[-1] // (halves * batches)
    gains = as_column(gain_ref)
    total = None
    for z, ref in enumerate((near_ref, far_ref)):
        for x in range(2):
            for core in range(2):
                quad = 2 * (at_ref[0] ^ x) + (at_ref[1] ^ core)
                term = ref[x, core].astype(F32)
                for index in range(halves * batches):
                    group = 2 * (index // batches) + (at_ref[2] ^ z)
                    block = (QUAD * group + quad) * batches + index % batches
                    columns = pl.ds(pl.multiple_of(block * chunk, chunk), chunk)
                    part = term[:, index * chunk : (index + 1) * chunk]
                    out_ref[:, columns] = part * gains
                    part = part * weight_ref[:, columns].astype(F32)
                    total = part if total is None else total + part
    gain_grad_ref[...] = jnp.sum(total.T, axis=0, keepdims=True)


def finish_up(at, gains, near, far, weight, sizes):
    lines, columns = weight.shape
    return whole_call(
        functools.partial(finish_up_kernel, sizes),
        at,
        [gains, near, far, weight],
        [jax.ShapeDtypeStruct((lines, columns), F32), jax.ShapeDtypeStruct((1, lines), F32)],
    )


def place_kernel(plan, count, at_ref, *refs):
    sources, targets = refs[:count], refs[count:]
    for source, block, lanes, target, where in plan:
        rows = sources[source][block] if lanes is None else sources[source][block, :, lanes]
        targets[target][tuple(at_ref[entry] for entry in where)] = rows


def place(at, sources, plan, shapes):
    outs = [jax.ShapeDtypeStruct(shape, BF16) for shape in shapes]
    return whole_call(functools.partial(place_kernel, plan, len(sources)), at, sources, outs)


def flip(array, axis, bit, size):
    return lax.ppermute(array, axis, [(i, i ^ bit) for i in range(size)])


def shifter(axis, size, stride):
    def shift(array, step):
        return lax.ppermute(
            array, axis, [(i, (i + step * stride) % size) for i in range(size)]
        )

    return shift


def after(array, *others):
    return lax.optimization_barrier((array, *others))[0]


def join(*values):
    flat, shape = jax.tree.flatten(values)
    return jax.tree.unflatten(shape, lax.optimization_barrier(tuple(flat)))


class Ring:
    def __init__(self, block, ring, shift, split):
        self.ring, self.shift, self.split = ring, shift, split
        self.right = self.left = block
        self.taken = 0

    def step(self, *gates):
        self.taken += 1
        right, left = after(self.right, *gates), after(self.left, *gates)
        if 2 * self.taken == self.ring:
            right, left = right[: self.split], left[self.split :]
        self.right, self.left = self.shift(right, 1), self.shift(left, -1)
        return [self.right, self.left]


class Reduce:
    def __init__(self, block_at, ring, shift):
        self.block_at, self.ring, self.shift = block_at, ring, shift
        self.distance = ring // 2
        self.got = self.half = None
        if ring == 1:
            self.sum = block_at(0)

    def step(self, *gates):
        distance, shift, block_at = self.distance, self.shift, self.block_at
        if distance == 0:
            return []
        self.distance -= 1
        if self.ring == 2:
            self.got = [shift(after(block_at(1).astype(BF16), *gates), 1)]
        elif self.got is None and self.ring % 2 == 0:
            far = block_at(distance).astype(BF16)
            self.half = far.shape[0] // 2
            self.got = [
                shift(after(far[: self.half], *gates), 1),
                shift(after(far[self.half :], *gates), -1),
            ]
        else:
            terms = [block_at(distance), block_at(-distance)]
            if self.half is not None:
                at = self.half
                terms = [
                    jnp.concatenate([terms[0][:at] + self.got[0], terms[0][at:]]),
                    jnp.concatenate([terms[1][:at], terms[1][at:] + self.got[1]]),
                ]
                self.half = None
            elif self.got is not None:
                terms = [term + got for term, got in zip(terms, self.got)]
            self.got = [
                shift(after(term.astype(BF16), *gates), way)
                for term, way in zip(terms, (1, -1))
            ]
        if self.distance == 0:
            self.sum = block_at(0)
            for got in self.got:
                self.sum = self.sum + got
        return self.got

    def finish(self, *gates):
        new = []
        while self.distance > 0:
            new = self.step(*gates)
        return new


def standardize(values):
    average = jnp.mean(values, axis=-1, keepdims=True)
    centred = values - average
    variance = jnp.mean(centred * centred, axis=-1, keepdims=True)
    inverse = lax.rsqrt(variance + EPSILON)
    return centred * inverse, inverse


def standardize_back(grad, hat, inverse):
    return inverse * (
        grad
        - jnp.mean(grad, axis=-1, keepdims=True)
        - hat * jnp.mean(grad * hat, axis=-1, keepdims=True)
    )


def local(
    seqs,
    batches,
    patches,
    cotangent,
    segment_ids,
    kept_mask,
    first_gain,
    qkv_weight,
    out_weight,
    second_gain,
    up_weight,
    down_weight,
):
    width = HEADS * HDIM
    tokens = patches.shape[1]
    length = tokens * seqs
    devices = seqs * batches
    groups = seqs // QUAD
    pairs = batches // 2
    splits = seqs // HEADS
    lines = qkv_weight.shape[0]
    hidden_rows = down_weight.shape[0]
    halves = groups // 2
    units = hidden_rows * halves * batches
    at_seq = lax.axis_index("seq")
    at_batch = lax.axis_index("batch")
    group, at_x, at_core = at_seq // QUAD, (at_seq // 2) % 2, at_seq % 2
    pair, at_y = at_batch // 2, at_batch % 2
    half_group, at_z = group // 2, group % 2
    quad = at_seq % QUAD
    along_groups = shifter("seq", seqs, QUAD)
    along_pairs = shifter("batch", batches, 2)
    along_halves = shifter("seq", seqs, 2 * QUAD)
    along_batch = shifter("batch", batches, 1)
    distances = sorted(range(groups), key=lambda step: min(step, groups - step))
    hops = [(step, hop) for hop in range(pairs) for step in distances]

    def flip_x(array, *gates):
        return flip(after(array, *gates), "seq", 2, seqs)

    def flip_core(array, *gates):
        return flip(after(array, *gates), "seq", 1, seqs)

    def flip_z(array, *gates):
        return flip(after(array, *gates), "seq", QUAD, seqs)

    def flip_y(array, *gates):
        return flip(after(array, *gates), "batch", 1, batches)

    def pick(array, at, axis):
        return lax.dynamic_index_in_dim(array, at, axis, keepdims=False)

    def rows(*arrays):
        return jnp.concatenate(arrays, axis=0)

    def shifted(array, step, hop):
        array = along_groups(array, step) if step else array
        return along_pairs(array, hop) if hop else array

    def from_halves(block, *gates):
        block = after(block, *gates)
        return [along_halves(block, step) for step in range(1, halves)]

    def from_batch(block, *gates):
        block = after(block, *gates)
        return [along_batch(block, hop) for hop in range(1, batches)]

    def deliver(terms, *gates):
        return [
            shifted(after(term, *gates), step, hop) for term, (step, hop) in zip(terms[1:], hops[1:])
        ]

    out_full = lax.all_gather(out_weight, EVERY, axis=0, tiled=True)
    at, plan = [], []
    for step in range(halves):
        for hop in range(batches):
            index = step * batches + hop
            first = len(at)
            at += [(half_group - step) % halves, (at_batch - hop) % batches]
            for block in range(EIGHT):
                z, x, c = block // 4, block // 2 % 2, block % 2
                where = (first, len(at), len(at) + 1, first + 1)
                plan.append((index, (z, x, c), None, 0, where))
                at += [at_z ^ z, quad ^ (2 * x + c)]
            plan.append((halves * batches + index, slice(None), None, 1, (first, first + 1)))
    place_numbers = jnp.stack(at).astype(jnp.int32)
    order = [(3 + 2 * index, 4 + 2 * index) for index in range(len(hops))]
    at = [at_x, at_core, at_y]
    for step, hop in hops:
        at += [(group + step) % groups, (pair + hop) % pairs]
    out_numbers = jnp.stack(at).astype(jnp.int32)
    place_at = (4 * at_z + 2 * at_x + at_core).astype(jnp.int32)[None]
    group_numbers = [(half_group + step) % halves for step in range(halves)]
    group_numbers += [(at_batch + hop) % batches for hop in range(batches)]
    group_numbers = jnp.stack([place_at[0], *group_numbers]).astype(jnp.int32)
    core = at_core.astype(jnp.int32)[None]
    sides = jnp.stack([at_x, at_core, at_z]).astype(jnp.int32)
    numbers = [place_numbers, out_numbers, place_at, group_numbers, core, sides]

    inputs = patches[0].astype(F32)
    own = standard_patches(patches[0])
    first_rows = first_gain.astype(F32)[:, None]
    second_rows = second_gain.astype(F32)[:, None]
    ring = Ring(own, groups, along_groups, tokens // 2)
    rounds = [[own], ring.step()]
    beside = [flip_x(own)]
    qkv_rows = after(qkv_weight, own).astype(F32) * first_rows
    qkv_rows = qkv_rows.reshape(lines, 3, HEADS, HDIM).transpose(2, 0, 1, 3)
    scales = jnp.array([SCALING, 1.0, 1.0], F32)[:, None]
    sent = jnp.broadcast_to(
        (qkv_rows * scales).astype(BF16).reshape(HEADS, 1, lines, 3 * HDIM),
        (HEADS, splits * batches, lines, 3 * HDIM),
    ).reshape(devices, lines, 3 * HDIM)
    eights = [
        [((2 * g + z) * QUAD + q) * batches + b for z in range(2) for q in range(QUAD)]
        for g in range(halves)
        for b in range(batches)
    ]
    up_rows = (after(up_weight, own).astype(F32) * second_rows).astype(BF16)
    up_rows = up_rows.reshape(lines, halves, 2, 2, 2, batches, hidden_rows)
    up_rows = up_rows.transpose(3, 4, 2, 0, 1, 5, 6).reshape(2, 2, 2, lines, units)
    up_kept = pick(up_rows, at_core, 1)
    up_core = flip_core(pick(up_rows, 1 - at_core, 1))
    head_weight = lax.all_to_all(sent, EVERY, split_axis=0, concat_axis=0, tiled=True)
    rounds[1], beside, up_core = join(rounds[1], beside, up_core)

    while ring.taken < groups // 2:
        beside.append(flip_x(rows(*rounds[-1])))
        rounds.append(ring.step(*rounds[-1]))
    def by_side(row):
        row = row.reshape(2 * groups, 2, tokens)
        sides = [pick(row, side, 1) for side in (at_core, 1 - at_core)]
        return rows(*sides).reshape(length)

    ids = by_side(segment_ids[0])
    key_ids = jnp.where(by_side(kept_mask[0]) == 1, ids, -1)[None]
    farthest = rounds[-1]
    down_rows = [[down_weight, *from_batch(down_weight, *rounds[1])]]
    beside.append(flip_x(rows(*rounds[-1])))
    head_weight, ids, key_ids, numbers, rounds = join(
        head_weight, ids, key_ids, numbers, rounds
    )

    place_numbers, out_numbers, place_at, group_numbers, core, sides = numbers

    head_weight = head_weight.reshape(width, 3 * HDIM).T
    near_weight = flip_core(head_weight)
    up_rows = jnp.stack([up_kept, up_core], axis=1)
    up_kept, up_x = pick(up_rows, at_x, 0), flip_x(pick(up_rows, 1 - at_x, 0))
    down_far = from_halves(down_weight, *farthest)
    beside, near_weight = join(beside, near_weight)

    pieces, layout, where = [own], [(0, 0)], [2 * group + at_x]
    flipped = [(0, 0, 2 * group + 1 - at_x)]
    for number in range(1, len(rounds)):
        steps = [number] if 2 * number == groups else [-number, number]
        spots = [2 * ((group + step) % groups) for step in steps]
        if len(steps) == 1 and len(rounds[number]) == 2:
            layout.append(((len(pieces), len(pieces) + 1), 0))
        else:
            layout += [(len(pieces) + index, 0) for index in range(len(steps))]
        where += [spot + at_x for spot in spots]
        pieces += rounds[number]
        flipped += [(number, row * tokens, spot + 1 - at_x) for row, spot in enumerate(spots)]
    layout += [(len(pieces) + number, row) for number, row, spot in flipped]
    where += [spot for number, row, spot in flipped]
    pieces += beside
    where = jnp.stack(where).astype(jnp.int32)
    mine, theirs, first_own = project_pieces(
        where, head_weight, near_weight, pieces, layout, tokens
    )

    other = flip_core(theirs)
    other, up_x = join(other, up_x)
    up_rows = jnp.stack([up_kept, up_x], axis=0)
    up_kept, up_z = pick(up_rows, at_z, 2), flip_z(pick(up_rows, 1 - at_z, 2))
    first_own = first_own.reshape(length // 2, width)
    first_other = flip_core(first_own)
    upstream = cotangent[0]
    upstream_all = lax.all_gather(
        after(upstream, mine), EVERY, axis=0, axis_index_groups=eights
    )

    query_ids = ids[None]
    mixed_blocks, attended, logs = attention_forward(
        core, mine, other, key_ids, query_ids, tokens, splits
    )
    mixed_blocks = mixed_blocks.reshape(seqs, HDIM, tokens)
    if splits > 1:
        filled = (jnp.arange(seqs, dtype=jnp.int32) % 2 == at_core)[:, None, None]
        mixed_blocks = jnp.where(filled, mixed_blocks, 0)
    mixed_blocks, down_rows, up_z, down_far, first_other = join(
        mixed_blocks, down_rows, up_z, down_far, first_other
    )
    up_packed = jnp.stack([up_kept, up_z], axis=0)
    up_far = from_halves(up_packed)
    up_rows = [[up_packed, *from_batch(up_packed)]]
    down_rows += [[block, *from_batch(block)] for block in down_far]

    mixed = lax.all_to_all(mixed_blocks, "seq", split_axis=0, concat_axis=0, tiled=True)
    if splits > 1:
        mixed = mixed.reshape(HEADS, splits, HDIM, tokens).sum(1)
    mixed, out_full = join(mixed.reshape(width, tokens), out_full)
    up_rows += [[block, *from_batch(block)] for block in up_far]

    qkv_part = after(qkv_rows.astype(BF16), mixed_blocks).transpose(1, 0, 2, 3)
    qkv_part = qkv_part.reshape(lines, 3 * width)
    qkv_full = lax.all_gather(qkv_part, EVERY, axis=0, tiled=True)

    middle = inputs + contract(mixed, out_full, 0, 0)
    second_hat, second_inverse = standardize(middle)
    second = second_hat.astype(BF16)
    second_x, second_z, second_core = flip_x(second), flip_z(second), flip_core(second)
    second_x, second_z, second_core, up_rows, down_rows, upstream_all = join(
        second_x, second_z, second_core, up_rows, down_rows, upstream_all
    )
    second_xz = flip_x(second_z)
    second_x_core, second_z_core = flip_core(second_x), flip_core(second_z)
    up_part, down_part = place(
        place_numbers,
        sum(up_rows + down_rows, []),
        plan,
        [(halves, 2, QUAD, batches, lines, units), (halves, batches, hidden_rows, width)],
    )
    up_part = up_part.reshape(width, units)
    down_part = down_part.reshape(units, width)

    weights = (place_at, upstream_all, up_part, down_part)
    hidden_near, pre_near, sum_near, grad_near = mlp([second, second_core], (0, 1), *weights)
    second_x_core, second_z_core, second_xz, grad_near = join(
        second_x_core, second_z_core, second_xz, grad_near
    )
    second_xz_core = flip_core(second_xz)
    hidden_mid, pre_mid, sum_mid, grad_mid = mlp(
        [second_x, second_z, second_x_core, second_z_core], (2, 4, 3, 5), *weights
    )
    second_xz_core, grad_mid = join(second_xz_core, grad_mid)
    hidden_far, pre_far, sum_far, grad_far = mlp([second_xz, second_xz_core], (6, 7), *weights)

    far_sum = (grad_far[0] + flip_core(grad_far[1])).astype(BF16)
    far_x = flip_x(far_sum)
    x_sum = grad_mid[0] + flip_core(grad_mid[2])
    z_sum = grad_mid[1] + flip_core(grad_mid[3])
    near_sum = grad_near[0] + flip_core(grad_near[1])
    seconds = [
        second, second_core, second_x, second_z, second_x_core, second_z_core, second_xz,
        second_xz_core,
    ]
    toggles = (0, 1, 2, 4, 3, 5, 6, 7)
    hiddens = [hidden_near, hidden_mid, hidden_far]
    pres = [pre_near, pre_mid, after(pre_far, far_sum)]
    if lines % 16 == 0 and hidden_rows % 16 == 0:
        mlp_terms = mlp_weight_terms(
            group_numbers, (halves, batches, lines, hidden_rows), seconds, toggles, pres, hiddens,
            upstream_all,
        )
    else:
        up_terms = contract(rows(*seconds), rows(*pres), 0, 0).astype(BF16)
        up_terms = up_terms.reshape(halves, 2, QUAD, batches, lines, units)
        up_terms = up_terms.transpose(3, 0, 2, 1, 4, 5).reshape(batches, halves, -1, units)
        sorted_places = jnp.stack([place_at[0] ^ toggle for toggle in toggles])
        down_terms = jnp.take(upstream_all, sorted_places, axis=0).reshape(-1, width)
        down_terms = contract(rows(*hiddens), down_terms, 0, 0).astype(BF16)
        down_terms = down_terms.reshape(halves, batches, hidden_rows, 2, units)
        down_terms = down_terms.transpose(1, 0, 3, 2, 4).reshape(batches, halves, -1, units)
        mlp_terms = jnp.roll(
            jnp.concatenate([up_terms, down_terms], axis=2), (-at_batch, -half_group), (0, 1)
        )
        mlp_terms = [mlp_terms[hop] for hop in range(batches)]
    sum_other = [flip_core(term, far_sum) for term in (sum_near[1], *sum_mid[2:])]
    sum_other.append(flip_core(sum_far[1], mlp_terms[0]))
    far_x, sum_other[3] = join(far_x, sum_other[3])
    mid_x = flip_x(x_sum.astype(BF16), far_x)
    mid_z = flip_z((z_sum + far_x).astype(BF16))
    over_batch = Reduce(lambda hop: mlp_terms[hop % batches], batches, along_batch)
    over_batch.step()
    mid_x, mid_z = join(mid_x, mid_z)
    second_grad = near_sum + mid_x + mid_z

    middle_grad = upstream.astype(F32) + standardize_back(second_grad, second_hat, second_inverse)
    middle_low = middle_grad.astype(BF16)
    mixed_grad = contract(out_full, middle_low, 1, 1).astype(BF16)
    sent = jnp.broadcast_to(
        mixed_grad.reshape(HEADS, 1, HDIM, tokens), (HEADS, splits, HDIM, tokens)
    ).reshape(seqs, HDIM, tokens)
    grads = lax.all_to_all(sent, "seq", split_axis=0, concat_axis=0, tiled=True)
    far_part, x_part, z_part = two_sums(
        [sum_far[0], *sum_mid[:2]], [sum_other[3], *sum_other[1:3]], sent
    )
    while over_batch.distance > 0:
        over_batch.step()
    grads, over_batch.got, qkv_full = join(grads, over_batch.got, qkv_full)
    over_halves = Reduce(
        lambda step: sum(
            [got[step % halves] for got in over_batch.got], over_batch.block_at(0)[step % halves]
        ),
        halves,
        along_halves,
    )

    grads = grads.reshape(groups, 2, 2, HDIM, tokens)
    far_x, mid_x = flip_x(far_part), flip_x(x_part)
    last_step = over_halves.finish(grads)
    project_grad, own_grad, other_grad = attention_backward(
        core, mine, other, key_ids, query_ids, attended, logs, grads, tokens, splits
    )
    project_grad, own_grad, other_grad, far_x, mid_x = join(
        project_grad, own_grad, other_grad, far_x, mid_x
    )

    got = lax.all_to_all(
        project_grad.reshape(seqs, 3 * HDIM, tokens), "seq", split_axis=0, concat_axis=0, tiled=True
    )
    mlp_sum = sum(last_step, over_halves.block_at(0)).astype(BF16)
    up_sum = mlp_sum[: EIGHT * lines].reshape(2, 2, 2, lines, units)
    up_kept, up_core = pick(up_sum, at_core, 1), flip_core(pick(up_sum, 1 - at_core, 1))
    up_rows = jnp.stack([up_kept, up_core], axis=1)
    up_kept, up_x = pick(up_rows, at_x, 0), flip_x(pick(up_rows, 1 - at_x, 0))
    out_kept, out_kept_x, out_sent, out_sent_x = out_weight_terms(
        out_numbers, order, after(mixed, project_grad), middle_low,
        (groups, 2, 2, pairs, 2, lines, width),
    )
    out_core, out_core_x = flip_core(out_sent), flip_core(out_sent_x)
    out_x = flip_x(out_kept_x + out_core_x)
    qkv_terms = contract(first_own, own_grad, 0, 1)
    qkv_terms = qkv_terms + contract(first_other, other_grad, 0, 1)
    if splits > 1:
        got = got.reshape(HEADS, splits, 3 * HDIM, tokens).sum(1)
    qkv_terms = after(qkv_terms, got)
    mid_z = flip_z(z_part + far_x)
    got, up_x, out_x, mid_z = join(got, up_x, out_x, mid_z)

    qkv_terms = lax.all_to_all(
        qkv_terms.astype(BF16).reshape(devices, lines, 3 * HDIM),
        EVERY, split_axis=0, concat_axis=0, tiled=True,
    )

    input_grad = finish_input(
        got.reshape(3 * width, tokens), qkv_full, patches[0], middle_grad
    )
    up_rows = jnp.stack([up_kept, up_x], axis=0)
    up_kept, up_z = pick(up_rows, at_z, 2), flip_z(pick(up_rows, 1 - at_z, 2))
    out_sum = out_kept + out_core + out_x
    out_sum = out_sum[0] + flip_y(out_sum[1])
    out_got = deliver([out_sum[index] for index in range(len(hops))])
    block_output = middle + (sum_near[0] + sum_other[0] + mid_x + mid_z)
    block_output = block_output.astype(BF16)
    qkv_terms, input_grad, block_output = join(qkv_terms, input_grad, block_output)
    qkv_sum, first_gain_grad = finish_qkv(first_gain.reshape(1, lines), qkv_terms, qkv_weight)
    if hidden_rows % 128 == 0:
        up_sum, second_gain_grad = finish_up(
            sides, second_gain.reshape(1, lines), up_kept, up_z,
            up_weight, (halves, batches),
        )
    else:
        up_sum = jnp.stack([up_kept, up_z], axis=2)
        for axis, at in ((0, at_x), (1, at_core), (2, at_z)):
            up_sum = jnp.where(at == 0, up_sum, jnp.flip(up_sum, axis))
        up_sum = up_sum.astype(F32).reshape(2, 2, 2, lines, halves, batches, hidden_rows)
        up_sum = up_sum.transpose(3, 4, 2, 0, 1, 5, 6).reshape(lines, -1)
        second_gain_grad = jnp.sum(up_weight.astype(F32) * up_sum, axis=1)
        up_sum = up_sum * second_rows
    down_sum = mlp_sum[EIGHT * lines :].astype(F32).reshape(2, hidden_rows, units)
    down_sum = jnp.concatenate([down_sum[0], down_sum[1]], axis=1)
    out_sum = sum(out_got, out_sum[0]).astype(F32)

    return (
        block_output[None],
        input_grad[None],
        first_gain_grad.reshape(lines),
        qkv_sum,
        out_sum,
        second_gain_grad.reshape(lines),
        up_sum,
        down_sum,
    )


def solution(mesh):
    rows = P(EVERY)
    tokens = P("batch", "seq", None)
    in_specs = (
        tokens, tokens, P("batch", None), P("batch", None), rows, P(EVERY, None), P(EVERY, None),
        rows, P(EVERY, None), P(EVERY, None),
    )
    out_specs = (
        tokens, tokens, rows, P(EVERY, None), P(EVERY, None), rows, P(EVERY, None), P(EVERY, None)
    )
    body = functools.partial(local, mesh.shape["seq"], mesh.shape["batch"])
    return jax.shard_map(body, mesh=mesh, in_specs=in_specs, out_specs=out_specs, check_vma=False)
```
